32 devices in a mesh: groups: 2 (over y), seq: 4 (over z), seg: 4 (over x, core).
Axes of the slice: x: 2, y: 2, z: 4, core: 2. Of those that a mesh axis runs over, the one named last changes fastest.
Arguments:
- layer_input: bfloat16 [8, 1024, 2048], P(('groups', 'seq'), 'seg'), parts along dimension 0, may hold values from -6 to 6
- out_cot: bfloat16 [8, 1024, 512], P(('groups', 'seq'), 'seg'), parts along dimension 0, may hold values from -6 to 6
- w_proj: bfloat16 [2048, 1536], P('seq'), may hold values from -0.125 to 0.125
- inner_start: float32 [8, 4, 2, 8, 64, 256], P(('groups', 'seq'), 'seg'), parts along dimension 0, may hold values from -1.5 to 1.5
- rates: float32 [8], replicated, may hold values from 0.01 to 0.06
Outputs:
- grad_input: bfloat16 [8, 1024, 2048], P(('groups', 'seq'), 'seg'), parts along dimension 0
- grad_proj: float32 [4096, 1536], P(('groups', 'seq')), parts along dimension 0
- grad_inner: float32 [8, 4, 2, 8, 64, 256], P(('groups', 'seq'), 'seg'), parts along dimension 0
The draws below stay inside these ranges and needn't reach their ends.
There are 2 independent parts, one for each index of `groups`. The reference program is written for one: setup_inputs(seed, part) draws one part's arguments, and reference() takes and returns one part's arrays. A program takes and returns all parts, laid end to end along the dimension named above; an argument that names none is the same for every part. Nothing has to cross between parts.
All inputs are finite; a program needn't handle non-finite values.
Results may differ from the reference program's by a relative error of at most 0.008.
Values may be sent and summed in bfloat16 or wider, within the bound.
No kernel may reach another device: no remote copies, remote signals or barrier semaphores. Data moves between devices by JAX's collectives and lax.ppermute only.
A program may use at most 128 MiB of HBM per device.

```python
import math
import jax
import jax.numpy as jnp
from jax import lax

D = 2048
H = 8
F = 64
HID = 256
MB = 256
STOK = 256
NSEQ = 4
NSEG = 4
LEN = 1024


def block_scale(key, dims, pieces, least, high):
    def one(dim, blocks):
        heights = jax.random.uniform(jax.random.fold_in(jax.random.fold_in(key, 6), dim), (blocks,), jnp.float32, least / len(pieces), high / len(pieces))
        return jnp.repeat(jnp.exp(heights), dims[dim] // blocks).reshape((-1,) + (1,) * (len(dims) - dim - 1))

    gain = one(*pieces[0])
    for cut in pieces[1:]:
        gain = gain * one(*cut)
    return gain


def normal_values(rng, extent, width, limit, shards=(), dtype=jnp.bfloat16):
    gain = block_scale(rng, extent, shards, -0.22, 0.18) if shards else 1.0
    drawn = jax.random.normal(rng, extent, jnp.float32) * width * gain
    return jnp.minimum(jnp.maximum(drawn, -limit), limit).astype(dtype)


def setup_inputs(seed: int = 0, part: int = 0) -> dict:
    key_list = jax.random.split(jax.random.key(seed), 6)
    part_splits = jax.random.split(jax.random.fold_in(key_list[5], part), 6)
    layer_input = normal_values(part_splits[0], (NSEQ, LEN, D), 1.0, 6.0, ((0, 4), (1, 4)))
    out_cot = normal_values(part_splits[1], (NSEQ, LEN, H * F), 1.0, 6.0, ((0, 4), (1, 4)))
    w_proj = normal_values(key_list[2], (D, 3 * H * F), D ** -0.5, 0.125, ((0, 4),))
    inner_start = normal_values(part_splits[3], (NSEQ, NSEG, 2, H, F, HID), 0.1, 1.5, ((0, 4), (1, 4)), jnp.float32)
    rates = jnp.clip(jnp.exp(jax.random.uniform(key_list[4], (H,), jnp.float32, math.log(0.01), math.log(0.06))), 0.01, 0.06)
    return {"layer_input": layer_input, "out_cot": out_cot, "w_proj": w_proj, "inner_start": inner_start, "rates": rates}


HIGH = lax.Precision.HIGHEST

def predict(first, second, inputs):
    hidden = jax.nn.gelu(jnp.einsum('thf,hfk->thk', inputs, first, precision=HIGH))
    return jnp.einsum('thk,hfk->thf', hidden, second, precision=HIGH)

def segment_map(inner, queries, keys, values, rates):
    first = inner[0]
    second = inner[1]
    blocks = queries.shape[0] // MB
    outputs = []
    for block in range(blocks):
        lower = block * MB
        key_rows = keys[lower:lower + MB]
        value_rows = values[lower:lower + MB]
        query_rows = queries[lower:lower + MB]

        def inner_loss(first_w, second_w):
            resid = key_rows + predict(first_w, second_w, key_rows) - value_rows
            return 0.5 * jnp.sum(resid * resid) / MB
        grad_first, grad_second = jax.grad(inner_loss, argnums=(0, 1))(first, second)
        first = first - rates[:, None, None] * grad_first
        second = second - rates[:, None, None] * grad_second
        outputs.append(query_rows + predict(first, second, query_rows))
    return (jnp.stack([first, second]), jnp.concatenate(outputs, 0))

def reference(layer_input, out_cot, w_proj, inner_start, rates):
    flat_input = layer_input.reshape(NSEQ * LEN, D).astype(jnp.float32)
    weights = w_proj.astype(jnp.float32)
    qkv = jnp.dot(flat_input, weights, precision=HIGH).astype(jnp.bfloat16)
    qkv = qkv.reshape(NSEQ, NSEG, STOK, 3, H, F)
    cots = out_cot.reshape(NSEQ, NSEG, STOK, H, F)

    def one_sequence(qkv_seq, cot_seq, inner_seq):
        qkv_float = qkv_seq.astype(jnp.float32)
        cot_float = cot_seq.astype(jnp.float32)

        def step(carry, item):
            qkv_seg, cot_seg, inner_seg = item

            def local(inner_a, queries, keys, values):
                return segment_map(inner_a, queries, keys, values, rates)
            _, pull = jax.vjp(local, inner_seg, qkv_seg[:, 0], qkv_seg[:, 1], qkv_seg[:, 2])
            grad_seg, grad_q, grad_k, grad_v = pull((carry, cot_seg))
            return (grad_seg, (grad_seg, jnp.stack([grad_q, grad_k, grad_v], 1)))
        start = jnp.zeros(inner_seq.shape[1:], jnp.float32)
        _, outs = lax.scan(step, start, (qkv_float, cot_float, inner_seq), reverse=True)
        return outs
    grad_inner, grad_qkv = jax.vmap(one_sequence)(qkv, cots, inner_start)
    qkv_grad = grad_qkv.reshape(NSEQ * LEN, 3 * H * F).astype(jnp.bfloat16)
    qkv_grad_f = qkv_grad.astype(jnp.float32)
    grad_input = jnp.dot(qkv_grad_f, weights.T, precision=HIGH).astype(jnp.bfloat16)
    grad_proj = jnp.dot(flat_input.T, qkv_grad_f, precision=HIGH)
    return (grad_input.reshape(NSEQ, LEN, D), grad_proj, grad_inner)
```

```python
import functools

import jax
import jax.numpy as jnp
from jax import lax
from jax.experimental import pallas as pl
from jax.experimental.pallas import tpu as pltpu
from jax.sharding import PartitionSpec as P

MB = 256
BF = jnp.bfloat16
F32 = jnp.float32
CORES = 2
GELU_A = 0.7978845608028654
GELU_B = 0.044715
VMEM = 56 * 1024 * 1024


def dot(a, b, ca, cb):
    return lax.dot_general(a, b, (((ca,), (cb,)), ((), ())), preferred_element_type=F32)


def gelu_parts(u):
    square = u * u
    tanh = jnp.tanh(u * (GELU_A + (GELU_A * GELU_B) * square))
    half = 0.5 * (1.0 + tanh)
    sech = 1.0 - tanh * tanh
    slope = GELU_A + (3.0 * GELU_A * GELU_B) * square
    return square, tanh, half, sech, slope


def inner_kernel(dims, table, rates, *refs):
    nseg, nseq, hpd, feats, hid, tokens, chunk = dims
    li = refs[:nseg]
    wt = refs[nseg : nseg + nseq]
    inner = refs[nseg + nseq : 2 * nseg + nseq]
    cot = refs[2 * nseg + nseq : 3 * nseg + nseq]
    gp, gq, gi = refs[3 * nseg + nseq : 3 * nseg + nseq + 3]
    qkv, wts, cts, ht, rt, g1, g2p, gu, gab = refs[3 * nseg + nseq + 3 :]
    rows = 3 * hpd * feats

    for slot in range(nseg):
        total = jnp.zeros((rows, tokens), F32)
        for back in range(nseq):
            at = pl.multiple_of(table[nseg + back] * chunk, chunk)
            total += dot(wt[back][...], li[slot][:, pl.ds(at, chunk)], 1, 1)
        qkv[slot] = total.astype(BF).reshape(3, hpd, feats, tokens)
        wts[slot] = inner[slot][...].reshape(2, hpd, feats, hid)
        cts[slot] = cot[slot][...].reshape(hpd, feats, tokens)

    def local(index, carry):
        slot = index // hpd
        head = index % hpd
        rate = rates[table[nseg + nseq] + head] * (1.0 / MB)
        a_b, b_b = wts[slot, 0, head], wts[slot, 1, head]
        q_b, k_b, v_b = qkv[slot, 0, head], qkv[slot, 1, head], qkv[slot, 2, head]
        c_b = cts[slot, head]
        u = dot(a_b, k_b, 0, 0)
        square, tanh, half, sech, slope = gelu_parts(u)
        h_b = (u * half).astype(BF)
        first = half + 0.5 * u * sech * slope
        second = sech * (GELU_A + (6.0 * GELU_A * GELU_B) * square - u * tanh * slope * slope)
        ht[slot, head] = h_b
        g1[slot, head] = first
        resid = k_b.astype(F32) - v_b.astype(F32) + dot(b_b, h_b, 1, 0)
        r_b = resid.astype(BF)
        rt[slot, head] = r_b
        p = dot(b_b, r_b, 0, 0)
        g2p[slot, head] = second * p
        gu_b = (first * p).astype(BF)
        gu[slot, head] = gu_b
        new_a = (a_b.astype(F32) - rate * dot(k_b, gu_b, 1, 1)).astype(BF)
        new_b = (b_b.astype(F32) - rate * dot(r_b, h_b, 1, 1)).astype(BF)
        uq = dot(new_a, q_b, 0, 0)
        square, tanh, half, sech, slope = gelu_parts(uq)
        hq_b = (uq * half).astype(BF)
        guq_b = ((half + 0.5 * uq * sech * slope) * dot(new_b, c_b, 0, 0)).astype(BF)
        gab[slot, 0, head] = dot(q_b, guq_b, 1, 1)
        gab[slot, 1, head] = dot(c_b, hq_b, 1, 1)
        gq[slot, 0, head] = (c_b.astype(F32) + dot(new_a, guq_b, 1, 0)).astype(BF)
        return carry

    lax.fori_loop(0, nseg * hpd, local, 0)

    def step(turn, carry):
        slot = table[nseg - 1 - turn]
        result = []
        for head in range(hpd):
            rate = rates[table[nseg + nseq] + head] * (1.0 / MB)
            t_a = carry[head][0] + gab[slot, 0, head]
            t_b = carry[head][1] + gab[slot, 1, head]
            a_b, b_b = wts[slot, 0, head], wts[slot, 1, head]
            k_b = qkv[slot, 1, head]
            h_b, r_b, gu_b = ht[slot, head], rt[slot, head], gu[slot, head]
            ta_b, tb_b = t_a.astype(BF), t_b.astype(BF)
            du = dot(ta_b, k_b, 0, 0)
            dh_b = (g1[slot, head] * du).astype(BF)
            dr = dot(b_b, dh_b, 1, 0) + dot(tb_b, h_b, 1, 0)
            dr_b = dr.astype(BF)
            dp = dot(b_b, dr_b, 0, 0) + dot(tb_b, r_b, 0, 0)
            dgu_b = (g2p[slot, head] * du + g1[slot, head] * dp).astype(BF)
            c_a = t_a - rate * dot(k_b, dgu_b, 1, 1)
            c_b = t_b - rate * (dot(dr_b, h_b, 1, 1) + dot(r_b, dh_b, 1, 1))
            left = jnp.concatenate([a_b, ta_b], 1)
            gk = dr + dot(left, jnp.concatenate([dgu_b, gu_b], 0), 1, 0)
            gq[slot, 1, head] = (-rate * gk).astype(BF)
            gq[slot, 2, head] = (rate * dr).astype(BF)
            gi[slot, 0, head] = c_a.astype(BF)
            gi[slot, 1, head] = c_b.astype(BF)
            result.append((c_a, c_b))
        return tuple(result)

    zero = jnp.zeros((feats, hid), F32)
    lax.fori_loop(0, nseg, step, tuple((zero, zero) for _ in range(hpd)))

    for piece in range(nseq):
        total = jnp.zeros((rows, chunk), F32)
        for slot in range(nseg):
            part = li[slot][:, piece * chunk : (piece + 1) * chunk]
            total += dot(gq[slot].reshape(rows, tokens), part, 1, 0)
        gp[piece] = total.astype(BF)


def input_kernel(nseg, nseq, chunk, table, gq, *refs):
    wt = refs[:nseq]
    out = refs[nseq]
    for back in range(nseq):
        at = pl.multiple_of(table[nseg + back] * chunk, chunk)
        for slot in range(nseg):
            value = dot(gq[slot].reshape(-1, gq.shape[-1]), wt[back][...], 0, 0)
            out[slot, :, pl.ds(at, chunk)] = value.astype(BF)


def per_device(layer_input, out_cot, w_proj, inner_start, rates):
    rows = layer_input[0]
    tokens, width = rows.shape
    heads = rates.shape[0]
    feats, hid = inner_start.shape[4:]
    nseg, nseq = lax.axis_size("seg"), lax.axis_size("seq")
    chips = nseg // CORES
    hpd = heads // nseg
    own = hpd * feats
    chunk = width // nseq
    me, place = lax.axis_index("seg"), lax.axis_index("seq")
    chip, core = me // CORES, me % CORES
    slots = [(dx, dc) for dx in range(chips) for dc in range(CORES)]

    def other(index, dx, dc):
        return ((index // CORES + dx) % chips) * CORES + (index % CORES + dc) % CORES

    def to_seg(value, dx, dc):
        if dx % chips == 0 and dc == 0:
            return value
        return lax.ppermute(value, "seg", [(i, other(i, dx, dc)) for i in range(nseg)])

    def to_seq(value, dz):
        return lax.ppermute(value, "seq", [(i, (i + dz) % nseq) for i in range(nseq)])

    def pick(values, order):
        return jnp.stack(
            [lax.dynamic_index_in_dim(values, order[i], 0, keepdims=False) for i in range(nseg)]
        )

    columns = w_proj.reshape(chunk, 3, nseg, own)
    mine = lax.dynamic_index_in_dim(columns, me, 2, keepdims=False)
    mine = mine.transpose(1, 2, 0).reshape(3 * own, chunk)
    wt = [mine] + [to_seq(mine, dz) for dz in range(1, nseq)]

    far = [to_seg(rows, dx, 0) for dx in range(chips)]
    near = [to_seg(value, 0, 1) for value in far]
    li = [value for pair in zip(far, near) for value in pair]

    start = inner_start[0, 0].astype(BF).reshape(2, nseg, own, hid)
    cots = out_cot[0].T.reshape(nseg, own, tokens)
    inner, cot = [], []
    for dx, dc in slots:
        dest = other(me, dx, dc)
        piece = lax.dynamic_index_in_dim(start, dest, 1, keepdims=False)
        inner.append(to_seg(piece, dx, dc))
        cot.append(to_seg(lax.dynamic_index_in_dim(cots, dest, 0, keepdims=False), dx, dc))

    segs = jnp.arange(nseg, dtype=jnp.int32)
    slot_of = ((chip - segs // CORES) % chips) * CORES + (core + segs) % CORES
    back = (place - jnp.arange(nseq, dtype=jnp.int32)) % nseq
    table = jnp.concatenate([slot_of, back, (me * hpd)[None]]).astype(jnp.int32)

    dims = (nseg, nseq, hpd, feats, hid, tokens, chunk)
    smem = pl.BlockSpec(memory_space=pltpu.SMEM)
    vmem = pl.BlockSpec(memory_space=pltpu.VMEM)
    gp, gq, gi = pl.pallas_call(
        functools.partial(inner_kernel, dims),
        in_specs=[smem, smem] + [vmem] * (3 * nseg + nseq),
        out_specs=[vmem] * 3,
        out_shape=[
            jax.ShapeDtypeStruct((nseq, 3 * own, chunk), BF),
            jax.ShapeDtypeStruct((nseg, 3, hpd, feats, tokens), BF),
            jax.ShapeDtypeStruct((nseg, 2, hpd, feats, hid), BF),
        ],
        scratch_shapes=[
            pltpu.VMEM((nseg, 3, hpd, feats, tokens), BF),
            pltpu.VMEM((nseg, 2, hpd, feats, hid), BF),
            pltpu.VMEM((nseg, hpd, feats, tokens), BF),
            pltpu.VMEM((nseg, hpd, hid, tokens), BF),
            pltpu.VMEM((nseg, hpd, feats, tokens), BF),
            pltpu.VMEM((nseg, hpd, hid, tokens), F32),
            pltpu.VMEM((nseg, hpd, hid, tokens), F32),
            pltpu.VMEM((nseg, hpd, hid, tokens), BF),
            pltpu.VMEM((nseg, 2, hpd, feats, hid), F32),
        ],
        compiler_params=pltpu.CompilerParams(vmem_limit_bytes=VMEM),
        cost_estimate=pl.CostEstimate(
            flops=40 * 10**9, bytes_accessed=10**7, transcendentals=10**6
        ),
        name="inner",
    )(table, rates, *li, *wt, *inner, *cot)

    total = lax.dynamic_index_in_dim(gp, place, 0, keepdims=False).astype(F32)
    for dz in range(1, nseq):
        piece = lax.dynamic_index_in_dim(gp, (place + dz) % nseq, 0, keepdims=False)
        total += to_seq(piece, dz).astype(F32)
    far = jnp.stack([to_seg(total, dx, 0) for dx in range(chips)])
    near = to_seg(far, 0, 1)
    both = jnp.stack([far, near], 1).reshape(nseg, 3, hpd, feats, chunk)
    ordered = pick(both, slot_of)
    grad_proj = ordered.transpose(4, 1, 0, 2, 3).reshape(chunk, 3 * heads * feats)

    part = pl.pallas_call(
        functools.partial(input_kernel, nseg, nseq, chunk),
        in_specs=[smem] + [vmem] * (1 + nseq),
        out_specs=vmem,
        out_shape=jax.ShapeDtypeStruct((nseg, tokens, width), BF),
        compiler_params=pltpu.CompilerParams(vmem_limit_bytes=VMEM),
        cost_estimate=pl.CostEstimate(flops=3 * 10**9, bytes_accessed=10**7, transcendentals=0),
        name="input",
    )(table, gq, *wt)
    part = part.reshape(chips, CORES, tokens, width)
    summed = part[:, 0].astype(F32) + to_seg(part[:, 1], 0, 1).astype(F32)
    grad_input = summed[0]
    for dx in range(1, chips):
        grad_input += to_seg(summed[dx].astype(BF), -dx, 0).astype(F32)

    pieces = jnp.stack([to_seg(gi[i], -dx, dc) for i, (dx, dc) in enumerate(slots)])
    source = ((segs // CORES - chip) % chips) * CORES + (core + segs) % CORES
    grad_inner = pick(pieces, source).transpose(1, 0, 2, 3, 4)
    grad_inner = grad_inner.reshape(2, heads, feats, hid).astype(F32)
    return (grad_input.astype(BF)[None], grad_proj, grad_inner[None, None])


def solution(mesh):
    placed = (
        P(("groups", "seq"), "seg", None),
        P(("groups", "seq"), "seg", None),
        P("seq", None),
        P(("groups", "seq"), "seg", None, None, None, None),
        P(),
    )
    return jax.shard_map(
        per_device,
        mesh=mesh,
        in_specs=placed,
        out_specs=(
            P(("groups", "seq"), "seg", None),
            P(("groups", "seq"), None),
            P(("groups", "seq"), "seg", None, None, None, None),
        ),
        check_vma=False,
    )
```

```python
import functools

import jax
import jax.numpy as jnp
from jax import lax
from jax.experimental import pallas as pl
from jax.experimental.pallas import tpu as pltpu
from jax.sharding import PartitionSpec as P

MB = 256
BF = jnp.bfloat16
F32 = jnp.float32
CORES = 2
GELU_A = 0.7978845608028654
GELU_B = 0.044715
VMEM = 56 * 1024 * 1024


def dot(a, b, ca, cb):
    return lax.dot_general(a, b, (((ca,), (cb,)), ((), ())), preferred_element_type=F32)


def gelu_parts(u):
    square = u * u
    tanh = jnp.tanh(u * (GELU_A + (GELU_A * GELU_B) * square))
    half = 0.5 * (1.0 + tanh)
    sech = 1.0 - tanh * tanh
    slope = GELU_A + (3.0 * GELU_A * GELU_B) * square
    return square, tanh, half, sech, slope


def prep_kernel(dims, table, w, cots, start, mine, *refs):
    nseg, nseq, hpd, feats, hid, tokens, chunk = dims
    packs = refs[:nseg]
    block, turned = refs[nseg:]
    own = hpd * feats
    total = own * nseg
    wide = block.shape[0]
    me = table[nseg + nseq + 1]
    base = me * own // wide * wide
    for part in range(3):
        at = pl.multiple_of(part * total + base, wide)
        block[...] = w[:, pl.ds(at, wide)].T
        rest = pl.multiple_of(me * own - base, own)
        mine[part * own : (part + 1) * own] = block[pl.ds(rest, own)]
    turned[...] = cots[...].T
    for slot in range(nseg):
        dest = table[nseg + nseq + 2 + slot]
        piece = start[:, pl.ds(dest * hpd, hpd)].astype(BF)
        packs[slot][: 2 * own] = piece.reshape(2 * own, hid)
        packs[slot][2 * own :] = turned[pl.ds(pl.multiple_of(dest * own, own), own)]


def inner_kernel(dims, table, rates, *refs):
    nseg, nseq, hpd, feats, hid, tokens, chunk = dims
    li, refs = refs[:nseg], refs[nseg:]
    wt, refs = refs[:nseq], refs[nseq:]
    packs, refs = refs[:nseg], refs[nseg:]
    gp, refs = refs[:nseq], refs[nseq:]
    gq, refs = refs[0], refs[1:]
    gi, refs = refs[:nseg], refs[nseg:]
    qkv, wts, cts, ht, rt, g1, g2p, gu, gab, gis = refs
    own = hpd * feats
    rows = 3 * own

    for slot in range(nseg):
        total = jnp.zeros((rows, tokens), F32)
        for back in range(nseq):
            at = pl.multiple_of(table[nseg + back] * chunk, chunk)
            total += dot(wt[back][...], li[slot][:, pl.ds(at, chunk)], 1, 1)
        qkv[slot] = total.astype(BF).reshape(3, hpd, feats, tokens)
        wts[slot] = packs[slot][: 2 * own].reshape(2, hpd, feats, hid)
        cts[slot] = packs[slot][2 * own :].reshape(hpd, feats, tokens)

    def local(index, carry):
        slot = index // hpd
        head = index % hpd
        rate = rates[table[nseg + nseq] + head] * (1.0 / MB)
        a_b, b_b = wts[slot, 0, head], wts[slot, 1, head]
        q_b, k_b, v_b = qkv[slot, 0, head], qkv[slot, 1, head], qkv[slot, 2, head]
        c_b = cts[slot, head]
        u = dot(a_b, k_b, 0, 0)
        square, tanh, half, sech, slope = gelu_parts(u)
        h_b = (u * half).astype(BF)
        first = half + 0.5 * u * sech * slope
        second = sech * (GELU_A + (6.0 * GELU_A * GELU_B) * square - u * tanh * slope * slope)
        ht[slot, head] = h_b
        g1[slot, head] = first
        resid = k_b.astype(F32) - v_b.astype(F32) + dot(b_b, h_b, 1, 0)
        r_b = resid.astype(BF)
        rt[slot, head] = r_b
        p = dot(b_b, r_b, 0, 0)
        g2p[slot, head] = second * p
        gu_b = (first * p).astype(BF)
        gu[slot, head] = gu_b
        new_a = (a_b.astype(F32) - rate * dot(k_b, gu_b, 1, 1)).astype(BF)
        new_b = (b_b.astype(F32) - rate * dot(r_b, h_b, 1, 1)).astype(BF)
        uq = dot(new_a, q_b, 0, 0)
        square, tanh, half, sech, slope = gelu_parts(uq)
        hq_b = (uq * half).astype(BF)
        guq_b = ((half + 0.5 * uq * sech * slope) * dot(new_b, c_b, 0, 0)).astype(BF)
        gab[slot, 0, head] = dot(q_b, guq_b, 1, 1)
        gab[slot, 1, head] = dot(c_b, hq_b, 1, 1)
        gq[slot, 0, head] = (c_b.astype(F32) + dot(new_a, guq_b, 1, 0)).astype(BF)
        return carry

    lax.fori_loop(0, nseg * hpd, local, 0)

    def step(turn, carry):
        slot = table[nseg - 1 - turn]
        result = []
        for head in range(hpd):
            rate = rates[table[nseg + nseq] + head] * (1.0 / MB)
            t_a = carry[head][0] + gab[slot, 0, head]
            t_b = carry[head][1] + gab[slot, 1, head]
            a_b, b_b = wts[slot, 0, head], wts[slot, 1, head]
            k_b = qkv[slot, 1, head]
            h_b, r_b, gu_b = ht[slot, head], rt[slot, head], gu[slot, head]
            ta_b, tb_b = t_a.astype(BF), t_b.astype(BF)
            du = dot(ta_b, k_b, 0, 0)
            dh_b = (g1[slot, head] * du).astype(BF)
            dr = dot(b_b, dh_b, 1, 0) + dot(tb_b, h_b, 1, 0)
            dr_b = dr.astype(BF)
            dp = dot(b_b, dr_b, 0, 0) + dot(tb_b, r_b, 0, 0)
            dgu_b = (g2p[slot, head] * du + g1[slot, head] * dp).astype(BF)
            c_a = t_a - rate * dot(k_b, dgu_b, 1, 1)
            c_b = t_b - rate * (dot(dr_b, h_b, 1, 1) + dot(r_b, dh_b, 1, 1))
            left = jnp.concatenate([a_b, ta_b], 1)
            gk = dr + dot(left, jnp.concatenate([dgu_b, gu_b], 0), 1, 0)
            gq[slot, 1, head] = (-rate * gk).astype(BF)
            gq[slot, 2, head] = (rate * dr).astype(BF)
            gis[slot, 0, head] = c_a.astype(BF)
            gis[slot, 1, head] = c_b.astype(BF)
            result.append((c_a, c_b))
        return tuple(result)

    zero = jnp.zeros((feats, hid), F32)
    lax.fori_loop(0, nseg, step, tuple((zero, zero) for _ in range(hpd)))

    for slot in range(nseg):
        gi[slot][...] = gis[slot]
    for dz in range(nseq):
        at = pl.multiple_of(table[nseg + (nseq - dz) % nseq] * chunk, chunk)
        total = jnp.zeros((rows, chunk), F32)
        for slot in range(nseg):
            total += dot(gq[slot].reshape(rows, tokens), li[slot][:, pl.ds(at, chunk)], 1, 0)
        gp[dz][...] = total.astype(gp[dz].dtype)


def input_kernel(nseg, nseq, chunk, table, gq, *refs):
    wt = refs[:nseq]
    outs = refs[nseq:]
    for slot in range(nseg):
        left = gq[slot].reshape(-1, gq.shape[-1])
        for back in range(nseq):
            at = pl.multiple_of(table[nseg + back] * chunk, chunk)
            value = dot(left, wt[back][...], 0, 0)
            outs[slot % CORES][slot // CORES, :, pl.ds(at, chunk)] = value.astype(BF)


def sum_kernel(*refs):
    total = refs[0][...]
    for ref in refs[1:-1]:
        total += ref[...].astype(F32)
    refs[-1][...] = total.T.astype(BF)


def join_kernel(dims, table, *refs):
    nseg, nseq, hpd, feats, hid, tokens, chunk = dims
    chips = nseg // CORES
    far, near, out = refs[:chips], refs[chips], refs[chips + 1]
    own = hpd * feats
    me = table[nseg + nseq + 1]
    chip = me // CORES
    even = me % CORES == 0
    for dx in range(chips):
        source = (chip - dx + chips) % chips
        for part in range(3):
            a = far[dx][:, part * own : (part + 1) * own].astype(F32)
            b = near[dx, :, part * own : (part + 1) * own].astype(F32)
            left, right = jnp.where(even, a, b), jnp.where(even, b, a)
            at = pl.multiple_of(part * nseg * own + source * CORES * own, CORES * own)
            out[:, pl.ds(at, CORES * own)] = jnp.concatenate([left, right], 1)


def weights_kernel(dims, table, *refs):
    nseg, nseq, hpd = dims[:3]
    out = refs[nseg]
    for slot in range(nseg):
        source = table[nseg + nseq + 2 + slot]
        out[:, pl.ds(source * hpd, hpd)] = refs[slot][...].astype(F32)


def per_device(layer_input, out_cot, w_proj, inner_start, rates):
    rows = layer_input[0]
    tokens, width = rows.shape
    heads = rates.shape[0]
    feats, hid = inner_start.shape[4:]
    nseg, nseq = lax.axis_size("seg"), lax.axis_size("seq")
    chips = nseg // CORES
    hpd = heads // nseg
    own = hpd * feats
    chunk = width // nseq
    me, place = lax.axis_index("seg"), lax.axis_index("seq")
    chip, core = me // CORES, me % CORES
    slots = [(dx, dc) for dx in range(chips) for dc in range(CORES)]

    def other(index, dx, dc):
        return ((index // CORES + dx) % chips) * CORES + (index % CORES + dc) % CORES

    def to_seg(value, dx, dc):
        if dx % chips == 0 and dc == 0:
            return value
        return lax.ppermute(value, "seg", [(i, other(i, dx, dc)) for i in range(nseg)])

    def to_seq(value, dz):
        return lax.ppermute(value, "seq", [(i, (i + dz) % nseq) for i in range(nseq)])

    def kernel(body, name, outs, scratch, flops, *operands):
        smem = pl.BlockSpec(memory_space=pltpu.SMEM)
        vmem = pl.BlockSpec(memory_space=pltpu.VMEM)
        moved = sum(o.size * o.dtype.itemsize for o in [*operands, *outs])
        return pl.pallas_call(
            body,
            in_specs=[smem if o.ndim == 1 else vmem for o in operands],
            out_specs=[vmem] * len(outs),
            out_shape=outs,
            scratch_shapes=scratch,
            compiler_params=pltpu.CompilerParams(vmem_limit_bytes=VMEM),
            cost_estimate=pl.CostEstimate(flops=flops, bytes_accessed=moved, transcendentals=0),
            name=name,
        )(*operands)

    def array(shape, dtype):
        return jax.ShapeDtypeStruct(shape, dtype)

    segs = jnp.arange(nseg, dtype=jnp.int32)
    slot_of = ((chip - segs // CORES) % chips) * CORES + (core + segs) % CORES
    back = (place - jnp.arange(nseq, dtype=jnp.int32)) % nseq
    dest = ((chip + segs // CORES) % chips) * CORES + (core + segs) % CORES
    table = jnp.concatenate([slot_of, back, jnp.stack([me * hpd, me]), dest]).astype(jnp.int32)
    dims = (nseg, nseq, hpd, feats, hid, tokens, chunk)

    mine, *packs = kernel(
        functools.partial(prep_kernel, dims),
        "prep",
        [array((3 * own, chunk), BF)] + [array((3 * own, tokens), BF)] * nseg,
        [pltpu.VMEM((max(own, 128), chunk), BF), pltpu.VMEM((heads * feats, tokens), BF)],
        10**6,
        table,
        w_proj,
        out_cot[0],
        inner_start[0, 0],
    )
    rows, mine, *packs = lax.optimization_barrier((rows, mine, *packs))
    wt = [mine] + [to_seq(mine, dz) for dz in range(1, nseq)]
    far = [to_seg(rows, dx, 0) for dx in range(chips)]
    near = [to_seg(value, 0, 1) for value in far]
    li = [value for pair in zip(far, near) for value in pair]
    packs = [to_seg(packs[i], dx, dc) for i, (dx, dc) in enumerate(slots)]

    outs = kernel(
        functools.partial(inner_kernel, dims),
        "inner",
        [array((3 * own, chunk), BF if dz else F32) for dz in range(nseq)]
        + [array((nseg, 3, hpd, feats, tokens), BF)]
        + [array((2, hpd, feats, hid), BF)] * nseg,
        [
            pltpu.VMEM((nseg, 3, hpd, feats, tokens), BF),
            pltpu.VMEM((nseg, 2, hpd, feats, hid), BF),
            pltpu.VMEM((nseg, hpd, feats, tokens), BF),
            pltpu.VMEM((nseg, hpd, hid, tokens), BF),
            pltpu.VMEM((nseg, hpd, feats, tokens), BF),
            pltpu.VMEM((nseg, hpd, hid, tokens), F32),
            pltpu.VMEM((nseg, hpd, hid, tokens), F32),
            pltpu.VMEM((nseg, hpd, hid, tokens), BF),
            pltpu.VMEM((nseg, 2, hpd, feats, hid), F32),
            pltpu.VMEM((nseg, 2, hpd, feats, hid), BF),
        ],
        20 * 10**9,
        table,
        rates,
        *li,
        *wt,
        *packs,
    )
    gp, gq, gi = outs[:nseq], outs[nseq], outs[nseq + 1 :]

    got = [to_seq(gp[dz], dz) for dz in range(1, nseq)]

    keep, send = kernel(
        functools.partial(input_kernel, nseg, nseq, chunk),
        "input",
        [array((chips, tokens, width), BF)] * CORES,
        [],
        3 * 10**9,
        table,
        gq,
        *wt,
    )
    summed = keep.astype(F32) + to_seg(send, 0, 1).astype(F32)
    grad_input = summed[0]
    for dx in range(1, chips):
        grad_input += to_seg(summed[dx].astype(BF), -dx, 0).astype(F32)

    (grad_inner,) = kernel(
        functools.partial(weights_kernel, dims),
        "weights",
        [array((2, heads, feats, hid), F32)],
        [],
        10**6,
        table,
        *[to_seg(gi[i], -dx, dc) for i, (dx, dc) in enumerate(slots)],
    )

    (total,) = kernel(sum_kernel, "sum", [array((chunk, 3 * own), BF)], [], 10**6, gp[0], *got)
    far = [to_seg(total, dx, 0) for dx in range(chips)]
    near = to_seg(jnp.stack(far), 0, 1)
    (grad_proj,) = kernel(
        functools.partial(join_kernel, dims),
        "join",
        [array((chunk, 3 * heads * feats), F32)],
        [],
        10**6,
        table,
        *far,
        near,
    )
    return (grad_input.astype(BF)[None], grad_proj, grad_inner[None, None])


def solution(mesh):
    placed = (
        P(("groups", "seq"), "seg", None),
        P(("groups", "seq"), "seg", None),
        P("seq", None),
        P(("groups", "seq"), "seg", None, None, None, None),
        P(),
    )
    return jax.shard_map(
        per_device,
        mesh=mesh,
        in_specs=placed,
        out_specs=(
            P(("groups", "seq"), "seg", None),
            P(("groups", "seq"), None),
            P(("groups", "seq"), "seg", None, None, None, None),
        ),
        check_vma=False,
    )
```

```python
import functools

import jax
import jax.numpy as jnp
from jax import lax
from jax.experimental import pallas as pl
from jax.experimental.pallas import tpu as pltpu
from jax.sharding import PartitionSpec as P

MB = 256
BF = jnp.bfloat16
F32 = jnp.float32
CORES = 2
GELU_A = 0.7978845608028654
GELU_B = 0.044715
MIB = 1024 * 1024


def dot(a, b, ca, cb):
    return lax.dot_general(a, b, (((ca,), (cb,)), ((), ())), preferred_element_type=F32)


def gelu_parts(u):
    square = u * u
    tanh = jnp.tanh(u * (GELU_A + (GELU_A * GELU_B) * square))
    half = 0.5 * (1.0 + tanh)
    sech = 1.0 - tanh * tanh
    slope = GELU_A + (3.0 * GELU_A * GELU_B) * square
    return square, tanh, half, sech, slope


def prep_kernel(dims, table, w, cots, start, mine, keep, send, block, turned):
    nseg, nseq, hpd, feats, hid, tokens, chunk = dims
    own = hpd * feats
    total = own * nseg
    wide = block.shape[0]
    me = table[nseg + nseq + 1]
    base = me * own // wide * wide
    for part in range(3):
        at = pl.multiple_of(part * total + base, wide)
        block[...] = w[:, pl.ds(at, wide)].T
        rest = pl.multiple_of(me * own - base, own)
        mine[part * own : (part + 1) * own] = block[pl.ds(rest, own)]
    turned[...] = cots[...].T
    for slot in range(nseg):
        dest = table[nseg + nseq + 2 + slot]
        piece = start[:, pl.ds(dest * hpd, hpd)].astype(BF)
        pack = (keep, send)[slot % CORES]
        pack[slot // CORES, : 2 * own] = piece.reshape(2 * own, hid)
        pack[slot // CORES, 2 * own :] = turned[pl.ds(pl.multiple_of(dest * own, own), own)]


def inner_kernel(dims, head, before, table, rates, *refs):
    nseg, nseq, hpd, feats, hid, tokens, chunk = dims
    chips = nseg // CORES
    li, refs = refs[:nseg], refs[nseg:]
    wt, refs = refs[:nseq], refs[nseq:]
    keep, got, refs = refs[0], refs[1], refs[2:]
    hops, refs = refs[: chips - 1], refs[chips - 1 :]
    earlier, refs = refs[:before], refs[before:]
    gp, refs = refs[:nseq], refs[nseq:]
    gq, stay, leave, qkv, wts, cts, ht, rt, g1, g2p, gu, gab = refs
    own = hpd * feats
    rows = 3 * feats

    for slot in range(nseg):
        dx, dc = slot // CORES, slot % CORES
        pack = ((keep, got)[dc].at[0]) if dx == 0 else hops[dx - 1].at[dc]
        total = jnp.zeros((rows, tokens), F32)
        for back in range(nseq):
            at = pl.multiple_of(table[nseg + back] * chunk, chunk)
            left = jnp.concatenate(
                [wt[back][p * own + head * feats : p * own + (head + 1) * feats] for p in range(3)]
            )
            total += dot(left, li[slot][:, pl.ds(at, chunk)], 1, 1)
        qkv[slot] = total.astype(BF).reshape(3, feats, tokens)
        wts[slot, 0] = pack[head * feats : (head + 1) * feats]
        wts[slot, 1] = pack[own + head * feats : own + (head + 1) * feats]
        cts[slot] = pack[2 * own + head * feats : 2 * own + (head + 1) * feats]
    rate = rates[table[nseg + nseq] + head] * (1.0 / MB)

    def local(slot):
        a_b, b_b = wts[slot, 0], wts[slot, 1]
        q_b, k_b, v_b = qkv[slot, 0], qkv[slot, 1], qkv[slot, 2]
        c_b = cts[slot]
        u = dot(a_b, k_b, 0, 0)
        square, tanh, half, sech, slope = gelu_parts(u)
        h_b = (u * half).astype(BF)
        first = half + 0.5 * u * sech * slope
        second = sech * (GELU_A + (6.0 * GELU_A * GELU_B) * square - u * tanh * slope * slope)
        ht[slot] = h_b
        g1[slot] = first
        resid = k_b.astype(F32) - v_b.astype(F32) + dot(b_b, h_b, 1, 0)
        r_b = resid.astype(BF)
        rt[slot] = r_b
        p = dot(b_b, r_b, 0, 0)
        g2p[slot] = second * p
        gu_b = (first * p).astype(BF)
        gu[slot] = gu_b
        new_a = (a_b.astype(F32) - rate * dot(k_b, gu_b, 1, 1)).astype(BF)
        new_b = (b_b.astype(F32) - rate * dot(r_b, h_b, 1, 1)).astype(BF)
        uq = dot(new_a, q_b, 0, 0)
        square, tanh, half, sech, slope = gelu_parts(uq)
        hq_b = (uq * half).astype(BF)
        guq_b = ((half + 0.5 * uq * sech * slope) * dot(new_b, c_b, 0, 0)).astype(BF)
        gab[slot, 0] = dot(q_b, guq_b, 1, 1)
        gab[slot, 1] = dot(c_b, hq_b, 1, 1)
        gq[slot, 0] = (c_b.astype(F32) + dot(new_a, guq_b, 1, 0)).astype(BF)

    for slot in range(nseg):
        local(slot)

    def step(turn, carry):
        slot = table[nseg - 1 - turn]
        t_a = carry[0] + gab[slot, 0]
        t_b = carry[1] + gab[slot, 1]
        a_b, b_b = wts[slot, 0], wts[slot, 1]
        k_b = qkv[slot, 1]
        h_b, r_b, gu_b = ht[slot], rt[slot], gu[slot]
        ta_b, tb_b = t_a.astype(BF), t_b.astype(BF)
        du = dot(ta_b, k_b, 0, 0)
        dh_b = (g1[slot] * du).astype(BF)
        dr = dot(b_b, dh_b, 1, 0) + dot(tb_b, h_b, 1, 0)
        dr_b = dr.astype(BF)
        dp = dot(b_b, dr_b, 0, 0) + dot(tb_b, r_b, 0, 0)
        dgu_b = (g2p[slot] * du + g1[slot] * dp).astype(BF)
        c_a = t_a - rate * dot(k_b, dgu_b, 1, 1)
        c_b = t_b - rate * (dot(dr_b, h_b, 1, 1) + dot(r_b, dh_b, 1, 1))
        left = jnp.concatenate([a_b, ta_b], 1)
        gk = dr + dot(left, jnp.concatenate([dgu_b, gu_b], 0), 1, 0)
        gq[slot, 1] = (-rate * gk).astype(BF)
        gq[slot, 2] = (rate * dr).astype(BF)
        wts[slot, 0] = c_a.astype(BF)
        wts[slot, 1] = c_b.astype(BF)
        return (c_a, c_b)

    zero = jnp.zeros((feats, hid), F32)
    carry = (zero, zero)
    for turn in range(nseg):
        carry = step(turn, carry)

    for dx in range(chips):
        for dc, out in enumerate((stay, leave)):
            if before:
                for i in range(head):
                    out[dx, :, i] = earlier[CORES * i + dc][dx, :, 0]
                out[dx, :, head] = wts[dx * CORES + dc]
            else:
                out[dx, :, 0] = wts[dx * CORES + dc]
    for dz in range(nseq):
        at = pl.multiple_of(table[nseg + (nseq - dz) % nseq] * chunk, chunk)
        total = jnp.zeros((rows, chunk), F32)
        for slot in range(nseg):
            total += dot(gq[slot].reshape(rows, tokens), li[slot][:, pl.ds(at, chunk)], 1, 0)
        gp[dz][...] = total.astype(gp[dz].dtype)


def input_kernel(dims, slots, table, *refs):
    nseg, nseq, hpd, feats, hid, tokens, chunk = dims
    gq, wt, outs = refs[:hpd], refs[hpd : hpd + nseq], refs[hpd + nseq :]
    own = hpd * feats
    for i, slot in enumerate(slots):
        left = jnp.concatenate([gq[h][slot, p] for p in range(3) for h in range(hpd)])
        for back in range(nseq):
            at = pl.multiple_of(table[nseg + back] * chunk, chunk)
            value = dot(left, wt[back][...], 0, 0)
            outs[slot % CORES][i // CORES, :, pl.ds(at, chunk)] = value.astype(BF)


def sum_kernel(dims, *refs):
    nseg, nseq, hpd, feats, hid, tokens, chunk = dims
    out = refs[-1]
    for head in range(hpd):
        total = refs[head * nseq][...]
        for ref in refs[head * nseq + 1 : (head + 1) * nseq]:
            total += ref[...].astype(F32)
        for part in range(3):
            at = (part * hpd + head) * feats
            out[:, at : at + feats] = total[part * feats : (part + 1) * feats].T.astype(BF)


def join_kernel(dims, table, *refs):
    nseg, nseq, hpd, feats, hid, tokens, chunk = dims
    chips = nseg // CORES
    far, near, out = refs[:chips], refs[chips], refs[chips + 1]
    own = hpd * feats
    me = table[nseg + nseq + 1]
    chip = me // CORES
    even = me % CORES == 0
    for dx in range(chips):
        source = (chip - dx + chips) % chips
        for part in range(3):
            a = far[dx][:, part * own : (part + 1) * own].astype(F32)
            b = near[dx, :, part * own : (part + 1) * own].astype(F32)
            left, right = jnp.where(even, a, b), jnp.where(even, b, a)
            at = pl.multiple_of(part * nseg * own + source * CORES * own, CORES * own)
            out[:, pl.ds(at, CORES * own)] = jnp.concatenate([left, right], 1)


def weights_kernel(dims, table, stay, got, *refs):
    nseg, nseq, hpd = dims[:3]
    hops, out = refs[:-1], refs[-1]
    for slot in range(nseg):
        dx, dc = slot // CORES, slot % CORES
        source = table[nseg + nseq + 2 + slot]
        piece = (stay, got)[dc][0] if dx == 0 else hops[dx - 1][dc]
        out[:, pl.ds(source * hpd, hpd)] = piece.astype(F32)


def per_device(layer_input, out_cot, w_proj, inner_start, rates):
    rows = layer_input[0]
    tokens, width = rows.shape
    heads = rates.shape[0]
    feats, hid = inner_start.shape[4:]
    nseg, nseq = lax.axis_size("seg"), lax.axis_size("seq")
    chips = nseg // CORES
    hpd = heads // nseg
    own = hpd * feats
    chunk = width // nseq
    me, place = lax.axis_index("seg"), lax.axis_index("seq")
    chip, core = me // CORES, me % CORES
    barrier = lax.optimization_barrier

    def to_chip(value, dx):
        pairs = [(i, (i + dx * CORES) % nseg) for i in range(nseg)]
        return lax.ppermute(value, "seg", pairs)

    def to_core(value):
        return lax.ppermute(value, "seg", [(i, i ^ 1) for i in range(nseg)])

    def to_seq(value, dz):
        return lax.ppermute(value, "seq", [(i, (i + dz) % nseq) for i in range(nseq)])

    def kernel(body, name, limit, cost, outs, scratch, *operands):
        smem = pl.BlockSpec(memory_space=pltpu.SMEM)
        vmem = pl.BlockSpec(memory_space=pltpu.VMEM)
        return pl.pallas_call(
            body,
            in_specs=[smem if o.ndim == 1 else vmem for o in operands],
            out_specs=[vmem] * len(outs),
            out_shape=[jax.ShapeDtypeStruct(*o) for o in outs],
            scratch_shapes=[pltpu.VMEM(*o) for o in scratch],
            compiler_params=pltpu.CompilerParams(vmem_limit_bytes=limit * MIB),
            cost_estimate=pl.CostEstimate(flops=0, bytes_accessed=cost, transcendentals=0),
            name=name,
        )(*operands)

    segs = jnp.arange(nseg, dtype=jnp.int32)
    slot_of = ((chip - segs // CORES) % chips) * CORES + (core + segs) % CORES
    back = (place - jnp.arange(nseq, dtype=jnp.int32)) % nseq
    dest = ((chip + segs // CORES) % chips) * CORES + (core + segs) % CORES
    table = jnp.concatenate([slot_of, back, jnp.stack([me * hpd, me]), dest]).astype(jnp.int32)
    dims = (nseg, nseq, hpd, feats, hid, tokens, chunk)

    mine, keep, send = kernel(
        functools.partial(prep_kernel, dims),
        "prep",
        16,
        0,
        [((3 * own, chunk), BF)] + [((chips, 3 * own, tokens), BF)] * CORES,
        [((max(own, 128), chunk), BF), ((heads * feats, tokens), BF)],
        table,
        w_proj,
        out_cot[0],
        inner_start[0, 0],
    )
    rows, mine, keep, send = barrier((rows, mine, keep, send))
    far = [to_chip(rows, dx) for dx in range(1, chips)]
    near = to_core(rows)
    got = to_core(send)
    wt = [to_seq(mine, dz) for dz in range(1, nseq - 1)]
    near, got, keep, mine = barrier((near, got, keep, mine))
    wt = [mine] + wt + [to_seq(mine, nseq - 1)]
    hops = [to_chip(jnp.stack([keep[dx], got[dx]]), dx) for dx in range(1, chips)]
    wt, far, hops = barrier((wt, far, hops))
    li = [rows, near]
    for value in far:
        li += [value, to_core(value)]

    pieces, grads, inners = [], [], []
    for head in range(hpd):
        last = head == hpd - 1
        before = len(inners) if last else 0
        sent = hpd if last else 1
        outs = kernel(
            functools.partial(inner_kernel, dims, head, before),
            "inner",
            36,
            40 * MIB,
            [((3 * feats, chunk), BF if dz else F32) for dz in range(nseq)]
            + [((nseg, 3, feats, tokens), BF)]
            + [((chips, 2, sent, feats, hid), BF)] * CORES,
            [
                ((nseg, 3, feats, tokens), BF),
                ((nseg, 2, feats, hid), BF),
                ((nseg, feats, tokens), BF),
                ((nseg, hid, tokens), BF),
                ((nseg, feats, tokens), BF),
                ((nseg, hid, tokens), F32),
                ((nseg, hid, tokens), F32),
                ((nseg, hid, tokens), BF),
                ((nseg, 2, feats, hid), F32),
            ],
            table,
            rates,
            *li,
            *wt,
            keep,
            got,
            *hops,
            *(inners if last else []),
        )
        gp = outs[:nseq]
        grads.append(outs[nseq])
        inners += outs[nseq + 1 :]
        if pieces:
            pieces, gp, grads = barrier((pieces, gp, grads))
        pieces += [gp[0]] + [to_seq(gp[dz], dz) for dz in range(1, nseq)]

    stay, leave = inners[-CORES:]
    two = range(nseg)[:CORES]
    rest = range(nseg)[CORES:]

    def partial_input(name, limit, slots, grads):
        return kernel(
            functools.partial(input_kernel, dims, slots),
            name,
            limit,
            10 * MIB,
            [((len(slots) // CORES, tokens, width), BF)] * CORES,
            [],
            table,
            *grads,
            *wt,
        )

    out, cross = partial_input("far", 16, rest, grads)
    cross, leave = to_core(cross), to_core(leave)
    cross, leave, grads = barrier((cross, leave, grads))
    out = (out.astype(F32) + cross.astype(F32)).astype(BF)
    hops = [to_chip(out[dx - 1], -dx) for dx in range(1, chips)]
    backs = [to_chip(jnp.stack([stay[dx], leave[dx]]), -dx) for dx in range(1, chips)]
    home, aside = partial_input("home", 16, two, grads)
    aside = to_core(aside)
    pieces, hops, backs, aside = barrier((pieces, hops, backs, aside))
    grad_input = home[0].astype(F32) + aside[0].astype(F32)
    for hop in hops:
        grad_input += hop.astype(F32)

    (total,) = kernel(
        functools.partial(sum_kernel, dims),
        "sum",
        12,
        0,
        [((chunk, 3 * own), BF)],
        [],
        *pieces,
    )
    far = [total] + [to_chip(total, dx) for dx in range(1, chips)]
    near = to_core(jnp.stack(far))
    (grad_inner,) = kernel(
        functools.partial(weights_kernel, dims),
        "weights",
        8,
        10 * MIB,
        [((2, heads, feats, hid), F32)],
        [],
        table,
        stay,
        leave,
        *backs,
    )
    (grad_proj,) = kernel(
        functools.partial(join_kernel, dims),
        "join",
        16,
        0,
        [((chunk, 3 * heads * feats), F32)],
        [],
        table,
        *far,
        near,
    )
    return (grad_input.astype(BF)[None], grad_proj, grad_inner[None, None])


def solution(mesh):
    placed = (
        P(("groups", "seq"), "seg", None),
        P(("groups", "seq"), "seg", None),
        P("seq", None),
        P(("groups", "seq"), "seg", None, None, None, None),
        P(),
    )
    return jax.shard_map(
        per_device,
        mesh=mesh,
        in_specs=placed,
        out_specs=(
            P(("groups", "seq"), "seg", None),
            P(("groups", "seq"), None),
            P(("groups", "seq"), "seg", None, None, None, None),
        ),
        check_vma=False,
    )
```

```python
import functools

import jax
import jax.numpy as jnp
from jax import lax
from jax.experimental import pallas as pl
from jax.experimental.pallas import tpu as pltpu
from jax.sharding import PartitionSpec as P

MB = 256
BF = jnp.bfloat16
F32 = jnp.float32
CORES = 2
GELU_A = 0.7978845608028654
GELU_B = 0.044715
MIB = 1024 * 1024


def dot(a, b, ca, cb):
    return lax.dot_general(a, b, (((ca,), (cb,)), ((), ())), preferred_element_type=F32)


def gelu_parts(u):
    square = u * u
    tanh = jnp.tanh(u * (GELU_A + (GELU_A * GELU_B) * square))
    half = 0.5 * (1.0 + tanh)
    sech = 1.0 - tanh * tanh
    slope = GELU_A + (3.0 * GELU_A * GELU_B) * square
    return square, tanh, half, sech, slope


def columns_kernel(dims, table, w, *refs):
    nseg, nseq, hpd, feats, hid, tokens, chunk = dims
    outs, block = refs[:hpd], refs[hpd]
    own = hpd * feats
    wide = block.shape[0]
    me = table[nseg + nseq + 1]
    block[...] = w[...].T
    for head in range(hpd):
        at = me * own % wide + head * feats
        outs[head][...] = block[pl.ds(pl.multiple_of(at, feats), feats)]


def packs_kernel(dims, table, cots, start, keep, send, turned):
    nseg, nseq, hpd, feats, hid, tokens, chunk = dims
    turned[...] = cots[...].T
    for slot in range(nseg):
        dest = table[nseg + nseq + 2 + slot]
        pack = (keep, send)[slot % CORES]
        for head in range(hpd):
            index = dest * hpd + head
            for half in range(2):
                rows = pl.ds(half * feats, feats)
                pack[head, slot // CORES, rows] = start[half, index].astype(BF)
            at = pl.multiple_of(index * feats, feats)
            pack[head, slot // CORES, 2 * feats :] = turned[pl.ds(at, feats)]


def inner_kernel(dims, head, table, rates, *refs):
    nseg, nseq, hpd, feats, hid, tokens, chunk = dims
    chips = nseg // CORES
    li, refs = refs[:nseg], refs[nseg:]
    wt, refs = refs[:nseq], refs[nseq:]
    keep, got, refs = refs[0], refs[1], refs[2:]
    hops, refs = refs[: chips - 1], refs[chips - 1 :]
    gp, refs = refs[:nseq], refs[nseq:]
    gq, stay, leave, qkv, wts, cts, ht, rt, g1, g2p, gu, gab = refs
    rows = 3 * feats

    for slot in range(nseg):
        dx, dc = slot // CORES, slot % CORES
        pack = ((keep, got)[dc].at[head, 0]) if dx == 0 else hops[dx - 1].at[dc]
        total = jnp.zeros((rows, tokens), F32)
        for back in range(nseq):
            at = pl.multiple_of(table[nseg + back] * chunk, chunk)
            total += dot(wt[back][...], li[slot][:, pl.ds(at, chunk)], 1, 1)
        qkv[slot] = total.astype(BF).reshape(3, feats, tokens)
        wts[slot, 0] = pack[:feats]
        wts[slot, 1] = pack[feats : 2 * feats]
        cts[slot] = pack[2 * feats :]
    rate = rates[table[nseg + nseq] + head] * (1.0 / MB)

    def local(slot):
        a_b, b_b = wts[slot, 0], wts[slot, 1]
        q_b, k_b, v_b = qkv[slot, 0], qkv[slot, 1], qkv[slot, 2]
        c_b = cts[slot]
        u = dot(a_b, k_b, 0, 0)
        square, tanh, half, sech, slope = gelu_parts(u)
        h_b = (u * half).astype(BF)
        first = half + 0.5 * u * sech * slope
        second = sech * (GELU_A + (6.0 * GELU_A * GELU_B) * square - u * tanh * slope * slope)
        ht[slot] = h_b
        g1[slot] = first
        resid = k_b.astype(F32) - v_b.astype(F32) + dot(b_b, h_b, 1, 0)
        r_b = resid.astype(BF)
        rt[slot] = r_b
        p = dot(b_b, r_b, 0, 0)
        g2p[slot] = second * p
        gu_b = (first * p).astype(BF)
        gu[slot] = gu_b
        new_a = (a_b.astype(F32) - rate * dot(k_b, gu_b, 1, 1)).astype(BF)
        new_b = (b_b.astype(F32) - rate * dot(r_b, h_b, 1, 1)).astype(BF)
        uq = dot(new_a, q_b, 0, 0)
        square, tanh, half, sech, slope = gelu_parts(uq)
        hq_b = (uq * half).astype(BF)
        guq_b = ((half + 0.5 * uq * sech * slope) * dot(new_b, c_b, 0, 0)).astype(BF)
        gab[slot, 0] = dot(q_b, guq_b, 1, 1)
        gab[slot, 1] = dot(c_b, hq_b, 1, 1)
        gq[slot, 0] = (c_b.astype(F32) + dot(new_a, guq_b, 1, 0)).astype(BF)

    for slot in range(nseg):
        local(slot)

    def step(turn, carry):
        slot = table[nseg - 1 - turn]
        t_a = carry[0] + gab[slot, 0]
        t_b = carry[1] + gab[slot, 1]
        a_b, b_b = wts[slot, 0], wts[slot, 1]
        k_b = qkv[slot, 1]
        h_b, r_b, gu_b = ht[slot], rt[slot], gu[slot]
        ta_b, tb_b = t_a.astype(BF), t_b.astype(BF)
        du = dot(ta_b, k_b, 0, 0)
        dh_b = (g1[slot] * du).astype(BF)
        dr = dot(b_b, dh_b, 1, 0) + dot(tb_b, h_b, 1, 0)
        dr_b = dr.astype(BF)
        dp = dot(b_b, dr_b, 0, 0) + dot(tb_b, r_b, 0, 0)
        dgu_b = (g2p[slot] * du + g1[slot] * dp).astype(BF)
        c_a = t_a - rate * dot(k_b, dgu_b, 1, 1)
        c_b = t_b - rate * (dot(dr_b, h_b, 1, 1) + dot(r_b, dh_b, 1, 1))
        left = jnp.concatenate([a_b, ta_b], 1)
        gk = dr + dot(left, jnp.concatenate([dgu_b, gu_b], 0), 1, 0)
        gq[slot, 1] = (-rate * gk).astype(BF)
        gq[slot, 2] = (rate * dr).astype(BF)
        wts[slot, 0] = c_a.astype(BF)
        wts[slot, 1] = c_b.astype(BF)
        return (c_a, c_b)

    zero = jnp.zeros((feats, hid), F32)
    carry = (zero, zero)
    for turn in range(nseg):
        carry = step(turn, carry)

    for dx in range(chips):
        for dc, out in enumerate((stay, leave)):
            out[dx] = wts[dx * CORES + dc]
    for dz in range(nseq):
        at = pl.multiple_of(table[nseg + (nseq - dz) % nseq] * chunk, chunk)
        total = jnp.zeros((rows, chunk), F32)
        for slot in range(nseg):
            total += dot(gq[slot].reshape(rows, tokens), li[slot][:, pl.ds(at, chunk)], 1, 0)
        gp[dz][...] = total.astype(gp[dz].dtype)


def input_kernel(dims, slots, table, *refs):
    nseg, nseq, hpd, feats, hid, tokens, chunk = dims
    gq, wt, outs = refs[:hpd], refs[hpd : hpd + hpd * nseq], refs[hpd + hpd * nseq :]
    for i, slot in enumerate(slots):
        left = jnp.concatenate([gq[h][slot].reshape(3 * feats, tokens) for h in range(hpd)])
        for back in range(nseq):
            at = pl.multiple_of(table[nseg + back] * chunk, chunk)
            right = jnp.concatenate([wt[h * nseq + back][...] for h in range(hpd)])
            value = dot(left, right, 0, 0)
            outs[slot % CORES][i // CORES, :, pl.ds(at, chunk)] = value.astype(BF)


def sum_kernel(*refs):
    total = refs[0][...]
    for ref in refs[1:-1]:
        total += ref[...].astype(F32)
    total = total.T.astype(BF)
    half = total.shape[0] // 2
    refs[-1][...] = jnp.concatenate([total[:half], total[half:]], 1)


def join_kernel(dims, table, *refs):
    nseg, nseq, hpd, feats, hid, tokens, chunk = dims
    chips = nseg // CORES
    out = refs[-1]
    wide = CORES * hpd * feats
    half = chunk // 2
    me = table[nseg + nseq + 1]
    chip = me // CORES
    even = me % CORES == 0
    for dx in range(chips):
        source = (chip - dx + chips) % chips
        for side in range(2):
            mine, other = [], []
            for head in range(hpd):
                far, near = refs[head * (chips + 1) + dx], refs[head * (chips + 1) + chips]
                mine.append(far[:, side * 3 * feats : (side + 1) * 3 * feats].astype(F32))
                other.append(near[dx, :, side * 3 * feats : (side + 1) * 3 * feats].astype(F32))
            for part in range(3):
                cut = slice(part * feats, (part + 1) * feats)
                a = jnp.concatenate([value[:, cut] for value in mine + other], 1)
                b = jnp.concatenate([value[:, cut] for value in other + mine], 1)
                at = pl.multiple_of((part * nseg * hpd * feats) + source * wide, wide)
                rows = pl.ds(side * half, half)
                out[rows, pl.ds(at, wide)] = jnp.where(even, a, b)


def weights_kernel(dims, table, *refs):
    nseg, nseq, hpd = dims[:3]
    chips = nseg // CORES
    out = refs[-1]
    for head in range(hpd):
        stay, got, *hops = refs[head * (chips + 1) : (head + 1) * (chips + 1)]
        for slot in range(nseg):
            dx, dc = slot // CORES, slot % CORES
            source = table[nseg + nseq + 2 + slot]
            piece = (stay, got)[dc][0] if dx == 0 else hops[dx - 1][dc]
            for half in range(2):
                out[half, source * hpd + head] = piece[half].astype(F32)


def per_device(layer_input, out_cot, w_proj, inner_start, rates):
    rows = layer_input[0]
    tokens, width = rows.shape
    heads = rates.shape[0]
    feats, hid = inner_start.shape[4:]
    nseg, nseq = lax.axis_size("seg"), lax.axis_size("seq")
    chips = nseg // CORES
    hpd = heads // nseg
    own = hpd * feats
    chunk = width // nseq
    me, place = lax.axis_index("seg"), lax.axis_index("seq")
    chip, core = me // CORES, me % CORES
    barrier = lax.optimization_barrier

    def to_chip(value, dx):
        pairs = [(i, (i + dx * CORES) % nseg) for i in range(nseg)]
        return lax.ppermute(value, "seg", pairs)

    def to_core(value):
        return lax.ppermute(value, "seg", [(i, i ^ 1) for i in range(nseg)])

    def to_seq(value, dz):
        return lax.ppermute(value, "seq", [(i, (i + dz) % nseq) for i in range(nseq)])

    def kernel(body, name, limit, cost, outs, scratch, *operands):
        smem = pl.BlockSpec(memory_space=pltpu.SMEM)
        vmem = pl.BlockSpec(memory_space=pltpu.VMEM)
        return pl.pallas_call(
            body,
            in_specs=[smem if o.ndim == 1 else vmem for o in operands],
            out_specs=[vmem] * len(outs),
            out_shape=[jax.ShapeDtypeStruct(*o) for o in outs],
            scratch_shapes=[pltpu.VMEM(*o) for o in scratch],
            compiler_params=pltpu.CompilerParams(vmem_limit_bytes=limit * MIB),
            cost_estimate=pl.CostEstimate(flops=0, bytes_accessed=cost, transcendentals=0),
            name=name,
        )(*operands)

    segs = jnp.arange(nseg, dtype=jnp.int32)
    slot_of = ((chip - segs // CORES) % chips) * CORES + (core + segs) % CORES
    back = (place - jnp.arange(nseq, dtype=jnp.int32)) % nseq
    dest = ((chip + segs // CORES) % chips) * CORES + (core + segs) % CORES
    table = jnp.concatenate([slot_of, back, jnp.stack([me * hpd, me]), dest]).astype(jnp.int32)
    dims = (nseg, nseq, hpd, feats, hid, tokens, chunk)

    wide = max(own, 128)
    mine = pl.pallas_call(
        functools.partial(columns_kernel, dims),
        grid_spec=pltpu.PrefetchScalarGridSpec(
            num_scalar_prefetch=1,
            grid=(3,),
            in_specs=[
                pl.BlockSpec(
                    (chunk, wide),
                    lambda part, table: (0, (part * nseg + table[nseg + nseq + 1]) * own // wide),
                )
            ],
            out_specs=[pl.BlockSpec((feats, chunk), lambda part, table: (part, 0))] * hpd,
            scratch_shapes=[pltpu.VMEM((wide, chunk), BF)],
        ),
        out_shape=[jax.ShapeDtypeStruct((3 * feats, chunk), BF)] * hpd,
        compiler_params=pltpu.CompilerParams(vmem_limit_bytes=8 * MIB),
        cost_estimate=pl.CostEstimate(flops=0, bytes_accessed=0, transcendentals=0),
        name="columns",
    )(table, w_proj)
    mine, after = barrier((mine, table))
    keep, send = kernel(
        functools.partial(packs_kernel, dims),
        "packs",
        16,
        0,
        [((hpd, chips, 3 * feats, tokens), BF)] * CORES,
        [((heads * feats, tokens), BF)],
        after,
        out_cot[0],
        inner_start[0, 0],
    )
    far = [to_chip(rows, dx) for dx in range(1, chips)]
    near = to_core(rows)
    got = to_core(send)
    wt = [[block] for block in mine]
    wt[0] += [to_seq(mine[0], dz) for dz in range(1, nseq - 1)]
    near, got, keep, mine = barrier((near, got, keep, mine))
    wt[0] += [to_seq(mine[0], nseq - 1)]

    def pack_hops(head):
        return [
            to_chip(jnp.stack([keep[head, dx], got[head, dx]]), dx) for dx in range(1, chips)
        ]

    hops = [pack_hops(0)]
    wt[0], far, hops, mine, keep, got = barrier((wt[0], far, hops, mine, keep, got))
    li = [rows, near]
    for value in far:
        li += [value, to_core(value)]
    for head in range(1, hpd):
        wt[head] += [to_seq(mine[head], dz) for dz in range(1, nseq)]
        hops.append(pack_hops(head))

    def inner(head):
        outs = kernel(
            functools.partial(inner_kernel, dims, head),
            "inner",
            36,
            40 * MIB,
            [((3 * feats, chunk), BF if dz else F32) for dz in range(nseq)]
            + [((nseg, 3, feats, tokens), BF)]
            + [((chips, 2, feats, hid), BF)] * CORES,
            [
                ((nseg, 3, feats, tokens), BF),
                ((nseg, 2, feats, hid), BF),
                ((nseg, feats, tokens), BF),
                ((nseg, hid, tokens), BF),
                ((nseg, feats, tokens), BF),
                ((nseg, hid, tokens), F32),
                ((nseg, hid, tokens), F32),
                ((nseg, hid, tokens), BF),
                ((nseg, 2, feats, hid), F32),
            ],
            table,
            rates,
            *li,
            *wt[head],
            keep,
            got,
            *hops[head],
        )
        return outs[:nseq], outs[nseq], outs[nseq + 1], outs[nseq + 2]

    def to_rows(gp):
        return [gp[0]] + [to_seq(gp[dz], dz) for dz in range(1, nseq)]

    def summed(head, pieces):
        return kernel(sum_kernel, "sum", 12, 0, [((chunk // 2, 6 * feats), BF)], [], *pieces)[0]

    def to_owner(stay, leave):
        return [to_chip(jnp.stack([stay[dx], leave[dx]]), -dx) for dx in range(1, chips)]

    grads, projs, inners = [], [], []
    for head in range(hpd):
        gp, gq, stay, leave = inner(head)
        grads.append(gq)
        if head < hpd - 1:
            gp, leave, wt[head + 1], hops[head + 1] = barrier(
                (gp, leave, wt[head + 1], hops[head + 1])
            )
            pieces = to_rows(gp)
            leave = to_core(leave)
            backs = to_owner(stay, leave)
        if head > 0:
            gp, grads, stay, leave, pieces, backs = barrier(
                (gp, grads, stay, leave, pieces, backs)
            )
            total = summed(head - 1, pieces)
            projs.append([total] + [to_chip(total, dx) for dx in range(1, chips)])
            inners += [inners_stay, inners_leave, *backs]
        inners_stay, inners_leave = stay, leave

    def partial_input(name, limit, slots, grads):
        return kernel(
            functools.partial(input_kernel, dims, slots),
            name,
            limit,
            10 * MIB,
            [((len(slots) // CORES, tokens, width), BF)] * CORES,
            [],
            table,
            *grads,
            *[block for blocks in wt for block in blocks],
        )

    out, cross = partial_input("far", 20, range(nseg)[CORES:], grads)
    cross, leave = to_core(cross), to_core(leave)
    cross, leave, grads, projs, gp = barrier((cross, leave, grads, projs, gp))
    out = (out.astype(F32) + cross.astype(F32)).astype(BF)
    arrived = [to_chip(out[dx - 1], -dx) for dx in range(1, chips)]
    pieces = to_rows(gp)
    home, aside = partial_input("home", 20, range(CORES), grads)
    aside = to_core(aside)
    backs = to_owner(stay, leave)

    total = summed(hpd - 1, pieces)
    projs.append([total] + [to_chip(total, dx) for dx in range(1, chips)])
    projs, arrived, aside, backs = barrier((projs, arrived, aside, backs))
    projs = [value for far in projs for value in [*far, to_core(jnp.stack(far))]]
    grad_input = home[0].astype(F32) + aside[0].astype(F32)
    for value in arrived:
        grad_input += value.astype(F32)
    (grad_inner,) = kernel(
        functools.partial(weights_kernel, dims),
        "weights",
        8,
        10 * MIB,
        [((2, heads, feats, hid), F32)],
        [],
        table,
        *inners,
        stay,
        leave,
        *backs,
    )
    (grad_proj,) = kernel(
        functools.partial(join_kernel, dims),
        "join",
        16,
        0,
        [((chunk, 3 * heads * feats), F32)],
        [],
        table,
        *projs,
    )
    return (grad_input.astype(BF)[None], grad_proj, grad_inner[None, None])


def solution(mesh):
    placed = (
        P(("groups", "seq"), "seg", None),
        P(("groups", "seq"), "seg", None),
        P("seq", None),
        P(("groups", "seq"), "seg", None, None, None, None),
        P(),
    )
    return jax.shard_map(
        per_device,
        mesh=mesh,
        in_specs=placed,
        out_specs=(
            P(("groups", "seq"), "seg", None),
            P(("groups", "seq"), None),
            P(("groups", "seq"), "seg", None, None, None, None),
        ),
        check_vma=False,
    )
```

```python
import functools

import jax
import jax.numpy as jnp
from jax import lax
from jax.experimental import pallas as pl
from jax.experimental.pallas import tpu as pltpu
from jax.sharding import PartitionSpec as P

MB = 256
BF = jnp.bfloat16
F32 = jnp.float32
CORES = 2
GELU_A = 0.7978845608028654
GELU_B = 0.044715
MIB = 1024 * 1024


def dot(a, b, ca, cb):
    return lax.dot_general(a, b, (((ca,), (cb,)), ((), ())), preferred_element_type=F32)


def gelu_parts(u):
    square = u * u
    tanh = jnp.tanh(u * (GELU_A + (GELU_A * GELU_B) * square))
    half = 0.5 * (1.0 + tanh)
    sech = 1.0 - tanh * tanh
    slope = GELU_A + (3.0 * GELU_A * GELU_B) * square
    return square, tanh, half, sech, slope


def prep_kernel(dims, table, rows, w, cots, start, mine, pack, *refs):
    nseg, nseq, hpd, feats, hid, tokens, chunk = dims
    ships, refs = refs[: nseg // CORES], refs[nseg // CORES :]
    cut, held, weights, turned, sem = refs
    own = hpd * feats
    wide = cut.shape[2]
    per = rows.shape[1] // hid
    deep = pack.shape[0]
    me = table[nseg + nseq + 1]
    base = me * own // wide * wide
    copies = []
    for part in range(3):
        at = pl.multiple_of(part * nseg * own + base, wide)
        copies.append(pltpu.make_async_copy(w.at[:, pl.ds(at, wide)], cut.at[part], sem.at[part]))
    copies.append(pltpu.make_async_copy(cots, held, sem.at[3]))
    copies.append(pltpu.make_async_copy(start, weights, sem.at[4]))
    for i, ship in enumerate(ships):
        copies.append(pltpu.make_async_copy(rows, ship.at[pl.ds(0, tokens)], sem.at[5 + i]))
    for copy in copies:
        copy.start()
    for part in range(3):
        copies[part].wait()
        block = cut[part].T
        even = block[:own]
        for i in range(1, wide // own):
            even = jnp.where(me * own % wide == i * own, block[i * own : (i + 1) * own], even)
        mine[part * own : (part + 1) * own] = even
    copies[3].wait()
    turned[...] = held[...].T
    copies[4].wait()
    for slot in range(nseg):
        dest = table[nseg + nseq + 2 + slot]
        dx, dc = slot // CORES, slot % CORES
        target, low = (pack, 0) if slot == 0 else (ships[dx], tokens + (deep * dc if dx else 0))
        for i in range(3 * hpd):
            kind, head = i // hpd, i % hpd
            if kind < 2:
                value = weights[kind, dest * hpd + head].astype(BF)
            else:
                value = turned[pl.ds(pl.multiple_of((dest * hpd + head) * feats, feats), feats)]
            top, left = low + i // per * feats, i % per * hid
            target[top : top + feats, left : left + hid] = value
    for copy in copies[5:]:
        copy.wait()


def inner_kernel(dims, head, table, rates, *refs):
    nseg, nseq, hpd, feats, hid, tokens, chunk = dims
    chips = nseg // CORES
    li, refs = refs[:nseg], refs[nseg:]
    wt, refs = refs[:nseq], refs[nseq:]
    pack, refs = refs[0], refs[1:]
    gp, refs = refs[:nseq], refs[nseq:]
    gq, sent, kept, qkv, wts, cts, ht, rt, g1, g2p, gu, gab = refs
    rows = 3 * feats
    own = hpd * feats
    first = head * feats

    per = li[0].shape[1] // hid
    deep = pack.shape[0]

    for slot in range(nseg):
        dx, dc = slot // CORES, slot % CORES
        source, low = (pack, 0) if slot == 0 else (li[slot], tokens + (deep * dc if dx else 0))
        pieces = []
        for i in range(head, 3 * hpd, hpd):
            top, left = low + i // per * feats, i % per * hid
            pieces.append(source[top : top + feats, left : left + hid])
        total = jnp.zeros((rows, tokens), F32)
        for back in range(nseq):
            at = pl.multiple_of(table[nseg + back] * chunk, chunk)
            left = jnp.concatenate(
                [wt[back][p * own + first : p * own + first + feats] for p in range(3)]
            )
            total += dot(left, li[slot][:tokens, pl.ds(at, chunk)], 1, 1)
        qkv[slot] = total.astype(BF).reshape(3, feats, tokens)
        wts[slot, 0], wts[slot, 1], cts[slot] = pieces
    rate = rates[table[nseg + nseq] + head] * (1.0 / MB)

    def local(slot):
        a_b, b_b = wts[slot, 0], wts[slot, 1]
        q_b, k_b, v_b = qkv[slot, 0], qkv[slot, 1], qkv[slot, 2]
        c_b = cts[slot]
        u = dot(a_b, k_b, 0, 0)
        square, tanh, half, sech, slope = gelu_parts(u)
        h_b = (u * half).astype(BF)
        slope1 = half + 0.5 * u * sech * slope
        second = sech * (GELU_A + (6.0 * GELU_A * GELU_B) * square - u * tanh * slope * slope)
        ht[slot] = h_b
        g1[slot] = slope1
        resid = k_b.astype(F32) - v_b.astype(F32) + dot(b_b, h_b, 1, 0)
        r_b = resid.astype(BF)
        rt[slot] = r_b
        p = dot(b_b, r_b, 0, 0)
        g2p[slot] = second * p
        gu_b = (slope1 * p).astype(BF)
        gu[slot] = gu_b
        new_a = (a_b.astype(F32) - rate * dot(k_b, gu_b, 1, 1)).astype(BF)
        new_b = (b_b.astype(F32) - rate * dot(r_b, h_b, 1, 1)).astype(BF)
        uq = dot(new_a, q_b, 0, 0)
        square, tanh, half, sech, slope = gelu_parts(uq)
        hq_b = (uq * half).astype(BF)
        guq_b = ((half + 0.5 * uq * sech * slope) * dot(new_b, c_b, 0, 0)).astype(BF)
        gab[slot, 0] = dot(q_b, guq_b, 1, 1)
        gab[slot, 1] = dot(c_b, hq_b, 1, 1)
        gq[slot, 0] = (c_b.astype(F32) + dot(new_a, guq_b, 1, 0)).astype(BF)

    for slot in range(nseg):
        local(slot)

    def step(turn, carry):
        slot = table[nseg - 1 - turn]
        t_a = carry[0] + gab[slot, 0]
        t_b = carry[1] + gab[slot, 1]
        a_b, b_b = wts[slot, 0], wts[slot, 1]
        k_b = qkv[slot, 1]
        h_b, r_b, gu_b = ht[slot], rt[slot], gu[slot]
        ta_b, tb_b = t_a.astype(BF), t_b.astype(BF)
        du = dot(ta_b, k_b, 0, 0)
        dh_b = (g1[slot] * du).astype(BF)
        dr = dot(b_b, dh_b, 1, 0) + dot(tb_b, h_b, 1, 0)
        dr_b = dr.astype(BF)
        dp = dot(b_b, dr_b, 0, 0) + dot(tb_b, r_b, 0, 0)
        dgu_b = (g2p[slot] * du + g1[slot] * dp).astype(BF)
        c_a = t_a - rate * dot(k_b, dgu_b, 1, 1)
        c_b = t_b - rate * (dot(dr_b, h_b, 1, 1) + dot(r_b, dh_b, 1, 1))
        left = jnp.concatenate([a_b, ta_b], 1)
        gk = dr + dot(left, jnp.concatenate([dgu_b, gu_b], 0), 1, 0)
        gq[slot, 1] = (-rate * gk).astype(BF)
        gq[slot, 2] = (rate * dr).astype(BF)
        wts[slot, 0] = c_a.astype(BF)
        wts[slot, 1] = c_b.astype(BF)
        return (c_a, c_b)

    zero = jnp.zeros((feats, hid), F32)
    carry = (zero, zero)
    for turn in range(nseg):
        carry = step(turn, carry)

    for slot in range(nseg):
        dx, dc = slot // CORES, slot % CORES
        if dx == 0:
            kept[dc] = wts[slot]
        else:
            sent[dx - 1, dc * rows : (dc + 1) * rows] = gq[slot].reshape(rows, tokens)
            at = CORES * rows + dc * 2 * feats
            sent[dx - 1, at : at + 2 * feats] = wts[slot].reshape(2 * feats, hid)
    for dz in range(nseq):
        at = pl.multiple_of(table[nseg + (nseq - dz) % nseq] * chunk, chunk)
        total = jnp.zeros((rows, chunk), F32)
        for slot in range(nseg):
            part = li[slot][:tokens, pl.ds(at, chunk)]
            total += dot(gq[slot].reshape(rows, tokens), part, 1, 0)
        gp[dz][...] = total.astype(gp[dz].dtype)


def input_kernel(dims, table, *refs):
    nseg, nseq, hpd, feats, hid, tokens, chunk = dims
    chips = nseg // CORES
    rows = 3 * feats
    gq, refs = refs[:hpd], refs[hpd:]
    kept, refs = refs[:hpd], refs[hpd:]
    sent, refs = refs[: hpd * (chips - 1)], refs[hpd * (chips - 1) :]
    wt, refs = refs[: chips * nseq], refs[chips * nseq :]
    home, aside, leave = refs
    for dc in range(CORES):
        left = [gq[h][dc, p] for p in range(3) for h in range(hpd)]
        for dx in range(chips - 1):
            for p in range(3):
                at = dc * rows + p * feats
                left += [sent[h * (chips - 1) + dx][at : at + feats] for h in range(hpd)]
        left = jnp.concatenate(left)
        for back in range(nseq):
            at = pl.multiple_of(table[nseg + back] * chunk, chunk)
            right = jnp.concatenate([wt[dx * nseq + back][...] for dx in range(chips)])
            value = dot(left, right, 0, 0)
            out = (home, aside)[dc]
            out[:, pl.ds(at, chunk)] = value.astype(out.dtype)
    at = CORES * rows + 2 * feats
    for head in range(hpd):
        leave[head * chips] = kept[head][1].reshape(2 * feats, hid)
        for dx in range(1, chips):
            leave[head * chips + dx] = sent[head * (chips - 1) + dx - 1][at : at + 2 * feats]


def sum_kernel(*refs):
    total = refs[0][...]
    for ref in refs[1:-1]:
        total += ref[...].astype(F32)
    total = total.T.astype(BF)
    half = total.shape[0] // 2
    refs[-1][...] = jnp.concatenate([total[:half], total[half:]], 1)


def join_kernel(dims, table, *refs):
    nseg, nseq, hpd, feats, hid, tokens, chunk = dims
    chips = nseg // CORES
    far, near, out = refs[: hpd * chips], refs[hpd * chips], refs[hpd * chips + 1]
    wide = CORES * hpd * feats
    half = chunk // 2
    me = table[nseg + nseq + 1]
    chip = me // CORES
    even = me % CORES == 0
    for dx in range(chips):
        source = (chip - dx + chips) % chips
        for side in range(2):
            cut = slice(side * 3 * feats, (side + 1) * 3 * feats)
            mine = [far[h * chips + dx][:, cut].astype(F32) for h in range(hpd)]
            other = [near[h * chips + dx, :, cut].astype(F32) for h in range(hpd)]
            for part in range(3):
                cut = slice(part * feats, (part + 1) * feats)
                a = jnp.concatenate([value[:, cut] for value in mine + other], 1)
                b = jnp.concatenate([value[:, cut] for value in other + mine], 1)
                at = pl.multiple_of((part * nseg * hpd * feats) + source * wide, wide)
                rows = pl.ds(side * half, half)
                out[rows, pl.ds(at, wide)] = jnp.where(even, a, b)


def weights_kernel(dims, table, *refs):
    nseg, nseq, hpd, feats, hid, tokens, chunk = dims
    chips = nseg // CORES
    kept, refs = refs[:hpd], refs[hpd:]
    sent, refs = refs[: hpd * (chips - 1)], refs[hpd * (chips - 1) :]
    got, out = refs
    at = CORES * 3 * feats
    for head in range(hpd):
        for slot in range(nseg):
            dx, dc = slot // CORES, slot % CORES
            if dc == 1:
                piece = got[head * chips + dx]
            elif dx == 0:
                piece = kept[head][0].reshape(2 * feats, hid)
            else:
                piece = sent[head * (chips - 1) + dx - 1][at : at + 2 * feats]
            index = table[nseg + nseq + 2 + slot] * hpd + head
            out[0, index] = piece[:feats].astype(F32)
            out[1, index] = piece[feats:].astype(F32)


def per_device(layer_input, out_cot, w_proj, inner_start, rates):
    rows = layer_input[0]
    tokens, width = rows.shape
    heads = rates.shape[0]
    feats, hid = inner_start.shape[4:]
    nseg, nseq = lax.axis_size("seg"), lax.axis_size("seq")
    chips = nseg // CORES
    hpd = heads // nseg
    own = hpd * feats
    chunk = width // nseq
    me, place = lax.axis_index("seg"), lax.axis_index("seq")
    chip, core = me // CORES, me % CORES
    barrier = lax.optimization_barrier

    def to_chip(value, dx):
        pairs = [(i, (i + dx * CORES) % nseg) for i in range(nseg)]
        return lax.ppermute(value, "seg", pairs)

    def to_core(value):
        return lax.ppermute(value, "seg", [(i, i ^ 1) for i in range(nseg)])

    def to_seq(value, dz):
        return lax.ppermute(value, "seq", [(i, (i + dz) % nseq) for i in range(nseq)])

    def kernel(body, name, limit, cost, outs, scratch, *operands):
        smem = pl.BlockSpec(memory_space=pltpu.SMEM)
        vmem = pl.BlockSpec(memory_space=pltpu.VMEM)
        return pl.pallas_call(
            body,
            in_specs=[smem if o.ndim == 1 else vmem for o in operands],
            out_specs=[vmem] * len(outs),
            out_shape=[jax.ShapeDtypeStruct(*o) for o in outs],
            scratch_shapes=[pltpu.VMEM(*o) for o in scratch],
            compiler_params=pltpu.CompilerParams(vmem_limit_bytes=limit * MIB),
            cost_estimate=pl.CostEstimate(flops=0, bytes_accessed=cost, transcendentals=0),
            name=name,
        )(*operands)

    def summed(pieces):
        return kernel(sum_kernel, "sum", 12, 0, [((chunk // 2, 6 * feats), BF)], [], *pieces)[0]

    crossed = chips == 2 and lax.axis_size("groups") == 2
    shift = lax.axis_index("groups") if crossed else 0

    segs = jnp.arange(nseg, dtype=jnp.int32)
    slot_of = ((chip - segs // CORES) % chips) * CORES + (core + segs) % CORES
    back = (place - jnp.arange(nseq, dtype=jnp.int32)) % nseq
    dest = ((chip + shift + segs // CORES) % chips) * CORES + (core + segs) % CORES
    table = jnp.concatenate([slot_of, back, jnp.stack([dest[0] * hpd, dest[0]]), dest])
    table = table.astype(jnp.int32)
    dims = (nseg, nseq, hpd, feats, hid, tokens, chunk)

    wide = max(own, 128)
    deep = -(-3 * hpd * hid // width) * feats
    hbm = pl.BlockSpec(memory_space=pltpu.HBM)
    vmem = pl.BlockSpec(memory_space=pltpu.VMEM)
    outs = [((3 * own, chunk), BF), ((deep, width), BF), ((tokens + deep, width), BF)]
    outs += [((tokens + CORES * deep, width), BF)] * (chips - 1)
    operands = (rows, w_proj, out_cot[0], inner_start[0, 0])
    mine, pack, *ships = pl.pallas_call(
        functools.partial(prep_kernel, dims),
        in_specs=[pl.BlockSpec(memory_space=pltpu.SMEM)] + [hbm] * 4,
        out_specs=[vmem] * len(outs),
        out_shape=[jax.ShapeDtypeStruct(*o) for o in outs],
        scratch_shapes=[
            pltpu.VMEM((3, chunk, wide), BF),
            pltpu.VMEM((tokens, heads * feats), BF),
            pltpu.VMEM((2, heads, feats, hid), F32),
            pltpu.VMEM((heads * feats, tokens), BF),
            pltpu.SemaphoreType.DMA((5 + chips,)),
        ],
        compiler_params=pltpu.CompilerParams(vmem_limit_bytes=16 * MIB),
        cost_estimate=pl.CostEstimate(flops=0, bytes_accessed=0, transcendentals=0),
        name="prep",
    )(table, *[pltpu.with_memory_space_constraint(o, pltpu.HBM) for o in operands])
    near = to_core(ships[0])
    far = [to_chip(ships[dx], dx) for dx in range(1, chips)]
    wt = [mine] + [to_seq(mine, dz) for dz in range(1, nseq)]
    far, near, wt = barrier((far, near, wt))
    li = [rows, near]
    for value in far:
        li += [value, to_core(value)]

    def to_others(value):
        if crossed:
            return [lax.ppermute(value, "groups", [(0, 1), (1, 0)])]
        return [to_chip(value, -dx) for dx in range(1, chips)]

    def inner(head):
        return kernel(
            functools.partial(inner_kernel, dims, head),
            "inner",
            36,
            40 * MIB,
            [((3 * feats, chunk), BF if dz else F32) for dz in range(nseq)]
            + [((nseg, 3, feats, tokens), BF)]
            + [((chips - 1, 10 * feats, tokens), BF)]
            + [((CORES, 2, feats, hid), BF)],
            [
                ((nseg, 3, feats, tokens), BF),
                ((nseg, 2, feats, hid), BF),
                ((nseg, feats, tokens), BF),
                ((nseg, hid, tokens), BF),
                ((nseg, feats, tokens), BF),
                ((nseg, hid, tokens), F32),
                ((nseg, hid, tokens), F32),
                ((nseg, hid, tokens), BF),
                ((nseg, 2, feats, hid), F32),
            ],
            table,
            rates,
            *li,
            *wt,
            pack,
        )

    share = nseq // hpd
    grads, kept, sent, projs, away, pieces = [], [], [], [], [], None
    blocks = wt
    for head in range(hpd):
        away.append(to_others(jnp.stack(blocks[head * share : (head + 1) * share])))
        outs = inner(head)
        gp, gq, send, keep = outs[:nseq], outs[nseq], outs[nseq + 1], outs[nseq + 2]
        gp, send, away, blocks, pieces, sent = barrier((gp, send, away, blocks, pieces, sent))
        if pieces is not None:
            total = summed(pieces)
            projs += [total] + [to_chip(total, dx) for dx in range(1, chips)]
        pieces = [gp[0]] + [to_seq(gp[dz], dz) for dz in range(1, nseq)]
        sent += [to_chip(send[dx - 1], -dx) for dx in range(1, chips)]
        grads.append(gq)
        kept.append(keep)

    pieces, sent, projs = barrier((pieces, sent, projs))
    total = summed(pieces)
    projs += [total] + [to_chip(total, dx) for dx in range(1, chips)]

    others = [
        group[dx][i] for dx in range(chips - 1) for group in away for i in range(share)
    ]
    home, aside, leave = kernel(
        functools.partial(input_kernel, dims),
        "input",
        24,
        10 * MIB,
        [((tokens, width), F32), ((tokens, width), BF)]
        + [((hpd * chips, 2 * feats, hid), BF)],
        [],
        table,
        *grads,
        *kept,
        *sent,
        *wt,
        *others,
    )
    grad_input = home + to_core(aside).astype(F32)
    (grad_inner,) = kernel(
        functools.partial(weights_kernel, dims),
        "weights",
        8,
        10 * MIB,
        [((2, heads, feats, hid), F32)],
        [],
        table,
        *kept,
        *sent,
        to_core(leave),
    )
    (grad_proj,) = kernel(
        functools.partial(join_kernel, dims),
        "join",
        16,
        0,
        [((chunk, 3 * heads * feats), F32)],
        [],
        table,
        *projs,
        to_core(jnp.stack(projs)),
    )
    return (grad_input.astype(BF)[None], grad_proj, grad_inner[None, None])


def solution(mesh):
    placed = (
        P(("groups", "seq"), "seg", None),
        P(("groups", "seq"), "seg", None),
        P("seq", None),
        P(("groups", "seq"), "seg", None, None, None, None),
        P(),
    )
    return jax.shard_map(
        per_device,
        mesh=mesh,
        in_specs=placed,
        out_specs=(
            P(("groups", "seq"), "seg", None),
            P(("groups", "seq"), None),
            P(("groups", "seq"), "seg", None, None, None, None),
        ),
        check_vma=False,
    )
```

```python
import functools

import jax
import jax.numpy as jnp
from jax import lax
from jax.experimental import pallas as pl
from jax.experimental.pallas import tpu as pltpu
from jax.sharding import PartitionSpec as P

MB = 256
BF = jnp.bfloat16
F32 = jnp.float32
CORES = 2
GELU_A = 0.7978845608028654
GELU_B = 0.044715
MIB = 1024 * 1024
TILE = 16


def dot(a, b, ca, cb):
    return lax.dot_general(a, b, (((ca,), (cb,)), ((), ())), preferred_element_type=F32)


def gelu_parts(u):
    square = u * u
    tanh = jnp.tanh(u * (GELU_A + (GELU_A * GELU_B) * square))
    half = 0.5 * (1.0 + tanh)
    sech = 1.0 - tanh * tanh
    slope = GELU_A + (3.0 * GELU_A * GELU_B) * square
    return square, tanh, half, sech, slope


def packed(row, deep, hid):
    return row % deep, row // deep * hid


def prep_kernel(dims, table, rows, w, cots, start, mine, pack, *refs):
    nseg, nseq, hpd, feats, hid, tokens, chunk = dims
    ships, refs = refs[: nseg // CORES], refs[nseg // CORES :]
    cut, held, weights, turned, sem = refs
    own = hpd * feats
    wide = cut.shape[2]
    deep = pack.shape[0]
    me = table[nseg + nseq + 1]
    base = me * own // wide * wide
    copies = []
    for part in range(3):
        at = pl.multiple_of(part * nseg * own + base, wide)
        copies.append(pltpu.make_async_copy(w.at[:, pl.ds(at, wide)], cut.at[part], sem.at[part]))
    copies.append(pltpu.make_async_copy(cots, held, sem.at[3]))
    copies.append(pltpu.make_async_copy(start, weights, sem.at[4]))
    for i, ship in enumerate(ships):
        copies.append(pltpu.make_async_copy(rows, ship.at[pl.ds(0, tokens)], sem.at[5 + i]))
    for copy in copies:
        copy.start()
    for part in range(3):
        copies[part].wait()
        block = cut[part].T
        even = block[:own]
        for i in range(1, wide // own):
            even = jnp.where(me * own % wide == i * own, block[i * own : (i + 1) * own], even)
        mine[part * own : (part + 1) * own] = even
    copies[3].wait()
    turned[...] = held[...].T
    copies[4].wait()
    for slot in range(nseg):
        dest = table[nseg + nseq + 2 + slot]
        dx, dc = slot // CORES, slot % CORES
        target, low = (pack, 0) if slot == 0 else (ships[dx], tokens + (deep * dc if dx else 0))
        for i in range(3 * hpd):
            kind, head = i // hpd, i % hpd
            if kind < 2:
                value = weights[kind, dest * hpd + head].astype(BF)
            else:
                value = turned[pl.ds(pl.multiple_of((dest * hpd + head) * feats, feats), feats)]
            for j in range(0, feats, TILE):
                top, left = packed(i * feats + j, deep, hid)
                target[low + top : low + top + TILE, left : left + hid] = value[j : j + TILE]
    for copy in copies[5:]:
        copy.wait()


def inner_kernel(dims, head, table, rates, *refs):
    nseg, nseq, hpd, feats, hid, tokens, chunk = dims
    chips = nseg // CORES
    li, refs = refs[:nseg], refs[nseg:]
    wt, refs = refs[:nseq], refs[nseq:]
    pack, refs = refs[0], refs[1:]
    gp, refs = refs[:nseq], refs[nseq:]
    gq, sent, kept, qkv, wts, cts, ht, rt, g1, g2p, gu, gab = refs
    rows = 3 * feats
    own = hpd * feats
    first = head * feats

    deep = pack.shape[0]

    for slot in range(nseg):
        dx, dc = slot // CORES, slot % CORES
        source, low = (pack, 0) if slot == 0 else (li[slot], tokens + (deep * dc if dx else 0))
        for i, piece in enumerate((wts.at[slot, 0], wts.at[slot, 1], cts.at[slot])):
            for j in range(0, feats, TILE):
                top, left = packed((i * hpd + head) * feats + j, deep, hid)
                value = source[low + top : low + top + TILE, left : left + hid]
                piece[j : j + TILE] = value
        total = jnp.zeros((rows, tokens), F32)
        for back in range(nseq):
            at = pl.multiple_of(table[nseg + back] * chunk, chunk)
            left = jnp.concatenate(
                [wt[back][p * own + first : p * own + first + feats] for p in range(3)]
            )
            total += dot(left, li[slot][:tokens, pl.ds(at, chunk)], 1, 1)
        qkv[slot] = total.astype(BF).reshape(3, feats, tokens)
    rate = rates[table[nseg + nseq] + head] * (1.0 / MB)

    def local(slot):
        a_b, b_b = wts[slot, 0], wts[slot, 1]
        q_b, k_b, v_b = qkv[slot, 0], qkv[slot, 1], qkv[slot, 2]
        c_b = cts[slot]
        u = dot(a_b, k_b, 0, 0)
        square, tanh, half, sech, slope = gelu_parts(u)
        h_b = (u * half).astype(BF)
        slope1 = half + 0.5 * u * sech * slope
        second = sech * (GELU_A + (6.0 * GELU_A * GELU_B) * square - u * tanh * slope * slope)
        ht[slot] = h_b
        g1[slot] = slope1
        resid = k_b.astype(F32) - v_b.astype(F32) + dot(b_b, h_b, 1, 0)
        r_b = resid.astype(BF)
        rt[slot] = r_b
        p = dot(b_b, r_b, 0, 0)
        g2p[slot] = second * p
        gu_b = (slope1 * p).astype(BF)
        gu[slot] = gu_b
        new_a = (a_b.astype(F32) - rate * dot(k_b, gu_b, 1, 1)).astype(BF)
        new_b = (b_b.astype(F32) - rate * dot(r_b, h_b, 1, 1)).astype(BF)
        uq = dot(new_a, q_b, 0, 0)
        square, tanh, half, sech, slope = gelu_parts(uq)
        hq_b = (uq * half).astype(BF)
        guq_b = ((half + 0.5 * uq * sech * slope) * dot(new_b, c_b, 0, 0)).astype(BF)
        gab[slot, 0] = dot(q_b, guq_b, 1, 1)
        gab[slot, 1] = dot(c_b, hq_b, 1, 1)
        gq[slot, 0] = (c_b.astype(F32) + dot(new_a, guq_b, 1, 0)).astype(BF)

    for slot in range(nseg):
        local(slot)

    def step(turn, carry):
        slot = table[nseg - 1 - turn]
        t_a = carry[0] + gab[slot, 0]
        t_b = carry[1] + gab[slot, 1]
        a_b, b_b = wts[slot, 0], wts[slot, 1]
        k_b = qkv[slot, 1]
        h_b, r_b, gu_b = ht[slot], rt[slot], gu[slot]
        ta_b, tb_b = t_a.astype(BF), t_b.astype(BF)
        du = dot(ta_b, k_b, 0, 0)
        dh_b = (g1[slot] * du).astype(BF)
        dr = dot(b_b, dh_b, 1, 0) + dot(tb_b, h_b, 1, 0)
        dr_b = dr.astype(BF)
        dp = dot(b_b, dr_b, 0, 0) + dot(tb_b, r_b, 0, 0)
        dgu_b = (g2p[slot] * du + g1[slot] * dp).astype(BF)
        c_a = t_a - rate * dot(k_b, dgu_b, 1, 1)
        c_b = t_b - rate * (dot(dr_b, h_b, 1, 1) + dot(r_b, dh_b, 1, 1))
        left = jnp.concatenate([a_b, ta_b], 1)
        gk = dr + dot(left, jnp.concatenate([dgu_b, gu_b], 0), 1, 0)
        gq[slot, 1] = (-rate * gk).astype(BF)
        gq[slot, 2] = (rate * dr).astype(BF)
        wts[slot, 0] = c_a.astype(BF)
        wts[slot, 1] = c_b.astype(BF)
        return (c_a, c_b)

    zero = jnp.zeros((feats, hid), F32)
    carry = (zero, zero)
    for turn in range(nseg):
        carry = step(turn, carry)

    for slot in range(nseg):
        dx, dc = slot // CORES, slot % CORES
        if dx == 0:
            kept[dc] = wts[slot]
        else:
            sent[dx - 1, dc * rows : (dc + 1) * rows] = gq[slot].reshape(rows, tokens)
            at = CORES * rows + dc * 2 * feats
            sent[dx - 1, at : at + 2 * feats] = wts[slot].reshape(2 * feats, hid)
    for dz in range(nseq):
        at = pl.multiple_of(table[nseg + (nseq - dz) % nseq] * chunk, chunk)
        total = jnp.zeros((rows, chunk), F32)
        for slot in range(nseg):
            part = li[slot][:tokens, pl.ds(at, chunk)]
            total += dot(gq[slot].reshape(rows, tokens), part, 1, 0)
        gp[dz][...] = total.astype(gp[dz].dtype)


def input_kernel(dims, table, *refs):
    nseg, nseq, hpd, feats, hid, tokens, chunk = dims
    chips = nseg // CORES
    rows = 3 * feats
    gq, refs = refs[:hpd], refs[hpd:]
    kept, refs = refs[:hpd], refs[hpd:]
    sent, refs = refs[: hpd * (chips - 1)], refs[hpd * (chips - 1) :]
    wt, refs = refs[: chips * nseq], refs[chips * nseq :]
    home, aside, leave = refs
    for dc in range(CORES):
        left = [gq[h][dc, p] for p in range(3) for h in range(hpd)]
        for dx in range(chips - 1):
            for p in range(3):
                at = dc * rows + p * feats
                left += [sent[h * (chips - 1) + dx][at : at + feats] for h in range(hpd)]
        left = jnp.concatenate(left)
        for back in range(nseq):
            at = pl.multiple_of(table[nseg + back] * chunk, chunk)
            right = jnp.concatenate([wt[dx * nseq + back][...] for dx in range(chips)])
            value = dot(left, right, 0, 0)
            out = (home, aside)[dc]
            out[:, pl.ds(at, chunk)] = value.astype(out.dtype)
    at = CORES * rows + 2 * feats
    for head in range(hpd):
        leave[head * chips] = kept[head][1].reshape(2 * feats, hid)
        for dx in range(1, chips):
            leave[head * chips + dx] = sent[head * (chips - 1) + dx - 1][at : at + 2 * feats]


def sum_kernel(*refs):
    total = refs[0][...]
    for ref in refs[1:-1]:
        total += ref[...].astype(F32)
    total = total.T.astype(BF)
    half = total.shape[0] // 2
    refs[-1][...] = jnp.concatenate([total[:half], total[half:]], 1)


def join_kernel(dims, table, *refs):
    nseg, nseq, hpd, feats, hid, tokens, chunk = dims
    chips = nseg // CORES
    far, near, out = refs[: hpd * chips], refs[hpd * chips], refs[hpd * chips + 1]
    wide = CORES * hpd * feats
    half = chunk // 2
    me = table[nseg + nseq + 1]
    chip = me // CORES
    even = me % CORES == 0
    for dx in range(chips):
        source = (chip - dx + chips) % chips
        for side in range(2):
            cut = slice(side * 3 * feats, (side + 1) * 3 * feats)
            mine = [far[h * chips + dx][:, cut].astype(F32) for h in range(hpd)]
            other = [near[h * chips + dx, :, cut].astype(F32) for h in range(hpd)]
            for part in range(3):
                cut = slice(part * feats, (part + 1) * feats)
                a = jnp.concatenate([value[:, cut] for value in mine + other], 1)
                b = jnp.concatenate([value[:, cut] for value in other + mine], 1)
                at = pl.multiple_of((part * nseg * hpd * feats) + source * wide, wide)
                rows = pl.ds(side * half, half)
                out[rows, pl.ds(at, wide)] = jnp.where(even, a, b)


def weights_kernel(dims, table, *refs):
    nseg, nseq, hpd, feats, hid, tokens, chunk = dims
    chips = nseg // CORES
    kept, refs = refs[:hpd], refs[hpd:]
    sent, refs = refs[: hpd * (chips - 1)], refs[hpd * (chips - 1) :]
    got, out = refs
    at = CORES * 3 * feats
    for head in range(hpd):
        for slot in range(nseg):
            dx, dc = slot // CORES, slot % CORES
            if dc == 1:
                piece = got[head * chips + dx]
            elif dx == 0:
                piece = kept[head][0].reshape(2 * feats, hid)
            else:
                piece = sent[head * (chips - 1) + dx - 1][at : at + 2 * feats]
            index = table[nseg + nseq + 2 + slot] * hpd + head
            out[0, index] = piece[:feats].astype(F32)
            out[1, index] = piece[feats:].astype(F32)


def per_device(layer_input, out_cot, w_proj, inner_start, rates):
    rows = layer_input[0]
    tokens, width = rows.shape
    heads = rates.shape[0]
    feats, hid = inner_start.shape[4:]
    nseg, nseq = lax.axis_size("seg"), lax.axis_size("seq")
    chips = nseg // CORES
    hpd = heads // nseg
    own = hpd * feats
    chunk = width // nseq
    me, place = lax.axis_index("seg"), lax.axis_index("seq")
    chip, core = me // CORES, me % CORES
    barrier = lax.optimization_barrier

    def to_chip(value, dx):
        pairs = [(i, (i + dx * CORES) % nseg) for i in range(nseg)]
        return lax.ppermute(value, "seg", pairs)

    def to_core(value):
        return lax.ppermute(value, "seg", [(i, i ^ 1) for i in range(nseg)])

    def to_seq(value, dz):
        return lax.ppermute(value, "seq", [(i, (i + dz) % nseq) for i in range(nseq)])

    def kernel(body, name, limit, cost, outs, scratch, *operands):
        smem = pl.BlockSpec(memory_space=pltpu.SMEM)
        vmem = pl.BlockSpec(memory_space=pltpu.VMEM)
        return pl.pallas_call(
            body,
            in_specs=[smem if o.ndim == 1 else vmem for o in operands],
            out_specs=[vmem] * len(outs),
            out_shape=[jax.ShapeDtypeStruct(*o) for o in outs],
            scratch_shapes=[pltpu.VMEM(*o) for o in scratch],
            compiler_params=pltpu.CompilerParams(vmem_limit_bytes=limit * MIB),
            cost_estimate=pl.CostEstimate(flops=0, bytes_accessed=cost, transcendentals=0),
            name=name,
        )(*operands)

    def summed(pieces):
        return kernel(sum_kernel, "sum", 12, 0, [((chunk // 2, 6 * feats), BF)], [], *pieces)[0]

    crossed = chips == 2 and lax.axis_size("groups") == 2
    shift = lax.axis_index("groups") if crossed else 0

    segs = jnp.arange(nseg, dtype=jnp.int32)
    slot_of = ((chip - segs // CORES) % chips) * CORES + (core + segs) % CORES
    back = (place - jnp.arange(nseq, dtype=jnp.int32)) % nseq
    dest = ((chip + shift + segs // CORES) % chips) * CORES + (core + segs) % CORES
    table = jnp.concatenate([slot_of, back, jnp.stack([dest[0] * hpd, dest[0]]), dest])
    table = table.astype(jnp.int32)
    dims = (nseg, nseq, hpd, feats, hid, tokens, chunk)

    wide = max(own, 128)
    deep = -(-3 * own * hid // (width * TILE)) * TILE
    hbm = pl.BlockSpec(memory_space=pltpu.HBM)
    vmem = pl.BlockSpec(memory_space=pltpu.VMEM)
    outs = [((3 * own, chunk), BF), ((deep, width), BF), ((tokens + deep, width), BF)]
    outs += [((tokens + CORES * deep, width), BF)] * (chips - 1)
    operands = (rows, w_proj, out_cot[0], inner_start[0, 0])
    mine, pack, *ships = pl.pallas_call(
        functools.partial(prep_kernel, dims),
        in_specs=[pl.BlockSpec(memory_space=pltpu.SMEM)] + [hbm] * 4,
        out_specs=[vmem] * len(outs),
        out_shape=[jax.ShapeDtypeStruct(*o) for o in outs],
        scratch_shapes=[
            pltpu.VMEM((3, chunk, wide), BF),
            pltpu.VMEM((tokens, heads * feats), BF),
            pltpu.VMEM((2, heads, feats, hid), F32),
            pltpu.VMEM((heads * feats, tokens), BF),
            pltpu.SemaphoreType.DMA((5 + chips,)),
        ],
        compiler_params=pltpu.CompilerParams(vmem_limit_bytes=16 * MIB),
        cost_estimate=pl.CostEstimate(flops=0, bytes_accessed=0, transcendentals=0),
        name="prep",
    )(table, *[pltpu.with_memory_space_constraint(o, pltpu.HBM) for o in operands])
    near = to_core(ships[0])
    far = [to_chip(ships[dx], dx) for dx in range(1, chips)]
    wt = [mine] + [to_seq(mine, dz) for dz in range(1, nseq)]
    far, near, wt = barrier((far, near, wt))
    li = [rows, near]
    for value in far:
        li += [value, to_core(value)]

    def to_others(value):
        if crossed:
            return [lax.ppermute(value, "groups", [(0, 1), (1, 0)])]
        return [to_chip(value, -dx) for dx in range(1, chips)]

    def inner(head):
        return kernel(
            functools.partial(inner_kernel, dims, head),
            "inner",
            36,
            0,
            [((3 * feats, chunk), BF if dz else F32) for dz in range(nseq)]
            + [((nseg, 3, feats, tokens), BF)]
            + [((chips - 1, 10 * feats, tokens), BF)]
            + [((CORES, 2, feats, hid), BF)],
            [
                ((nseg, 3, feats, tokens), BF),
                ((nseg, 2, feats, hid), BF),
                ((nseg, feats, tokens), BF),
                ((nseg, hid, tokens), BF),
                ((nseg, feats, tokens), BF),
                ((nseg, hid, tokens), F32),
                ((nseg, hid, tokens), F32),
                ((nseg, hid, tokens), BF),
                ((nseg, 2, feats, hid), F32),
            ],
            table,
            rates,
            *li,
            *wt,
            pack,
        )

    away = to_others(jnp.stack(wt))
    grads, kept, sent, projs, pieces = [], [], [], [], None
    for head in range(hpd):
        outs = inner(head)
        gp, gq, send, keep = outs[:nseq], outs[nseq], outs[nseq + 1], outs[nseq + 2]
        if head == hpd - 1:
            gp, send, away, pieces, sent = barrier((gp, send, away, pieces, sent))
        if pieces is not None:
            total = summed(pieces)
            projs += [total] + [to_chip(total, dx) for dx in range(1, chips)]
        pieces = [gp[0]] + [to_seq(gp[dz], dz) for dz in range(1, nseq)]
        sent += [to_chip(send[dx - 1], -dx) for dx in range(1, chips)]
        grads.append(gq)
        kept.append(keep)

    pieces, sent, projs = barrier((pieces, sent, projs))
    total = summed(pieces)
    projs += [total] + [to_chip(total, dx) for dx in range(1, chips)]

    others = [value[i] for value in away for i in range(nseq)]
    home, aside, leave = kernel(
        functools.partial(input_kernel, dims),
        "input",
        24,
        10 * MIB,
        [((tokens, width), F32), ((tokens, width), BF)]
        + [((hpd * chips, 2 * feats, hid), BF)],
        [],
        table,
        *grads,
        *kept,
        *sent,
        *wt,
        *others,
    )
    aside, leave = to_core(aside), to_core(leave)
    projs, aside, leave = barrier((projs, aside, leave))
    grad_input = home + aside.astype(F32)
    (grad_inner,) = kernel(
        functools.partial(weights_kernel, dims),
        "weights",
        8,
        10 * MIB,
        [((2, heads, feats, hid), F32)],
        [],
        table,
        *kept,
        *sent,
        leave,
    )
    (grad_proj,) = kernel(
        functools.partial(join_kernel, dims),
        "join",
        16,
        0,
        [((chunk, 3 * heads * feats), F32)],
        [],
        table,
        *projs,
        to_core(jnp.stack(projs)),
    )
    return (grad_input.astype(BF)[None], grad_proj, grad_inner[None, None])


def solution(mesh):
    placed = (
        P(("groups", "seq"), "seg", None),
        P(("groups", "seq"), "seg", None),
        P("seq", None),
        P(("groups", "seq"), "seg", None, None, None, None),
        P(),
    )
    return jax.shard_map(
        per_device,
        mesh=mesh,
        in_specs=placed,
        out_specs=(
            P(("groups", "seq"), "seg", None),
            P(("groups", "seq"), None),
            P(("groups", "seq"), "seg", None, None, None, None),
        ),
        check_vma=False,
    )
```

```python
import functools

import jax
import jax.numpy as jnp
from jax import lax
from jax.experimental import pallas as pl
from jax.experimental.pallas import tpu as pltpu
from jax.sharding import PartitionSpec as P

MB = 256
BF = jnp.bfloat16
F32 = jnp.float32
CORES = 2
GELU_A = 0.7978845608028654
GELU_B = 0.044715
MIB = 1024 * 1024
TILE = 16


def dot(a, b, ca, cb):
    return lax.dot_general(a, b, (((ca,), (cb,)), ((), ())), preferred_element_type=F32)


def gelu_parts(u):
    square = u * u
    tanh = jnp.tanh(u * (GELU_A + (GELU_A * GELU_B) * square))
    half = 0.5 * (1.0 + tanh)
    sech = 1.0 - tanh * tanh
    slope = GELU_A + (3.0 * GELU_A * GELU_B) * square
    return square, tanh, half, sech, slope


def packed(row, deep, hid):
    return row % deep, row // deep * hid


def prep_kernel(dims, table, rows, w, cots, start, mine, pack, *refs):
    nseg, nseq, hpd, feats, hid, tokens, chunk = dims
    ships, refs = refs[: nseg // CORES], refs[nseg // CORES :]
    cut, held, weights, turned, sem = refs
    own = hpd * feats
    wide = cut.shape[2]
    deep = pack.shape[0]
    me = table[nseg + nseq + 1]
    base = me * own // wide * wide
    copies = []
    for part in range(3):
        at = pl.multiple_of(part * nseg * own + base, wide)
        copies.append(pltpu.make_async_copy(w.at[:, pl.ds(at, wide)], cut.at[part], sem.at[part]))
    copies.append(pltpu.make_async_copy(cots, held, sem.at[3]))
    copies.append(pltpu.make_async_copy(start, weights, sem.at[4]))
    for i, ship in enumerate(ships):
        copies.append(pltpu.make_async_copy(rows, ship.at[pl.ds(0, tokens)], sem.at[5 + i]))
    for copy in copies:
        copy.start()
    for part in range(3):
        copies[part].wait()
        block = cut[part].T
        even = block[:own]
        for i in range(1, wide // own):
            even = jnp.where(me * own % wide == i * own, block[i * own : (i + 1) * own], even)
        mine[part * own : (part + 1) * own] = even
    copies[3].wait()
    turned[...] = held[...].T
    copies[4].wait()
    for slot in range(nseg):
        dest = table[nseg + nseq + 2 + slot]
        dx, dc = slot // CORES, slot % CORES
        target, low = (pack, 0) if slot == 0 else (ships[dx], tokens + (deep * dc if dx else 0))
        for i in range(3 * hpd):
            kind, head = i // hpd, i % hpd
            if kind < 2:
                value = weights[kind, dest * hpd + head].astype(BF)
            else:
                value = turned[pl.ds(pl.multiple_of((dest * hpd + head) * feats, feats), feats)]
            for j in range(0, feats, TILE):
                top, left = packed(i * feats + j, deep, hid)
                target[low + top : low + top + TILE, left : left + hid] = value[j : j + TILE]
    for copy in copies[5:]:
        copy.wait()


def inner_kernel(dims, head, table, rates, *refs):
    nseg, nseq, hpd, feats, hid, tokens, chunk = dims
    chips = nseg // CORES
    li, refs = refs[:nseg], refs[nseg:]
    wt, refs = refs[:nseq], refs[nseq:]
    pack, refs = refs[0], refs[1:]
    gp, refs = refs[:nseq], refs[nseq:]
    gq, sent, kept, qkv, wts, cts, ht, rt, g1, g2p, gu, gab = refs
    rows = 3 * feats
    own = hpd * feats
    first = head * feats

    deep = pack.shape[0]

    for slot in range(nseg):
        dx, dc = slot // CORES, slot % CORES
        source, low = (pack, 0) if slot == 0 else (li[slot], tokens + (deep * dc if dx else 0))
        for i, piece in enumerate((wts.at[slot, 0], wts.at[slot, 1], cts.at[slot])):
            for j in range(0, feats, TILE):
                top, left = packed((i * hpd + head) * feats + j, deep, hid)
                value = source[low + top : low + top + TILE, left : left + hid]
                piece[j : j + TILE] = value
        total = jnp.zeros((rows, tokens), F32)
        for back in range(nseq):
            at = pl.multiple_of(table[nseg + back] * chunk, chunk)
            left = jnp.concatenate(
                [wt[back][p * own + first : p * own + first + feats] for p in range(3)]
            )
            total += dot(left, li[slot][:tokens, pl.ds(at, chunk)], 1, 1)
        qkv[slot] = total.astype(BF).reshape(3, feats, tokens)
    rate = rates[table[nseg + nseq] + head] * (1.0 / MB)

    def local(slot):
        a_b, b_b = wts[slot, 0], wts[slot, 1]
        q_b, k_b, v_b = qkv[slot, 0], qkv[slot, 1], qkv[slot, 2]
        c_b = cts[slot]
        u = dot(a_b, k_b, 0, 0)
        square, tanh, half, sech, slope = gelu_parts(u)
        h_b = (u * half).astype(BF)
        slope1 = half + 0.5 * u * sech * slope
        second = sech * (GELU_A + (6.0 * GELU_A * GELU_B) * square - u * tanh * slope * slope)
        ht[slot] = h_b
        g1[slot] = slope1
        resid = k_b.astype(F32) - v_b.astype(F32) + dot(b_b, h_b, 1, 0)
        r_b = resid.astype(BF)
        rt[slot] = r_b
        p = dot(b_b, r_b, 0, 0)
        g2p[slot] = second * p
        gu_b = (slope1 * p).astype(BF)
        gu[slot] = gu_b
        new_a = (a_b.astype(F32) - rate * dot(k_b, gu_b, 1, 1)).astype(BF)
        new_b = (b_b.astype(F32) - rate * dot(r_b, h_b, 1, 1)).astype(BF)
        uq = dot(new_a, q_b, 0, 0)
        square, tanh, half, sech, slope = gelu_parts(uq)
        hq_b = (uq * half).astype(BF)
        guq_b = ((half + 0.5 * uq * sech * slope) * dot(new_b, c_b, 0, 0)).astype(BF)
        gab[slot, 0] = dot(q_b, guq_b, 1, 1)
        gab[slot, 1] = dot(c_b, hq_b, 1, 1)
        gq[slot, 0] = (c_b.astype(F32) + dot(new_a, guq_b, 1, 0)).astype(BF)

    for slot in range(nseg):
        local(slot)

    def step(turn, carry):
        slot = table[nseg - 1 - turn]
        t_a = carry[0] + gab[slot, 0]
        t_b = carry[1] + gab[slot, 1]
        a_b, b_b = wts[slot, 0], wts[slot, 1]
        k_b = qkv[slot, 1]
        h_b, r_b, gu_b = ht[slot], rt[slot], gu[slot]
        ta_b, tb_b = t_a.astype(BF), t_b.astype(BF)
        du = dot(ta_b, k_b, 0, 0)
        dh_b = (g1[slot] * du).astype(BF)
        dr = dot(b_b, dh_b, 1, 0) + dot(tb_b, h_b, 1, 0)
        dr_b = dr.astype(BF)
        dp = dot(b_b, dr_b, 0, 0) + dot(tb_b, r_b, 0, 0)
        dgu_b = (g2p[slot] * du + g1[slot] * dp).astype(BF)
        c_a = t_a - rate * dot(k_b, dgu_b, 1, 1)
        c_b = t_b - rate * (dot(dr_b, h_b, 1, 1) + dot(r_b, dh_b, 1, 1))
        left = jnp.concatenate([a_b, ta_b], 1)
        gk = dr + dot(left, jnp.concatenate([dgu_b, gu_b], 0), 1, 0)
        gq[slot, 1] = (-rate * gk).astype(BF)
        gq[slot, 2] = (rate * dr).astype(BF)
        wts[slot, 0] = c_a.astype(BF)
        wts[slot, 1] = c_b.astype(BF)
        return (c_a, c_b)

    zero = jnp.zeros((feats, hid), F32)
    carry = (zero, zero)
    for turn in range(nseg):
        carry = step(turn, carry)

    for slot in range(nseg):
        dx, dc = slot // CORES, slot % CORES
        if dx == 0:
            kept[dc] = wts[slot]
        else:
            sent[dx - 1, dc * rows : (dc + 1) * rows] = gq[slot].reshape(rows, tokens)
            at = CORES * rows + dc * 2 * feats
            sent[dx - 1, at : at + 2 * feats] = wts[slot].reshape(2 * feats, hid)
    for dz in range(nseq):
        at = pl.multiple_of(table[nseg + (nseq - dz) % nseq] * chunk, chunk)
        total = jnp.zeros((rows, chunk), F32)
        for slot in range(nseg):
            part = li[slot][:tokens, pl.ds(at, chunk)]
            total += dot(gq[slot].reshape(rows, tokens), part, 1, 0)
        gp[dz][...] = total.astype(gp[dz].dtype)


def input_kernel(dims, table, *refs):
    nseg, nseq, hpd, feats, hid, tokens, chunk = dims
    chips = nseg // CORES
    rows = 3 * feats
    gq, refs = refs[:hpd], refs[hpd:]
    kept, refs = refs[:hpd], refs[hpd:]
    sent, refs = refs[: hpd * (chips - 1)], refs[hpd * (chips - 1) :]
    wt, refs = refs[:nseq], refs[nseq:]
    away, (home, aside, leave) = refs[: chips - 1], refs[chips - 1 :]
    for dc in range(CORES):
        left = [gq[h][dc, p] for p in range(3) for h in range(hpd)]
        for dx in range(chips - 1):
            for p in range(3):
                at = dc * rows + p * feats
                left += [sent[h * (chips - 1) + dx][at : at + feats] for h in range(hpd)]
        left = jnp.concatenate(left)
        for back in range(nseq):
            at = pl.multiple_of(table[nseg + back] * chunk, chunk)
            right = jnp.concatenate([wt[back][...]] + [value[back] for value in away])
            value = dot(left, right, 0, 0)
            out = (home, aside)[dc]
            out[:, pl.ds(at, chunk)] = value.astype(out.dtype)
    at = CORES * rows + 2 * feats
    for head in range(hpd):
        leave[head * chips] = kept[head][1].reshape(2 * feats, hid)
        for dx in range(1, chips):
            leave[head * chips + dx] = sent[head * (chips - 1) + dx - 1][at : at + 2 * feats]


def sum_kernel(*refs):
    total = refs[0][...]
    for ref in refs[1:-1]:
        total += ref[...].astype(F32)
    total = total.T.astype(BF)
    half = total.shape[0] // 2
    refs[-1][...] = jnp.concatenate([total[:half], total[half:]], 1)


def join_kernel(dims, table, *refs):
    nseg, nseq, hpd, feats, hid, tokens, chunk = dims
    chips = nseg // CORES
    far, near, out = refs[: hpd * chips], refs[hpd * chips], refs[hpd * chips + 1]
    wide = CORES * hpd * feats
    half = chunk // 2
    me = table[nseg + nseq + 1]
    chip = me // CORES
    even = me % CORES == 0
    for dx in range(chips):
        source = (chip - dx + chips) % chips
        for side in range(2):
            cut = slice(side * 3 * feats, (side + 1) * 3 * feats)
            mine = [far[h * chips + dx][:, cut].astype(F32) for h in range(hpd)]
            other = [near[h * chips + dx, :, cut].astype(F32) for h in range(hpd)]
            for part in range(3):
                cut = slice(part * feats, (part + 1) * feats)
                a = jnp.concatenate([value[:, cut] for value in mine + other], 1)
                b = jnp.concatenate([value[:, cut] for value in other + mine], 1)
                at = pl.multiple_of((part * nseg * hpd * feats) + source * wide, wide)
                rows = pl.ds(side * half, half)
                out[rows, pl.ds(at, wide)] = jnp.where(even, a, b)


def weights_kernel(dims, table, *refs):
    nseg, nseq, hpd, feats, hid, tokens, chunk = dims
    chips = nseg // CORES
    kept, refs = refs[:hpd], refs[hpd:]
    sent, refs = refs[: hpd * (chips - 1)], refs[hpd * (chips - 1) :]
    got, out = refs
    at = CORES * 3 * feats
    for head in range(hpd):
        for slot in range(nseg):
            dx, dc = slot // CORES, slot % CORES
            if dc == 1:
                piece = got[head * chips + dx]
            elif dx == 0:
                piece = kept[head][0].reshape(2 * feats, hid)
            else:
                piece = sent[head * (chips - 1) + dx - 1][at : at + 2 * feats]
            index = table[nseg + nseq + 2 + slot] * hpd + head
            out[0, index] = piece[:feats].astype(F32)
            out[1, index] = piece[feats:].astype(F32)


def per_device(layer_input, out_cot, w_proj, inner_start, rates):
    rows = layer_input[0]
    tokens, width = rows.shape
    heads = rates.shape[0]
    feats, hid = inner_start.shape[4:]
    nseg, nseq = lax.axis_size("seg"), lax.axis_size("seq")
    chips = nseg // CORES
    hpd = heads // nseg
    own = hpd * feats
    chunk = width // nseq
    me, place = lax.axis_index("seg"), lax.axis_index("seq")
    chip, core = me // CORES, me % CORES
    barrier = lax.optimization_barrier

    def to_chip(value, dx):
        pairs = [(i, (i + dx * CORES) % nseg) for i in range(nseg)]
        return lax.ppermute(value, "seg", pairs)

    def to_core(value):
        return lax.ppermute(value, "seg", [(i, i ^ 1) for i in range(nseg)])

    def to_seq(value, dz):
        return lax.ppermute(value, "seq", [(i, (i + dz) % nseq) for i in range(nseq)])

    def kernel(body, name, limit, cost, outs, scratch, *operands):
        smem = pl.BlockSpec(memory_space=pltpu.SMEM)
        vmem = pl.BlockSpec(memory_space=pltpu.VMEM)
        return pl.pallas_call(
            body,
            in_specs=[smem if o.ndim == 1 else vmem for o in operands],
            out_specs=[vmem] * len(outs),
            out_shape=[jax.ShapeDtypeStruct(*o) for o in outs],
            scratch_shapes=[pltpu.VMEM(*o) for o in scratch],
            compiler_params=pltpu.CompilerParams(vmem_limit_bytes=limit * MIB),
            cost_estimate=pl.CostEstimate(flops=0, bytes_accessed=cost, transcendentals=0),
            name=name,
        )(*operands)

    def summed(pieces):
        return kernel(sum_kernel, "sum", 12, 0, [((chunk // 2, 6 * feats), BF)], [], *pieces)[0]

    crossed = chips == 2 and lax.axis_size("groups") == 2
    shift = lax.axis_index("groups") if crossed else 0

    segs = jnp.arange(nseg, dtype=jnp.int32)
    slot_of = ((chip - segs // CORES) % chips) * CORES + (core + segs) % CORES
    back = (place - jnp.arange(nseq, dtype=jnp.int32)) % nseq
    dest = ((chip + shift + segs // CORES) % chips) * CORES + (core + segs) % CORES
    table = jnp.concatenate([slot_of, back, jnp.stack([dest[0] * hpd, dest[0]]), dest])
    table = table.astype(jnp.int32)
    dims = (nseg, nseq, hpd, feats, hid, tokens, chunk)

    wide = max(own, 128)
    deep = -(-3 * own * hid // (width * TILE)) * TILE
    hbm = pl.BlockSpec(memory_space=pltpu.HBM)
    vmem = pl.BlockSpec(memory_space=pltpu.VMEM)
    outs = [((3 * own, chunk), BF), ((deep, width), BF), ((tokens + deep, width), BF)]
    outs += [((tokens + CORES * deep, width), BF)] * (chips - 1)
    operands = (rows, w_proj, out_cot[0], inner_start[0, 0])
    mine, pack, *ships = pl.pallas_call(
        functools.partial(prep_kernel, dims),
        in_specs=[pl.BlockSpec(memory_space=pltpu.SMEM)] + [hbm] * 4,
        out_specs=[vmem] * len(outs),
        out_shape=[jax.ShapeDtypeStruct(*o) for o in outs],
        scratch_shapes=[
            pltpu.VMEM((3, chunk, wide), BF),
            pltpu.VMEM((tokens, heads * feats), BF),
            pltpu.VMEM((2, heads, feats, hid), F32),
            pltpu.VMEM((heads * feats, tokens), BF),
            pltpu.SemaphoreType.DMA((5 + chips,)),
        ],
        compiler_params=pltpu.CompilerParams(vmem_limit_bytes=16 * MIB),
        cost_estimate=pl.CostEstimate(flops=0, bytes_accessed=0, transcendentals=0),
        name="prep",
    )(table, *[pltpu.with_memory_space_constraint(o, pltpu.HBM) for o in operands])
    near = to_core(ships[0])
    far = [to_chip(ships[dx], dx) for dx in range(1, chips)]
    wt = [mine] + [to_seq(mine, dz) for dz in range(1, nseq)]
    far, near, wt = barrier((far, near, wt))
    li = [rows, near]
    for value in far:
        li += [value, to_core(value)]

    def to_others(value):
        if crossed:
            return [lax.ppermute(value, "groups", [(0, 1), (1, 0)])]
        return [to_chip(value, -dx) for dx in range(1, chips)]

    def inner(head):
        return kernel(
            functools.partial(inner_kernel, dims, head),
            "inner",
            36,
            0,
            [((3 * feats, chunk), BF if dz else F32) for dz in range(nseq)]
            + [((nseg, 3, feats, tokens), BF)]
            + [((chips - 1, 10 * feats, tokens), BF)]
            + [((CORES, 2, feats, hid), BF)],
            [
                ((nseg, 3, feats, tokens), BF),
                ((nseg, 2, feats, hid), BF),
                ((nseg, feats, tokens), BF),
                ((nseg, hid, tokens), BF),
                ((nseg, feats, tokens), BF),
                ((nseg, hid, tokens), F32),
                ((nseg, hid, tokens), F32),
                ((nseg, hid, tokens), BF),
                ((nseg, 2, feats, hid), F32),
            ],
            table,
            rates,
            *li,
            *wt,
            pack,
        )

    away = to_others(jnp.stack(wt))
    grads, kept, sent, projs, pieces = [], [], [], [], None
    for head in range(hpd):
        outs = inner(head)
        gp, gq, send, keep = outs[:nseq], outs[nseq], outs[nseq + 1], outs[nseq + 2]
        if head == hpd - 1:
            gp, send, pieces, sent = barrier((gp, send, pieces, sent))
        if pieces is not None:
            total = summed(pieces)
            projs += [total] + [to_chip(total, dx) for dx in range(1, chips)]
        pieces = [gp[0]] + [to_seq(gp[dz], dz) for dz in range(1, nseq)]
        sent += [to_chip(send[dx - 1], -dx) for dx in range(1, chips)]
        grads.append(gq)
        kept.append(keep)

    home, aside, leave = kernel(
        functools.partial(input_kernel, dims),
        "input",
        24,
        10 * MIB,
        [((tokens, width), F32), ((tokens, width), BF)]
        + [((hpd * chips, 2 * feats, hid), BF)],
        [],
        table,
        *grads,
        *kept,
        *sent,
        *wt,
        *away,
    )
    pieces, projs, home, aside, leave = barrier((pieces, projs, home, aside, leave))

    total = summed(pieces)
    projs += [total] + [to_chip(total, dx) for dx in range(1, chips)]
    aside, leave = to_core(aside), to_core(leave)
    grad_input = (home + aside.astype(F32)).astype(BF)
    (grad_inner,) = kernel(
        functools.partial(weights_kernel, dims),
        "weights",
        8,
        10 * MIB,
        [((2, heads, feats, hid), F32)],
        [],
        table,
        *kept,
        *sent,
        leave,
    )
    projs, grad_input, grad_inner = barrier((projs, grad_input, grad_inner))
    (grad_proj,) = kernel(
        functools.partial(join_kernel, dims),
        "join",
        16,
        0,
        [((chunk, 3 * heads * feats), F32)],
        [],
        table,
        *projs,
        to_core(jnp.stack(projs)),
    )
    return (grad_input[None], grad_proj, grad_inner[None, None])


def solution(mesh):
    placed = (
        P(("groups", "seq"), "seg", None),
        P(("groups", "seq"), "seg", None),
        P("seq", None),
        P(("groups", "seq"), "seg", None, None, None, None),
        P(),
    )
    return jax.shard_map(
        per_device,
        mesh=mesh,
        in_specs=placed,
        out_specs=(
            P(("groups", "seq"), "seg", None),
            P(("groups", "seq"), None),
            P(("groups", "seq"), "seg", None, None, None, None),
        ),
        check_vma=False,
    )
```

```python
import functools
from itertools import zip_longest

import jax
import jax.numpy as jnp
from jax import lax
from jax.experimental import pallas as pl
from jax.experimental.pallas import tpu as pltpu
from jax.sharding import PartitionSpec as P

MB = 256
BF = jnp.bfloat16
F32 = jnp.float32
CORES = 2
GELU_A = 0.7978845608028654
GELU_B = 0.044715
MIB = 1024 * 1024
TILE = 16
GROUP = 4


def dot(a, b, ca, cb):
    return lax.dot_general(a, b, (((ca,), (cb,)), ((), ())), preferred_element_type=F32)


def gelu_parts(u):
    square = u * u
    tanh = jnp.tanh(u * (GELU_A + (GELU_A * GELU_B) * square))
    half = 0.5 * (1.0 + tanh)
    sech = 1.0 - tanh * tanh
    slope = GELU_A + (3.0 * GELU_A * GELU_B) * square
    return square, tanh, half, sech, slope


def packed(row, deep, hid):
    return row % deep, row // deep * hid


def prep_kernel(dims, table, rows, w, cots, start, mine, pack, *refs):
    nseg, nseq, hpd, feats, hid, tokens, chunk = dims
    ships, refs = refs[: nseg // CORES], refs[nseg // CORES :]
    cut, held, weights, turned, sem = refs
    own = hpd * feats
    wide = cut.shape[2]
    deep = pack.shape[0]
    me = table[nseg + nseq + 1]
    base = me * own // wide * wide
    copies = []
    for part in range(3):
        at = pl.multiple_of(part * nseg * own + base, wide)
        copies.append(pltpu.make_async_copy(w.at[:, pl.ds(at, wide)], cut.at[part], sem.at[part]))
    copies.append(pltpu.make_async_copy(cots, held, sem.at[3]))
    copies.append(pltpu.make_async_copy(start, weights, sem.at[4]))
    for i, ship in enumerate(ships):
        copies.append(pltpu.make_async_copy(rows, ship.at[pl.ds(0, tokens)], sem.at[5 + i]))
    for copy in copies:
        copy.start()
    for part in range(3):
        copies[part].wait()
        block = cut[part].T
        even = block[:own]
        for i in range(1, wide // own):
            even = jnp.where(me * own % wide == i * own, block[i * own : (i + 1) * own], even)
        mine[part * own : (part + 1) * own] = even
    copies[3].wait()
    turned[...] = held[...].T
    copies[4].wait()
    for slot in range(nseg):
        dest = table[nseg + nseq + 2 + slot]
        dx, dc = slot // CORES, slot % CORES
        target, low = (pack, 0) if slot == 0 else (ships[dx], tokens + (deep * dc if dx else 0))
        for i in range(3 * hpd):
            kind, head = i // hpd, i % hpd
            if kind < 2:
                value = weights[kind, dest * hpd + head].astype(BF)
            else:
                value = turned[pl.ds(pl.multiple_of((dest * hpd + head) * feats, feats), feats)]
            for j in range(0, feats, TILE):
                top, left = packed(i * feats + j, deep, hid)
                target[low + top : low + top + TILE, left : left + hid] = value[j : j + TILE]
    for copy in copies[5:]:
        copy.wait()


def inner_kernel(dims, head, table, rates, *refs):
    nseg, nseq, hpd, feats, hid, tokens, chunk = dims
    chips = nseg // CORES
    li, refs = refs[:nseg], refs[nseg:]
    wt, refs = refs[:nseq], refs[nseq:]
    pack, refs = refs[0], refs[1:]
    gp, refs = refs[:nseq], refs[nseq:]
    gq, sent, kept, qkv, wts, cts, ht, rt, g1, g2p, gu, gab, res = refs
    rows = 3 * feats
    own = hpd * feats
    first = head * feats

    deep = pack.shape[0]

    for slot in range(nseg):
        dx, dc = slot // CORES, slot % CORES
        source, low = (pack, 0) if slot == 0 else (li[slot], tokens + (deep * dc if dx else 0))
        for i, piece in enumerate((wts.at[slot, 0], wts.at[slot, 1], cts.at[slot])):
            for j in range(0, feats, TILE):
                top, left = packed((i * hpd + head) * feats + j, deep, hid)
                value = source[low + top : low + top + TILE, left : left + hid]
                piece[j : j + TILE] = value
        total = jnp.zeros((rows, tokens), F32)
        for back in range(nseq):
            at = pl.multiple_of(table[nseg + back] * chunk, chunk)
            left = jnp.concatenate(
                [wt[back][p * own + first : p * own + first + feats] for p in range(3)]
            )
            total += dot(left, li[slot][:tokens, pl.ds(at, chunk)], 1, 1)
        qkv[slot] = total.astype(BF).reshape(3, feats, tokens)
    rate = rates[table[nseg + nseq] + head] * (1.0 / MB)

    def local(slot):
        a_b, b_b = wts[slot, 0], wts[slot, 1]
        q_b, k_b, v_b = qkv[slot, 0], qkv[slot, 1], qkv[slot, 2]
        c_b = cts[slot]
        u = dot(a_b, k_b, 0, 0)
        yield
        square, tanh, half, sech, slope = gelu_parts(u)
        h_b = (u * half).astype(BF)
        yield
        slope1 = half + 0.5 * u * sech * slope
        second = sech * (GELU_A + (6.0 * GELU_A * GELU_B) * square - u * tanh * slope * slope)
        ht[slot] = h_b
        g1[slot] = slope1
        resid = k_b.astype(F32) - v_b.astype(F32) + dot(b_b, h_b, 1, 0)
        r_b = resid.astype(BF)
        yield
        rt[slot] = r_b
        p = dot(b_b, r_b, 0, 0)
        g2p[slot] = second * p
        gu_b = (slope1 * p).astype(BF)
        gu[slot] = gu_b
        yield
        new_a = (a_b.astype(F32) - rate * dot(k_b, gu_b, 1, 1)).astype(BF)
        new_b = (b_b.astype(F32) - rate * dot(r_b, h_b, 1, 1)).astype(BF)
        uq = dot(new_a, q_b, 0, 0)
        yield
        square, tanh, half, sech, slope = gelu_parts(uq)
        hq_b = (uq * half).astype(BF)
        guq_b = ((half + 0.5 * uq * sech * slope) * dot(new_b, c_b, 0, 0)).astype(BF)
        gab[slot, 0] = dot(q_b, guq_b, 1, 1)
        yield
        gab[slot, 1] = dot(c_b, hq_b, 1, 1)
        gq[slot, 0] = (c_b.astype(F32) + dot(new_a, guq_b, 1, 0)).astype(BF)

    for low in range(0, nseg, GROUP):
        for _ in zip_longest(*[local(slot) for slot in range(low, min(low + GROUP, nseg))]):
            pass

    def end(slot, k_b, a_b, ta_b, gu_b, dr, dgu_b, c_a, c_b):
        left = jnp.concatenate([a_b, ta_b], 1)
        gk = dr + dot(left, jnp.concatenate([dgu_b, gu_b], 0), 1, 0)
        gq[slot, 1] = (-rate * gk).astype(BF)
        gq[slot, 2] = (rate * dr).astype(BF)
        res[slot, 0] = c_a.astype(BF)
        res[slot, 1] = c_b.astype(BF)

    c_a = c_b = jnp.zeros((feats, hid), F32)
    late = None
    for turn in range(nseg):
        slot = table[nseg - 1 - turn]
        t_a = c_a + gab[slot, 0]
        t_b = c_b + gab[slot, 1]
        a_b, b_b = wts[slot, 0], wts[slot, 1]
        k_b = qkv[slot, 1]
        h_b, r_b, gu_b = ht[slot], rt[slot], gu[slot]
        ta_b, tb_b = t_a.astype(BF), t_b.astype(BF)
        du = dot(ta_b, k_b, 0, 0)
        dr_h, dp_r = dot(tb_b, h_b, 1, 0), dot(tb_b, r_b, 0, 0)
        if late is not None:
            end(*late)
        dh_b = (g1[slot] * du).astype(BF)
        dr = dot(b_b, dh_b, 1, 0) + dr_h
        dr_b = dr.astype(BF)
        dp = dot(b_b, dr_b, 0, 0) + dp_r
        c_b = t_b - rate * (dot(dr_b, h_b, 1, 1) + dot(r_b, dh_b, 1, 1))
        dgu_b = (g2p[slot] * du + g1[slot] * dp).astype(BF)
        c_a = t_a - rate * dot(k_b, dgu_b, 1, 1)
        late = (slot, k_b, a_b, ta_b, gu_b, dr, dgu_b, c_a, c_b)
    end(*late)

    for slot in range(nseg):
        dx, dc = slot // CORES, slot % CORES
        if dx == 0:
            kept[dc] = res[slot]
        else:
            sent[dx - 1, dc * rows : (dc + 1) * rows] = gq[slot].reshape(rows, tokens)
            at = CORES * rows + dc * 2 * feats
            sent[dx - 1, at : at + 2 * feats] = res[slot].reshape(2 * feats, hid)
    for dz in range(nseq):
        at = pl.multiple_of(table[nseg + (nseq - dz) % nseq] * chunk, chunk)
        total = jnp.zeros((rows, chunk), F32)
        for slot in range(nseg):
            part = li[slot][:tokens, pl.ds(at, chunk)]
            total += dot(gq[slot].reshape(rows, tokens), part, 1, 0)
        gp[dz][...] = total.astype(gp[dz].dtype)


def input_kernel(dims, table, *refs):
    nseg, nseq, hpd, feats, hid, tokens, chunk = dims
    chips = nseg // CORES
    rows = 3 * feats
    gq, refs = refs[:hpd], refs[hpd:]
    kept, refs = refs[:hpd], refs[hpd:]
    sent, refs = refs[: hpd * (chips - 1)], refs[hpd * (chips - 1) :]
    wt, refs = refs[:nseq], refs[nseq:]
    away, (home, aside, leave) = refs[: chips - 1], refs[chips - 1 :]
    for dc in range(CORES):
        left = [gq[h][dc, p] for p in range(3) for h in range(hpd)]
        for dx in range(chips - 1):
            for p in range(3):
                at = dc * rows + p * feats
                left += [sent[h * (chips - 1) + dx][at : at + feats] for h in range(hpd)]
        left = jnp.concatenate(left)
        for back in range(nseq):
            at = pl.multiple_of(table[nseg + back] * chunk, chunk)
            right = jnp.concatenate([wt[back][...]] + [value[back] for value in away])
            value = dot(left, right, 0, 0)
            out = (home, aside)[dc]
            out[:, pl.ds(at, chunk)] = value.astype(out.dtype)
    at = CORES * rows + 2 * feats
    for head in range(hpd):
        leave[head * chips] = kept[head][1].reshape(2 * feats, hid)
        for dx in range(1, chips):
            leave[head * chips + dx] = sent[head * (chips - 1) + dx - 1][at : at + 2 * feats]


def sum_kernel(*refs):
    total = refs[0][...]
    for ref in refs[1:-1]:
        total += ref[...].astype(F32)
    total = total.T.astype(BF)
    half = total.shape[0] // 2
    refs[-1][...] = jnp.concatenate([total[:half], total[half:]], 1)


def join_kernel(dims, table, *refs):
    nseg, nseq, hpd, feats, hid, tokens, chunk = dims
    chips = nseg // CORES
    far, near, out = refs[: hpd * chips], refs[hpd * chips], refs[hpd * chips + 1]
    wide = CORES * hpd * feats
    half = chunk // 2
    me = table[nseg + nseq + 1]
    chip = me // CORES
    even = me % CORES == 0
    for dx in range(chips):
        source = (chip - dx + chips) % chips
        for side in range(2):
            cut = slice(side * 3 * feats, (side + 1) * 3 * feats)
            mine = [far[h * chips + dx][:, cut].astype(F32) for h in range(hpd)]
            other = [near[h * chips + dx, :, cut].astype(F32) for h in range(hpd)]
            for part in range(3):
                cut = slice(part * feats, (part + 1) * feats)
                a = jnp.concatenate([value[:, cut] for value in mine + other], 1)
                b = jnp.concatenate([value[:, cut] for value in other + mine], 1)
                at = pl.multiple_of((part * nseg * hpd * feats) + source * wide, wide)
                rows = pl.ds(side * half, half)
                out[rows, pl.ds(at, wide)] = jnp.where(even, a, b)


def weights_kernel(dims, table, *refs):
    nseg, nseq, hpd, feats, hid, tokens, chunk = dims
    chips = nseg // CORES
    kept, refs = refs[:hpd], refs[hpd:]
    sent, refs = refs[: hpd * (chips - 1)], refs[hpd * (chips - 1) :]
    got, out = refs
    at = CORES * 3 * feats
    for head in range(hpd):
        for slot in range(nseg):
            dx, dc = slot // CORES, slot % CORES
            if dc == 1:
                piece = got[head * chips + dx]
            elif dx == 0:
                piece = kept[head][0].reshape(2 * feats, hid)
            else:
                piece = sent[head * (chips - 1) + dx - 1][at : at + 2 * feats]
            index = table[nseg + nseq + 2 + slot] * hpd + head
            out[0, index] = piece[:feats].astype(F32)
            out[1, index] = piece[feats:].astype(F32)


def per_device(layer_input, out_cot, w_proj, inner_start, rates):
    rows = layer_input[0]
    tokens, width = rows.shape
    heads = rates.shape[0]
    feats, hid = inner_start.shape[4:]
    nseg, nseq = lax.axis_size("seg"), lax.axis_size("seq")
    chips = nseg // CORES
    hpd = heads // nseg
    own = hpd * feats
    chunk = width // nseq
    me, place = lax.axis_index("seg"), lax.axis_index("seq")
    chip, core = me // CORES, me % CORES
    barrier = lax.optimization_barrier

    def to_chip(value, dx):
        pairs = [(i, (i + dx * CORES) % nseg) for i in range(nseg)]
        return lax.ppermute(value, "seg", pairs)

    def to_core(value):
        return lax.ppermute(value, "seg", [(i, i ^ 1) for i in range(nseg)])

    def to_seq(value, dz):
        return lax.ppermute(value, "seq", [(i, (i + dz) % nseq) for i in range(nseq)])

    def kernel(body, name, limit, cost, outs, scratch, *operands):
        smem = pl.BlockSpec(memory_space=pltpu.SMEM)
        vmem = pl.BlockSpec(memory_space=pltpu.VMEM)
        return pl.pallas_call(
            body,
            in_specs=[smem if o.ndim == 1 else vmem for o in operands],
            out_specs=[vmem] * len(outs),
            out_shape=[jax.ShapeDtypeStruct(*o) for o in outs],
            scratch_shapes=[pltpu.VMEM(*o) for o in scratch],
            compiler_params=pltpu.CompilerParams(vmem_limit_bytes=limit * MIB),
            cost_estimate=pl.CostEstimate(flops=0, bytes_accessed=cost, transcendentals=0),
            name=name,
        )(*operands)

    def summed(pieces):
        return kernel(sum_kernel, "sum", 12, 0, [((chunk // 2, 6 * feats), BF)], [], *pieces)[0]

    crossed = chips == 2 and lax.axis_size("groups") == 2
    shift = lax.axis_index("groups") if crossed else 0

    segs = jnp.arange(nseg, dtype=jnp.int32)
    slot_of = ((chip - segs // CORES) % chips) * CORES + (core + segs) % CORES
    back = (place - jnp.arange(nseq, dtype=jnp.int32)) % nseq
    dest = ((chip + shift + segs // CORES) % chips) * CORES + (core + segs) % CORES
    table = jnp.concatenate([slot_of, back, jnp.stack([dest[0] * hpd, dest[0]]), dest])
    table = table.astype(jnp.int32)
    dims = (nseg, nseq, hpd, feats, hid, tokens, chunk)

    wide = max(own, 128)
    deep = -(-3 * own * hid // (width * TILE)) * TILE
    hbm = pl.BlockSpec(memory_space=pltpu.HBM)
    vmem = pl.BlockSpec(memory_space=pltpu.VMEM)
    outs = [((3 * own, chunk), BF), ((deep, width), BF), ((tokens + deep, width), BF)]
    outs += [((tokens + CORES * deep, width), BF)] * (chips - 1)
    operands = (rows, w_proj, out_cot[0], inner_start[0, 0])
    mine, pack, *ships = pl.pallas_call(
        functools.partial(prep_kernel, dims),
        in_specs=[pl.BlockSpec(memory_space=pltpu.SMEM)] + [hbm] * 4,
        out_specs=[vmem] * len(outs),
        out_shape=[jax.ShapeDtypeStruct(*o) for o in outs],
        scratch_shapes=[
            pltpu.VMEM((3, chunk, wide), BF),
            pltpu.VMEM((tokens, heads * feats), BF),
            pltpu.VMEM((2, heads, feats, hid), F32),
            pltpu.VMEM((heads * feats, tokens), BF),
            pltpu.SemaphoreType.DMA((5 + chips,)),
        ],
        compiler_params=pltpu.CompilerParams(vmem_limit_bytes=16 * MIB),
        cost_estimate=pl.CostEstimate(flops=0, bytes_accessed=0, transcendentals=0),
        name="prep",
    )(table, *[pltpu.with_memory_space_constraint(o, pltpu.HBM) for o in operands])
    near = to_core(ships[0])
    far = [to_chip(ships[dx], dx) for dx in range(1, chips)]
    wt = [mine] + [to_seq(mine, dz) for dz in range(1, nseq)]
    far, near, wt = barrier((far, near, wt))
    li = [rows, near]
    for value in far:
        li += [value, to_core(value)]

    def to_others(value):
        if crossed:
            return [lax.ppermute(value, "groups", [(0, 1), (1, 0)])]
        return [to_chip(value, -dx) for dx in range(1, chips)]

    def inner(head):
        return kernel(
            functools.partial(inner_kernel, dims, head),
            "inner",
            36,
            0,
            [((3 * feats, chunk), BF if dz else F32) for dz in range(nseq)]
            + [((nseg, 3, feats, tokens), BF)]
            + [((chips - 1, 10 * feats, tokens), BF)]
            + [((CORES, 2, feats, hid), BF)],
            [
                ((nseg, 3, feats, tokens), BF),
                ((nseg, 2, feats, hid), BF),
                ((nseg, feats, tokens), BF),
                ((nseg, hid, tokens), BF),
                ((nseg, feats, tokens), BF),
                ((nseg, hid, tokens), F32),
                ((nseg, hid, tokens), F32),
                ((nseg, hid, tokens), BF),
                ((nseg, 2, feats, hid), F32),
                ((nseg, 2, feats, hid), BF),
            ],
            table,
            rates,
            *li,
            *wt,
            pack,
        )

    away = to_others(jnp.stack(wt))
    grads, kept, sent, projs, pieces = [], [], [], [], None
    for head in range(hpd):
        outs = inner(head)
        gp, gq, send, keep = outs[:nseq], outs[nseq], outs[nseq + 1], outs[nseq + 2]
        if pieces is not None:
            gp, send, pieces[1], sent = barrier((gp, send, pieces[1], sent))
        if pieces is not None:
            total = summed(pieces)
            projs += [total] + [to_chip(total, dx) for dx in range(1, chips)]
        pieces = [gp[0]] + [to_seq(gp[dz], dz) for dz in range(1, nseq)]
        sent += [to_chip(send[dx - 1], -dx) for dx in range(1, chips)]
        grads.append(gq)
        kept.append(keep)

    home, aside, leave = kernel(
        functools.partial(input_kernel, dims),
        "input",
        24,
        10 * MIB,
        [((tokens, width), F32), ((tokens, width), BF)]
        + [((hpd * chips, 2 * feats, hid), BF)],
        [],
        table,
        *grads,
        *kept,
        *sent,
        *wt,
        *away,
    )
    pieces, projs, home, aside, leave = barrier((pieces, projs, home, aside, leave))

    total = summed(pieces)
    projs += [total] + [to_chip(total, dx) for dx in range(1, chips)]
    aside, leave = to_core(aside), to_core(leave)
    grad_input = (home + aside.astype(F32)).astype(BF)
    (grad_inner,) = kernel(
        functools.partial(weights_kernel, dims),
        "weights",
        8,
        10 * MIB,
        [((2, heads, feats, hid), F32)],
        [],
        table,
        *kept,
        *sent,
        leave,
    )
    projs, grad_input, grad_inner = barrier((projs, grad_input, grad_inner))
    (grad_proj,) = kernel(
        functools.partial(join_kernel, dims),
        "join",
        16,
        0,
        [((chunk, 3 * heads * feats), F32)],
        [],
        table,
        *projs,
        to_core(jnp.stack(projs)),
    )
    return (grad_input[None], grad_proj, grad_inner[None, None])


def solution(mesh):
    placed = (
        P(("groups", "seq"), "seg", None),
        P(("groups", "seq"), "seg", None),
        P("seq", None),
        P(("groups", "seq"), "seg", None, None, None, None),
        P(),
    )
    return jax.shard_map(
        per_device,
        mesh=mesh,
        in_specs=placed,
        out_specs=(
            P(("groups", "seq"), "seg", None),
            P(("groups", "seq"), None),
            P(("groups", "seq"), "seg", None, None, None, None),
        ),
        check_vma=False,
    )
```

```python
import functools
from itertools import zip_longest

import jax
import jax.numpy as jnp
from jax import lax
from jax.experimental import pallas as pl
from jax.experimental.pallas import tpu as pltpu
from jax.sharding import PartitionSpec as P

MB = 256
BF = jnp.bfloat16
F32 = jnp.float32
CORES = 2
GELU_A = 0.7978845608028654
GELU_B = 0.044715
MIB = 1024 * 1024
TILE = 16
GROUP = 4


def dot(a, b, ca, cb):
    return lax.dot_general(a, b, (((ca,), (cb,)), ((), ())), preferred_element_type=F32)


def gelu_parts(u):
    square = u * u
    tanh = jnp.tanh(u * (GELU_A + (GELU_A * GELU_B) * square))
    half = 0.5 * (1.0 + tanh)
    sech = 1.0 - tanh * tanh
    slope = GELU_A + (3.0 * GELU_A * GELU_B) * square
    return square, tanh, half, sech, slope


def packed(row, deep, hid):
    return row % deep, row // deep * hid


def prep_kernel(dims, table, rows, w, cots, start, mine, pack, *refs):
    nseg, nseq, hpd, feats, hid, tokens, chunk = dims
    ships, refs = refs[: nseg // CORES], refs[nseg // CORES :]
    cut, held, weights, turned, sem = refs
    own = hpd * feats
    wide = cut.shape[2]
    deep = pack.shape[0]
    me = table[nseg + nseq + 1]
    base = me * own // wide * wide
    copies = []
    for part in range(3):
        at = pl.multiple_of(part * nseg * own + base, wide)
        copies.append(pltpu.make_async_copy(w.at[:, pl.ds(at, wide)], cut.at[part], sem.at[part]))
    copies.append(pltpu.make_async_copy(cots, held, sem.at[3]))
    copies.append(pltpu.make_async_copy(start, weights, sem.at[4]))
    for i, ship in enumerate(ships):
        copies.append(pltpu.make_async_copy(rows, ship.at[pl.ds(0, tokens)], sem.at[5 + i]))
    for copy in copies:
        copy.start()
    for part in range(3):
        copies[part].wait()
        block = cut[part].T
        even = block[:own]
        for i in range(1, wide // own):
            even = jnp.where(me * own % wide == i * own, block[i * own : (i + 1) * own], even)
        mine[part * own : (part + 1) * own] = even
    copies[3].wait()
    turned[...] = held[...].T
    copies[4].wait()
    for slot in range(nseg):
        dest = table[nseg + nseq + 2 + slot]
        dx, dc = slot // CORES, slot % CORES
        target, low = (pack, 0) if slot == 0 else (ships[dx], tokens + (deep * dc if dx else 0))
        for i in range(3 * hpd):
            kind, head = i // hpd, i % hpd
            if kind < 2:
                value = weights[kind, dest * hpd + head].astype(BF)
            else:
                value = turned[pl.ds(pl.multiple_of((dest * hpd + head) * feats, feats), feats)]
            for j in range(0, feats, TILE):
                top, left = packed(i * feats + j, deep, hid)
                target[low + top : low + top + TILE, left : left + hid] = value[j : j + TILE]
    for copy in copies[5:]:
        copy.wait()


def inner_kernel(dims, head, table, rates, *refs):
    nseg, nseq, hpd, feats, hid, tokens, chunk = dims
    chips = nseg // CORES
    li, refs = refs[:nseg], refs[nseg:]
    wt, refs = refs[:nseq], refs[nseq:]
    pack, refs = refs[0], refs[1:]
    gp, refs = refs[:nseq], refs[nseq:]
    gq, sent, kept, qkv, wts, cts, ht, rt, g1, g2p, gu, gab, res, wide = refs
    rows = 3 * feats
    own = hpd * feats
    first = head * feats
    for back in range(nseq):
        at = pl.multiple_of(table[nseg + back] * chunk, chunk)
        for p in range(3):
            block = wt[back][p * own + first : p * own + first + feats]
            wide[p * feats : (p + 1) * feats, pl.ds(at, chunk)] = block

    deep = pack.shape[0]

    for slot in range(nseg):
        dx, dc = slot // CORES, slot % CORES
        source, low = (pack, 0) if slot == 0 else (li[slot], tokens + (deep * dc if dx else 0))
        for i, piece in enumerate((wts.at[slot, 0], wts.at[slot, 1], cts.at[slot])):
            for j in range(0, feats, TILE):
                top, left = packed((i * hpd + head) * feats + j, deep, hid)
                value = source[low + top : low + top + TILE, left : left + hid]
                piece[j : j + TILE] = value
        total = dot(wide[...], li[slot][:tokens], 1, 1)
        qkv[slot] = total.astype(BF).reshape(3, feats, tokens)
    rate = rates[table[nseg + nseq] + head] * (1.0 / MB)

    def local(slot):
        a_b, b_b = wts[slot, 0], wts[slot, 1]
        q_b, k_b, v_b = qkv[slot, 0], qkv[slot, 1], qkv[slot, 2]
        c_b = cts[slot]
        u = dot(a_b, k_b, 0, 0)
        yield
        square, tanh, half, sech, slope = gelu_parts(u)
        h_b = (u * half).astype(BF)
        yield
        slope1 = half + 0.5 * u * sech * slope
        second = sech * (GELU_A + (6.0 * GELU_A * GELU_B) * square - u * tanh * slope * slope)
        ht[slot] = h_b
        g1[slot] = slope1
        resid = k_b.astype(F32) - v_b.astype(F32) + dot(b_b, h_b, 1, 0)
        r_b = resid.astype(BF)
        yield
        rt[slot] = r_b
        p = dot(b_b, r_b, 0, 0)
        g2p[slot] = second * p
        gu_b = (slope1 * p).astype(BF)
        gu[slot] = gu_b
        yield
        new_a = (a_b.astype(F32) - rate * dot(k_b, gu_b, 1, 1)).astype(BF)
        new_b = (b_b.astype(F32) - rate * dot(r_b, h_b, 1, 1)).astype(BF)
        uq = dot(new_a, q_b, 0, 0)
        yield
        square, tanh, half, sech, slope = gelu_parts(uq)
        hq_b = (uq * half).astype(BF)
        guq_b = ((half + 0.5 * uq * sech * slope) * dot(new_b, c_b, 0, 0)).astype(BF)
        gab[slot, 0] = dot(q_b, guq_b, 1, 1)
        yield
        gab[slot, 1] = dot(c_b, hq_b, 1, 1)
        gq[slot, 0] = (c_b.astype(F32) + dot(new_a, guq_b, 1, 0)).astype(BF)

    for low in range(0, nseg, GROUP):
        for _ in zip_longest(*[local(slot) for slot in range(low, min(low + GROUP, nseg))]):
            pass

    def end(slot, k_b, a_b, ta_b, gu_b, dr, dgu_b, c_a, c_b):
        left = jnp.concatenate([a_b, ta_b], 1)
        gk = dr + dot(left, jnp.concatenate([dgu_b, gu_b], 0), 1, 0)
        gq[slot, 1] = (-rate * gk).astype(BF)
        gq[slot, 2] = (rate * dr).astype(BF)
        res[slot, 0] = c_a.astype(BF)
        res[slot, 1] = c_b.astype(BF)

    c_a = c_b = jnp.zeros((feats, hid), F32)
    late = None
    for turn in range(nseg):
        slot = table[nseg - 1 - turn]
        t_a = c_a + gab[slot, 0]
        t_b = c_b + gab[slot, 1]
        a_b, b_b = wts[slot, 0], wts[slot, 1]
        k_b = qkv[slot, 1]
        h_b, r_b, gu_b = ht[slot], rt[slot], gu[slot]
        ta_b, tb_b = t_a.astype(BF), t_b.astype(BF)
        du = dot(ta_b, k_b, 0, 0)
        dr_h, dp_r = dot(tb_b, h_b, 1, 0), dot(tb_b, r_b, 0, 0)
        if late is not None:
            end(*late)
        dh_b = (g1[slot] * du).astype(BF)
        dr = dot(b_b, dh_b, 1, 0) + dr_h
        dr_b = dr.astype(BF)
        dp = dot(b_b, dr_b, 0, 0) + dp_r
        c_b = t_b - rate * (dot(dr_b, h_b, 1, 1) + dot(r_b, dh_b, 1, 1))
        dgu_b = (g2p[slot] * du + g1[slot] * dp).astype(BF)
        c_a = t_a - rate * dot(k_b, dgu_b, 1, 1)
        late = (slot, k_b, a_b, ta_b, gu_b, dr, dgu_b, c_a, c_b)
    end(*late)

    for slot in range(nseg):
        dx, dc = slot // CORES, slot % CORES
        if dx == 0:
            kept[dc] = res[slot]
        else:
            sent[dx - 1, dc * rows : (dc + 1) * rows] = gq[slot].reshape(rows, tokens)
            at = CORES * rows + dc * 2 * feats
            sent[dx - 1, at : at + 2 * feats] = res[slot].reshape(2 * feats, hid)
    for dz in range(nseq):
        at = pl.multiple_of(table[nseg + (nseq - dz) % nseq] * chunk, chunk)
        total = jnp.zeros((rows, chunk), F32)
        for slot in range(nseg):
            part = li[slot][:tokens, pl.ds(at, chunk)]
            total += dot(gq[slot].reshape(rows, tokens), part, 1, 0)
        gp[dz][...] = total.astype(gp[dz].dtype)


def input_kernel(dims, table, *refs):
    nseg, nseq, hpd, feats, hid, tokens, chunk = dims
    chips = nseg // CORES
    rows = 3 * feats
    gq, refs = refs[:hpd], refs[hpd:]
    kept, refs = refs[:hpd], refs[hpd:]
    sent, refs = refs[: hpd * (chips - 1)], refs[hpd * (chips - 1) :]
    wt, refs = refs[:nseq], refs[nseq:]
    away, (home, aside, leave) = refs[: chips - 1], refs[chips - 1 :]
    for dc in range(CORES):
        left = [gq[h][dc, p] for p in range(3) for h in range(hpd)]
        for dx in range(chips - 1):
            for p in range(3):
                at = dc * rows + p * feats
                left += [sent[h * (chips - 1) + dx][at : at + feats] for h in range(hpd)]
        left = jnp.concatenate(left)
        for back in range(nseq):
            at = pl.multiple_of(table[nseg + back] * chunk, chunk)
            right = jnp.concatenate([wt[back][...]] + [value[back] for value in away])
            value = dot(left, right, 0, 0)
            out = (home, aside)[dc]
            out[:, pl.ds(at, chunk)] = value.astype(out.dtype)
    at = CORES * rows + 2 * feats
    for head in range(hpd):
        leave[head * chips] = kept[head][1].reshape(2 * feats, hid)
        for dx in range(1, chips):
            leave[head * chips + dx] = sent[head * (chips - 1) + dx - 1][at : at + 2 * feats]


def sum_kernel(*refs):
    total = refs[0][...]
    for ref in refs[1:-1]:
        total += ref[...].astype(F32)
    total = total.T.astype(BF)
    half = total.shape[0] // 2
    refs[-1][...] = jnp.concatenate([total[:half], total[half:]], 1)


def join_kernel(dims, table, *refs):
    nseg, nseq, hpd, feats, hid, tokens, chunk = dims
    chips = nseg // CORES
    far, near, out, whole, sem = refs[: hpd * chips], *refs[hpd * chips :]
    wide = CORES * hpd * feats
    half = chunk // 2
    me = table[nseg + nseq + 1]
    chip = me // CORES
    even = me % CORES == 0
    copies = []
    for dx in range(chips):
        source = (chip - dx + chips) % chips
        for side in range(2):
            cut = slice(side * 3 * feats, (side + 1) * 3 * feats)
            mine = [far[h * chips + dx][:, cut].astype(F32) for h in range(hpd)]
            other = [near[h * chips + dx, :, cut].astype(F32) for h in range(hpd)]
            mine, other = (
                [jnp.where(even, a, b) for a, b in zip(mine, other)],
                [jnp.where(even, b, a) for a, b in zip(mine, other)],
            )
            for part in range(3):
                cut = slice(part * feats, (part + 1) * feats)
                whole[dx, side, part] = jnp.concatenate([v[:, cut] for v in mine + other], 1)
                at = pl.multiple_of((part * nseg * hpd * feats) + source * wide, wide)
                copy = pltpu.make_async_copy(
                    whole.at[dx, side, part],
                    out.at[pl.ds(side * half, half), pl.ds(at, wide)],
                    sem.at[len(copies)],
                )
                copy.start()
                copies.append(copy)
    for copy in copies:
        copy.wait()


def weights_kernel(dims, table, *refs):
    nseg, nseq, hpd, feats, hid, tokens, chunk = dims
    chips = nseg // CORES
    kept, refs = refs[:hpd], refs[hpd:]
    sent, refs = refs[: hpd * (chips - 1)], refs[hpd * (chips - 1) :]
    got, out = refs
    at = CORES * 3 * feats
    for head in range(hpd):
        for slot in range(nseg):
            dx, dc = slot // CORES, slot % CORES
            if dc == 1:
                piece = got[head * chips + dx]
            elif dx == 0:
                piece = kept[head][0].reshape(2 * feats, hid)
            else:
                piece = sent[head * (chips - 1) + dx - 1][at : at + 2 * feats]
            index = table[nseg + nseq + 2 + slot] * hpd + head
            out[0, index] = piece[:feats].astype(F32)
            out[1, index] = piece[feats:].astype(F32)


def per_device(layer_input, out_cot, w_proj, inner_start, rates):
    rows = layer_input[0]
    tokens, width = rows.shape
    heads = rates.shape[0]
    feats, hid = inner_start.shape[4:]
    nseg, nseq = lax.axis_size("seg"), lax.axis_size("seq")
    chips = nseg // CORES
    hpd = heads // nseg
    own = hpd * feats
    chunk = width // nseq
    me, place = lax.axis_index("seg"), lax.axis_index("seq")
    chip, core = me // CORES, me % CORES
    barrier = lax.optimization_barrier

    def to_chip(value, dx):
        pairs = [(i, (i + dx * CORES) % nseg) for i in range(nseg)]
        return lax.ppermute(value, "seg", pairs)

    def to_core(value):
        return lax.ppermute(value, "seg", [(i, i ^ 1) for i in range(nseg)])

    def to_seq(value, dz):
        return lax.ppermute(value, "seq", [(i, (i + dz) % nseq) for i in range(nseq)])

    def kernel(body, name, limit, cost, outs, scratch, *operands):
        smem = pl.BlockSpec(memory_space=pltpu.SMEM)
        vmem = pl.BlockSpec(memory_space=pltpu.VMEM)
        return pl.pallas_call(
            body,
            in_specs=[smem if o.ndim == 1 else vmem for o in operands],
            out_specs=[vmem] * len(outs),
            out_shape=[jax.ShapeDtypeStruct(*o) for o in outs],
            scratch_shapes=[pltpu.VMEM(*o) for o in scratch],
            compiler_params=pltpu.CompilerParams(vmem_limit_bytes=limit * MIB),
            cost_estimate=pl.CostEstimate(flops=0, bytes_accessed=cost, transcendentals=0),
            name=name,
        )(*operands)

    def summed(pieces):
        return kernel(sum_kernel, "sum", 12, 0, [((chunk // 2, 6 * feats), BF)], [], *pieces)[0]

    crossed = chips == 2 and lax.axis_size("groups") == 2
    shift = lax.axis_index("groups") if crossed else 0

    segs = jnp.arange(nseg, dtype=jnp.int32)
    slot_of = ((chip - segs // CORES) % chips) * CORES + (core + segs) % CORES
    back = (place - jnp.arange(nseq, dtype=jnp.int32)) % nseq
    dest = ((chip + shift + segs // CORES) % chips) * CORES + (core + segs) % CORES
    table = jnp.concatenate([slot_of, back, jnp.stack([dest[0] * hpd, dest[0]]), dest])
    table = table.astype(jnp.int32)
    dims = (nseg, nseq, hpd, feats, hid, tokens, chunk)

    wide = max(own, 128)
    deep = -(-3 * own * hid // (width * TILE)) * TILE
    hbm = pl.BlockSpec(memory_space=pltpu.HBM)
    vmem = pl.BlockSpec(memory_space=pltpu.VMEM)
    outs = [((3 * own, chunk), BF), ((deep, width), BF), ((tokens + deep, width), BF)]
    outs += [((tokens + CORES * deep, width), BF)] * (chips - 1)
    operands = (rows, w_proj, out_cot[0], inner_start[0, 0])
    mine, pack, *ships = pl.pallas_call(
        functools.partial(prep_kernel, dims),
        in_specs=[pl.BlockSpec(memory_space=pltpu.SMEM)] + [hbm] * 4,
        out_specs=[vmem] * len(outs),
        out_shape=[jax.ShapeDtypeStruct(*o) for o in outs],
        scratch_shapes=[
            pltpu.VMEM((3, chunk, wide), BF),
            pltpu.VMEM((tokens, heads * feats), BF),
            pltpu.VMEM((2, heads, feats, hid), F32),
            pltpu.VMEM((heads * feats, tokens), BF),
            pltpu.SemaphoreType.DMA((5 + chips,)),
        ],
        compiler_params=pltpu.CompilerParams(vmem_limit_bytes=16 * MIB),
        cost_estimate=pl.CostEstimate(flops=0, bytes_accessed=0, transcendentals=0),
        name="prep",
    )(table, *[pltpu.with_memory_space_constraint(o, pltpu.HBM) for o in operands])
    near = to_core(ships[0])
    far = [to_chip(ships[dx], dx) for dx in range(1, chips)]
    wt = [mine] + [to_seq(mine, dz) for dz in range(1, nseq)]
    far, near, wt = barrier((far, near, wt))
    li = [rows, near]
    for value in far:
        li += [value, to_core(value)]

    def to_others(value):
        if crossed:
            return [lax.ppermute(value, "groups", [(0, 1), (1, 0)])]
        return [to_chip(value, -dx) for dx in range(1, chips)]

    def inner(head):
        return kernel(
            functools.partial(inner_kernel, dims, head),
            "inner",
            36,
            0,
            [((3 * feats, chunk), BF if dz else F32) for dz in range(nseq)]
            + [((nseg, 3, feats, tokens), BF)]
            + [((chips - 1, 10 * feats, tokens), BF)]
            + [((CORES, 2, feats, hid), BF)],
            [
                ((nseg, 3, feats, tokens), BF),
                ((nseg, 2, feats, hid), BF),
                ((nseg, feats, tokens), BF),
                ((nseg, hid, tokens), BF),
                ((nseg, feats, tokens), BF),
                ((nseg, hid, tokens), F32),
                ((nseg, hid, tokens), F32),
                ((nseg, hid, tokens), BF),
                ((nseg, 2, feats, hid), F32),
                ((nseg, 2, feats, hid), BF),
                ((3 * feats, width), BF),
            ],
            table,
            rates,
            *li,
            *wt,
            pack,
        )

    away = to_others(jnp.stack(wt))
    grads, kept, sent, projs, pieces = [], [], [], [], None
    for head in range(hpd):
        outs = inner(head)
        gp, gq, send, keep = outs[:nseq], outs[nseq], outs[nseq + 1], outs[nseq + 2]
        if pieces is not None:
            gp, send, pieces[1], sent = barrier((gp, send, pieces[1], sent))
        if pieces is not None:
            total = summed(pieces)
            projs += [total] + [to_chip(total, dx) for dx in range(1, chips)]
        pieces = [gp[0]] + [to_seq(gp[dz], dz) for dz in range(1, nseq)]
        sent += [to_chip(send[dx - 1], -dx) for dx in range(1, chips)]
        grads.append(gq)
        kept.append(keep)

    home, aside, leave = kernel(
        functools.partial(input_kernel, dims),
        "input",
        24,
        10 * MIB,
        [((tokens, width), F32), ((tokens, width), BF)]
        + [((hpd * chips, 2 * feats, hid), BF)],
        [],
        table,
        *grads,
        *kept,
        *sent,
        *wt,
        *away,
    )
    pieces, projs, home, aside, leave = barrier((pieces, projs, home, aside, leave))

    total = summed(pieces)
    projs += [total] + [to_chip(total, dx) for dx in range(1, chips)]
    aside, leave = to_core(aside), to_core(leave)
    grad_input = (home + aside.astype(F32)).astype(BF)
    (grad_inner,) = kernel(
        functools.partial(weights_kernel, dims),
        "weights",
        8,
        10 * MIB,
        [((2, heads, feats, hid), F32)],
        [],
        table,
        *kept,
        *sent,
        leave,
    )
    projs, grad_input, grad_inner = barrier((projs, grad_input, grad_inner))
    near = to_core(jnp.stack(projs))
    grad_proj = pl.pallas_call(
        functools.partial(join_kernel, dims),
        in_specs=[pl.BlockSpec(memory_space=pltpu.SMEM)] + [vmem] * (hpd * chips + 1),
        out_specs=hbm,
        out_shape=jax.ShapeDtypeStruct((chunk, 3 * heads * feats), F32),
        scratch_shapes=[
            pltpu.VMEM((chips, 2, 3, chunk // 2, CORES * own), F32),
            pltpu.SemaphoreType.DMA((6 * chips,)),
        ],
        compiler_params=pltpu.CompilerParams(vmem_limit_bytes=16 * MIB),
        cost_estimate=pl.CostEstimate(flops=0, bytes_accessed=0, transcendentals=0),
        name="join",
    )(table, *projs, near)
    return (grad_input[None], grad_proj, grad_inner[None, None])


def solution(mesh):
    placed = (
        P(("groups", "seq"), "seg", None),
        P(("groups", "seq"), "seg", None),
        P("seq", None),
        P(("groups", "seq"), "seg", None, None, None, None),
        P(),
    )
    return jax.shard_map(
        per_device,
        mesh=mesh,
        in_specs=placed,
        out_specs=(
            P(("groups", "seq"), "seg", None),
            P(("groups", "seq"), None),
            P(("groups", "seq"), "seg", None, None, None, None),
        ),
        check_vma=False,
    )
```

```python
import functools
from itertools import zip_longest

import jax
import jax.numpy as jnp
from jax import lax
from jax.experimental import pallas as pl
from jax.experimental.pallas import tpu as pltpu
from jax.sharding import PartitionSpec as P

MB = 256
BF = jnp.bfloat16
F32 = jnp.float32
CORES = 2
GELU_A = 0.7978845608028654
GELU_B = 0.044715
MIB = 1024 * 1024
TILE = 16
GROUP = 4


def dot(a, b, ca, cb):
    return lax.dot_general(a, b, (((ca,), (cb,)), ((), ())), preferred_element_type=F32)


def gelu_parts(u):
    square = u * u
    tanh = jnp.tanh(u * (GELU_A + (GELU_A * GELU_B) * square))
    half = 0.5 * (1.0 + tanh)
    sech = 1.0 - tanh * tanh
    slope = GELU_A + (3.0 * GELU_A * GELU_B) * square
    return square, tanh, half, sech, slope


def packed(row, deep, hid):
    return row % deep, row // deep * hid


def prep_kernel(dims, table, rows, w, cots, start, mine, pack, *refs):
    nseg, nseq, hpd, feats, hid, tokens, chunk = dims
    ships, refs = refs[: nseg // CORES], refs[nseg // CORES :]
    cut, held, weights, turned, sem = refs
    own = hpd * feats
    wide = cut.shape[2]
    deep = pack.shape[0]
    me = table[nseg + nseq + 1]
    base = me * own // wide * wide
    copies = []
    for part in range(3):
        at = pl.multiple_of(part * nseg * own + base, wide)
        copies.append(pltpu.make_async_copy(w.at[:, pl.ds(at, wide)], cut.at[part], sem.at[part]))
    copies.append(pltpu.make_async_copy(cots, held, sem.at[3]))
    copies.append(pltpu.make_async_copy(start, weights, sem.at[4]))
    for i, ship in enumerate(ships):
        copies.append(pltpu.make_async_copy(rows, ship.at[pl.ds(0, tokens)], sem.at[5 + i]))
    for copy in copies:
        copy.start()
    for part in range(3):
        copies[part].wait()
        block = cut[part].T
        even = block[:own]
        for i in range(1, wide // own):
            even = jnp.where(me * own % wide == i * own, block[i * own : (i + 1) * own], even)
        mine[part * own : (part + 1) * own] = even
    copies[3].wait()
    turned[...] = held[...].T
    copies[4].wait()
    for slot in range(nseg):
        dest = table[nseg + nseq + 2 + slot]
        dx, dc = slot // CORES, slot % CORES
        target, low = (pack, 0) if slot == 0 else (ships[dx], tokens + (deep * dc if dx else 0))
        for i in range(3 * hpd):
            kind, head = i // hpd, i % hpd
            if kind < 2:
                value = weights[kind, dest * hpd + head].astype(BF)
            else:
                value = turned[pl.ds(pl.multiple_of((dest * hpd + head) * feats, feats), feats)]
            for j in range(0, feats, TILE):
                top, left = packed(i * feats + j, deep, hid)
                target[low + top : low + top + TILE, left : left + hid] = value[j : j + TILE]
    for copy in copies[5:]:
        copy.wait()


def inner_kernel(dims, head, table, rates, *refs):
    nseg, nseq, hpd, feats, hid, tokens, chunk = dims
    chips = nseg // CORES
    li, refs = refs[:nseg], refs[nseg:]
    wt, refs = refs[:nseq], refs[nseq:]
    pack, refs = refs[0], refs[1:]
    gp, refs = refs[:nseq], refs[nseq:]
    gq, sent, kept, qkv, wts, cts, ht, rt, g1, g2p, gu, gab, res, wide = refs
    rows = 3 * feats
    own = hpd * feats
    first = head * feats
    for back in range(nseq):
        at = pl.multiple_of(table[nseg + back] * chunk, chunk)
        for p in range(3):
            block = wt[back][p * own + first : p * own + first + feats]
            wide[p * feats : (p + 1) * feats, pl.ds(at, chunk)] = block

    deep = pack.shape[0]

    for slot in range(nseg):
        dx, dc = slot // CORES, slot % CORES
        source, low = (pack, 0) if slot == 0 else (li[slot], tokens + (deep * dc if dx else 0))
        for i, piece in enumerate((wts.at[slot, 0], wts.at[slot, 1], cts.at[slot])):
            for j in range(0, feats, TILE):
                top, left = packed((i * hpd + head) * feats + j, deep, hid)
                value = source[low + top : low + top + TILE, left : left + hid]
                piece[j : j + TILE] = value
        total = dot(wide[...], li[slot][:tokens], 1, 1)
        qkv[slot] = total.astype(BF).reshape(3, feats, tokens)
    rate = rates[table[nseg + nseq] + head] * (1.0 / MB)

    def local(slot):
        a_b, b_b = wts[slot, 0], wts[slot, 1]
        q_b, k_b, v_b = qkv[slot, 0], qkv[slot, 1], qkv[slot, 2]
        c_b = cts[slot]
        u = dot(a_b, k_b, 0, 0)
        yield
        square, tanh, half, sech, slope = gelu_parts(u)
        h_b = (u * half).astype(BF)
        yield
        slope1 = half + 0.5 * u * sech * slope
        second = sech * (GELU_A + (6.0 * GELU_A * GELU_B) * square - u * tanh * slope * slope)
        ht[slot] = h_b
        g1[slot] = slope1
        resid = k_b.astype(F32) - v_b.astype(F32) + dot(b_b, h_b, 1, 0)
        r_b = resid.astype(BF)
        yield
        rt[slot] = r_b
        p = dot(b_b, r_b, 0, 0)
        g2p[slot] = second * p
        gu_b = (slope1 * p).astype(BF)
        gu[slot] = gu_b
        yield
        new_a = (a_b.astype(F32) - rate * dot(k_b, gu_b, 1, 1)).astype(BF)
        new_b = (b_b.astype(F32) - rate * dot(r_b, h_b, 1, 1)).astype(BF)
        uq = dot(new_a, q_b, 0, 0)
        yield
        square, tanh, half, sech, slope = gelu_parts(uq)
        hq_b = (uq * half).astype(BF)
        guq_b = ((half + 0.5 * uq * sech * slope) * dot(new_b, c_b, 0, 0)).astype(BF)
        gab[slot, 0] = dot(q_b, guq_b, 1, 1)
        yield
        gab[slot, 1] = dot(c_b, hq_b, 1, 1)
        gq[slot, 0] = (c_b.astype(F32) + dot(new_a, guq_b, 1, 0)).astype(BF)

    for low in range(0, nseg, GROUP):
        for _ in zip_longest(*[local(slot) for slot in range(low, min(low + GROUP, nseg))]):
            pass

    def end(slot, k_b, a_b, ta_b, gu_b, dr, dgu_b, c_a, c_b):
        left = jnp.concatenate([a_b, ta_b], 1)
        gk = dr + dot(left, jnp.concatenate([dgu_b, gu_b], 0), 1, 0)
        gq[slot, 1] = (-rate * gk).astype(BF)
        gq[slot, 2] = (rate * dr).astype(BF)
        res[slot, 0] = c_a.astype(BF)
        res[slot, 1] = c_b.astype(BF)

    c_a = c_b = jnp.zeros((feats, hid), F32)
    late = None
    for turn in range(nseg):
        slot = table[nseg - 1 - turn]
        t_a = c_a + gab[slot, 0]
        t_b = c_b + gab[slot, 1]
        a_b, b_b = wts[slot, 0], wts[slot, 1]
        k_b = qkv[slot, 1]
        h_b, r_b, gu_b = ht[slot], rt[slot], gu[slot]
        ta_b, tb_b = t_a.astype(BF), t_b.astype(BF)
        du = dot(ta_b, k_b, 0, 0)
        dr_h, dp_r = dot(tb_b, h_b, 1, 0), dot(tb_b, r_b, 0, 0)
        if late is not None:
            end(*late)
        dh_b = (g1[slot] * du).astype(BF)
        dr = dot(b_b, dh_b, 1, 0) + dr_h
        dr_b = dr.astype(BF)
        dp = dot(b_b, dr_b, 0, 0) + dp_r
        c_b = t_b - rate * (dot(dr_b, h_b, 1, 1) + dot(r_b, dh_b, 1, 1))
        dgu_b = (g2p[slot] * du + g1[slot] * dp).astype(BF)
        c_a = t_a - rate * dot(k_b, dgu_b, 1, 1)
        late = (slot, k_b, a_b, ta_b, gu_b, dr, dgu_b, c_a, c_b)
    end(*late)

    for slot in range(nseg):
        dx, dc = slot // CORES, slot % CORES
        if dx == 0:
            kept[dc] = res[slot]
        else:
            sent[dx - 1, dc * rows : (dc + 1) * rows] = gq[slot].reshape(rows, tokens)
            at = CORES * rows + dc * 2 * feats
            sent[dx - 1, at : at + 2 * feats] = res[slot].reshape(2 * feats, hid)
    for dz in range(nseq):
        at = pl.multiple_of(table[nseg + (nseq - dz) % nseq] * chunk, chunk)
        total = jnp.zeros((rows, chunk), F32)
        for slot in range(nseg):
            part = li[slot][:tokens, pl.ds(at, chunk)]
            total += dot(gq[slot].reshape(rows, tokens), part, 1, 0)
        gp[dz][...] = total.astype(gp[dz].dtype)


def input_kernel(dims, table, *refs):
    nseg, nseq, hpd, feats, hid, tokens, chunk = dims
    chips = nseg // CORES
    rows = 3 * feats
    gq, refs = refs[:hpd], refs[hpd:]
    kept, refs = refs[:hpd], refs[hpd:]
    sent, refs = refs[: hpd * (chips - 1)], refs[hpd * (chips - 1) :]
    wt, refs = refs[:nseq], refs[nseq:]
    away, (home, aside, leave) = refs[: chips - 1], refs[chips - 1 :]
    for dc in range(CORES):
        left = [gq[h][dc, p] for p in range(3) for h in range(hpd)]
        for dx in range(chips - 1):
            for p in range(3):
                at = dc * rows + p * feats
                left += [sent[h * (chips - 1) + dx][at : at + feats] for h in range(hpd)]
        left = jnp.concatenate(left)
        for back in range(nseq):
            at = pl.multiple_of(table[nseg + back] * chunk, chunk)
            right = jnp.concatenate([wt[back][...]] + [value[back] for value in away])
            value = dot(left, right, 0, 0)
            out = (home, aside)[dc]
            out[:, pl.ds(at, chunk)] = value.astype(out.dtype)
    at = CORES * rows + 2 * feats
    for head in range(hpd):
        leave[head * chips] = kept[head][1].reshape(2 * feats, hid)
        for dx in range(1, chips):
            leave[head * chips + dx] = sent[head * (chips - 1) + dx - 1][at : at + 2 * feats]


def sum_kernel(*refs):
    total = refs[0][...]
    for ref in refs[1:-1]:
        total += ref[...].astype(F32)
    total = total.T.astype(BF)
    half = total.shape[0] // 2
    refs[-1][...] = jnp.concatenate([total[:half], total[half:]], 1)


def join_kernel(dims, table, *refs):
    nseg, nseq, hpd, feats, hid, tokens, chunk = dims
    chips = nseg // CORES
    far, near, out, whole, sem = refs[: hpd * chips], *refs[hpd * chips :]
    wide = CORES * hpd * feats
    half = chunk // 2
    me = table[nseg + nseq + 1]
    chip = me // CORES
    even = me % CORES == 0
    copies = []
    for dx in range(chips):
        source = (chip - dx + chips) % chips
        for side in range(2):
            cut = slice(side * 3 * feats, (side + 1) * 3 * feats)
            mine = [far[h * chips + dx][:, cut].astype(F32) for h in range(hpd)]
            other = [near[h * chips + dx, :, cut].astype(F32) for h in range(hpd)]
            mine, other = (
                [jnp.where(even, a, b) for a, b in zip(mine, other)],
                [jnp.where(even, b, a) for a, b in zip(mine, other)],
            )
            for part in range(3):
                cut = slice(part * feats, (part + 1) * feats)
                whole[dx, side, part] = jnp.concatenate([v[:, cut] for v in mine + other], 1)
                at = pl.multiple_of((part * nseg * hpd * feats) + source * wide, wide)
                copy = pltpu.make_async_copy(
                    whole.at[dx, side, part],
                    out.at[pl.ds(side * half, half), pl.ds(at, wide)],
                    sem.at[len(copies)],
                )
                copy.start()
                copies.append(copy)
    for copy in copies:
        copy.wait()


def weights_kernel(dims, table, *refs):
    nseg, nseq, hpd, feats, hid, tokens, chunk = dims
    chips = nseg // CORES
    kept, refs = refs[:hpd], refs[hpd:]
    sent, refs = refs[: hpd * (chips - 1)], refs[hpd * (chips - 1) :]
    got, out = refs
    at = CORES * 3 * feats
    for head in range(hpd):
        for slot in range(nseg):
            dx, dc = slot // CORES, slot % CORES
            if dc == 1:
                piece = got[head * chips + dx]
            elif dx == 0:
                piece = kept[head][0].reshape(2 * feats, hid)
            else:
                piece = sent[head * (chips - 1) + dx - 1][at : at + 2 * feats]
            index = table[nseg + nseq + 2 + slot] * hpd + head
            out[0, index] = piece[:feats].astype(F32)
            out[1, index] = piece[feats:].astype(F32)


def per_device(layer_input, out_cot, w_proj, inner_start, rates):
    rows = layer_input[0]
    tokens, width = rows.shape
    heads = rates.shape[0]
    feats, hid = inner_start.shape[4:]
    nseg, nseq = lax.axis_size("seg"), lax.axis_size("seq")
    chips = nseg // CORES
    hpd = heads // nseg
    own = hpd * feats
    chunk = width // nseq
    me, place = lax.axis_index("seg"), lax.axis_index("seq")
    chip, core = me // CORES, me % CORES
    barrier = lax.optimization_barrier

    def to_chip(value, dx):
        pairs = [(i, (i + dx * CORES) % nseg) for i in range(nseg)]
        return lax.ppermute(value, "seg", pairs)

    def to_core(value):
        return lax.ppermute(value, "seg", [(i, i ^ 1) for i in range(nseg)])

    def to_seq(value, dz):
        return lax.ppermute(value, "seq", [(i, (i + dz) % nseq) for i in range(nseq)])

    def kernel(body, name, limit, cost, outs, scratch, *operands):
        smem = pl.BlockSpec(memory_space=pltpu.SMEM)
        vmem = pl.BlockSpec(memory_space=pltpu.VMEM)
        return pl.pallas_call(
            body,
            in_specs=[smem if o.ndim == 1 else vmem for o in operands],
            out_specs=[vmem] * len(outs),
            out_shape=[jax.ShapeDtypeStruct(*o) for o in outs],
            scratch_shapes=[pltpu.VMEM(*o) for o in scratch],
            compiler_params=pltpu.CompilerParams(vmem_limit_bytes=limit * MIB),
            cost_estimate=pl.CostEstimate(flops=0, bytes_accessed=cost, transcendentals=0),
            name=name,
        )(*operands)

    def summed(pieces):
        return kernel(sum_kernel, "sum", 12, 0, [((chunk // 2, 6 * feats), BF)], [], *pieces)[0]

    crossed = chips == 2 and lax.axis_size("groups") == 2
    shift = lax.axis_index("groups") if crossed else 0

    segs = jnp.arange(nseg, dtype=jnp.int32)
    slot_of = ((chip - segs // CORES) % chips) * CORES + (core + segs) % CORES
    back = (place - jnp.arange(nseq, dtype=jnp.int32)) % nseq
    dest = ((chip + shift + segs // CORES) % chips) * CORES + (core + segs) % CORES
    table = jnp.concatenate([slot_of, back, jnp.stack([dest[0] * hpd, dest[0]]), dest])
    table = table.astype(jnp.int32)
    dims = (nseg, nseq, hpd, feats, hid, tokens, chunk)

    wide = max(own, 128)
    deep = -(-3 * own * hid // (width * TILE)) * TILE
    hbm = pl.BlockSpec(memory_space=pltpu.HBM)
    vmem = pl.BlockSpec(memory_space=pltpu.VMEM)
    outs = [((3 * own, chunk), BF), ((deep, width), BF), ((tokens + deep, width), BF)]
    outs += [((tokens + CORES * deep, width), BF)] * (chips - 1)
    operands = (rows, w_proj, out_cot[0], inner_start[0, 0])
    mine, pack, *ships = pl.pallas_call(
        functools.partial(prep_kernel, dims),
        in_specs=[pl.BlockSpec(memory_space=pltpu.SMEM)] + [hbm] * 4,
        out_specs=[vmem] * len(outs),
        out_shape=[jax.ShapeDtypeStruct(*o) for o in outs],
        scratch_shapes=[
            pltpu.VMEM((3, chunk, wide), BF),
            pltpu.VMEM((tokens, heads * feats), BF),
            pltpu.VMEM((2, heads, feats, hid), F32),
            pltpu.VMEM((heads * feats, tokens), BF),
            pltpu.SemaphoreType.DMA((5 + chips,)),
        ],
        compiler_params=pltpu.CompilerParams(vmem_limit_bytes=16 * MIB),
        cost_estimate=pl.CostEstimate(flops=0, bytes_accessed=0, transcendentals=0),
        name="prep",
    )(table, *[pltpu.with_memory_space_constraint(o, pltpu.HBM) for o in operands])
    near = to_core(ships[0])
    far = [to_chip(ships[dx], dx) for dx in range(1, chips)]
    wt = [mine] + [to_seq(mine, dz) for dz in range(1, nseq)]
    far, near, wt = barrier((far, near, wt))
    li = [rows, near]
    for value in far:
        li += [value, to_core(value)]

    def to_others(value):
        if crossed:
            return [lax.ppermute(value, "groups", [(0, 1), (1, 0)])]
        return [to_chip(value, -dx) for dx in range(1, chips)]

    def inner(head):
        return kernel(
            functools.partial(inner_kernel, dims, head),
            "inner",
            36,
            0,
            [((3 * feats, chunk), BF if dz else F32) for dz in range(nseq)]
            + [((nseg, 3, feats, tokens), BF)]
            + [((chips - 1, 10 * feats, tokens), BF)]
            + [((CORES, 2, feats, hid), BF)],
            [
                ((nseg, 3, feats, tokens), BF),
                ((nseg, 2, feats, hid), BF),
                ((nseg, feats, tokens), BF),
                ((nseg, hid, tokens), BF),
                ((nseg, feats, tokens), BF),
                ((nseg, hid, tokens), F32),
                ((nseg, hid, tokens), F32),
                ((nseg, hid, tokens), BF),
                ((nseg, 2, feats, hid), F32),
                ((nseg, 2, feats, hid), BF),
                ((3 * feats, width), BF),
            ],
            table,
            rates,
            *li,
            *wt,
            pack,
        )

    away = to_others(jnp.stack(wt))
    grads, kept, sent, projs, pieces = [], [], [], [], None
    for head in range(hpd):
        outs = inner(head)
        gp, gq, send, keep = outs[:nseq], outs[nseq], outs[nseq + 1], outs[nseq + 2]
        if pieces is not None:
            gp, send, pieces[nseq // 2], sent = barrier((gp, send, pieces[nseq // 2], sent))
        if pieces is not None:
            total = summed(pieces)
            projs += [total] + [to_chip(total, dx) for dx in range(1, chips)]
        pieces = [gp[0]] + [to_seq(gp[dz], dz) for dz in range(1, nseq)]
        sent += [to_chip(send[dx - 1], -dx) for dx in range(1, chips)]
        grads.append(gq)
        kept.append(keep)

    home, aside, leave = kernel(
        functools.partial(input_kernel, dims),
        "input",
        24,
        10 * MIB,
        [((tokens, width), F32), ((tokens, width), BF)]
        + [((hpd * chips, 2 * feats, hid), BF)],
        [],
        table,
        *grads,
        *kept,
        *sent,
        *wt,
        *away,
    )
    pieces, projs, home, aside, leave = barrier((pieces, projs, home, aside, leave))

    total = summed(pieces)
    projs += [total] + [to_chip(total, dx) for dx in range(1, chips)]
    aside, leave = to_core(aside), to_core(leave)
    grad_input = (home + aside.astype(F32)).astype(BF)
    (grad_inner,) = kernel(
        functools.partial(weights_kernel, dims),
        "weights",
        8,
        10 * MIB,
        [((2, heads, feats, hid), F32)],
        [],
        table,
        *kept,
        *sent,
        leave,
    )
    projs, grad_input, grad_inner = barrier((projs, grad_input, grad_inner))
    near = to_core(jnp.stack(projs))
    grad_proj = pl.pallas_call(
        functools.partial(join_kernel, dims),
        in_specs=[pl.BlockSpec(memory_space=pltpu.SMEM)] + [vmem] * (hpd * chips + 1),
        out_specs=hbm,
        out_shape=jax.ShapeDtypeStruct((chunk, 3 * heads * feats), F32),
        scratch_shapes=[
            pltpu.VMEM((chips, 2, 3, chunk // 2, CORES * own), F32),
            pltpu.SemaphoreType.DMA((6 * chips,)),
        ],
        compiler_params=pltpu.CompilerParams(vmem_limit_bytes=16 * MIB),
        cost_estimate=pl.CostEstimate(flops=0, bytes_accessed=0, transcendentals=0),
        name="join",
    )(table, *projs, near)
    return (grad_input[None], grad_proj, grad_inner[None, None])


def solution(mesh):
    placed = (
        P(("groups", "seq"), "seg", None),
        P(("groups", "seq"), "seg", None),
        P("seq", None),
        P(("groups", "seq"), "seg", None, None, None, None),
        P(),
    )
    return jax.shard_map(
        per_device,
        mesh=mesh,
        in_specs=placed,
        out_specs=(
            P(("groups", "seq"), "seg", None),
            P(("groups", "seq"), None),
            P(("groups", "seq"), "seg", None, None, None, None),
        ),
        check_vma=False,
    )
```

```python
import functools
from itertools import zip_longest

import jax
import jax.numpy as jnp
from jax import lax
from jax.experimental import pallas as pl
from jax.experimental.pallas import tpu as pltpu
from jax.sharding import PartitionSpec as P

MB = 256
BF = jnp.bfloat16
F32 = jnp.float32
CORES = 2
GELU_A = 0.7978845608028654
GELU_B = 0.044715
MIB = 1024 * 1024
TILE = 16
GROUP = 4


def dot(a, b, ca, cb):
    return lax.dot_general(a, b, (((ca,), (cb,)), ((), ())), preferred_element_type=F32)


def gelu_parts(u):
    square = u * u
    tanh = jnp.tanh(u * (GELU_A + (GELU_A * GELU_B) * square))
    half = 0.5 * (1.0 + tanh)
    sech = 1.0 - tanh * tanh
    slope = GELU_A + (3.0 * GELU_A * GELU_B) * square
    return square, tanh, half, sech, slope


def packed(row, deep, hid):
    return row % deep, row // deep * hid


def prep_kernel(dims, table, rows, w, cots, start, mine, pack, *refs):
    nseg, nseq, hpd, feats, hid, tokens, chunk = dims
    ships, refs = refs[: nseg // CORES], refs[nseg // CORES :]
    cut, held, weights, turned, sem = refs
    own = hpd * feats
    wide = cut.shape[2]
    deep = pack.shape[0]
    me = table[nseg + nseq + 1]
    base = me * own // wide * wide
    copies = []
    for part in range(3):
        at = pl.multiple_of(part * nseg * own + base, wide)
        copies.append(pltpu.make_async_copy(w.at[:, pl.ds(at, wide)], cut.at[part], sem.at[part]))
    copies.append(pltpu.make_async_copy(cots, held, sem.at[3]))
    copies.append(pltpu.make_async_copy(start, weights, sem.at[4]))
    for i, ship in enumerate(ships):
        copies.append(pltpu.make_async_copy(rows, ship.at[pl.ds(0, tokens)], sem.at[5 + i]))
    for copy in copies:
        copy.start()
    for part in range(3):
        copies[part].wait()
        block = cut[part].T
        even = block[:own]
        for i in range(1, wide // own):
            even = jnp.where(me * own % wide == i * own, block[i * own : (i + 1) * own], even)
        mine[part * own : (part + 1) * own] = even
    copies[3].wait()
    turned[...] = held[...].T
    copies[4].wait()
    for slot in range(nseg):
        dest = table[nseg + nseq + 2 + slot]
        dx, dc = slot // CORES, slot % CORES
        target, low = (pack, 0) if slot == 0 else (ships[dx], tokens + (deep * dc if dx else 0))
        for i in range(3 * hpd):
            kind, head = i // hpd, i % hpd
            if kind < 2:
                value = weights[kind, dest * hpd + head].astype(BF)
            else:
                value = turned[pl.ds(pl.multiple_of((dest * hpd + head) * feats, feats), feats)]
            for j in range(0, feats, TILE):
                top, left = packed(i * feats + j, deep, hid)
                target[low + top : low + top + TILE, left : left + hid] = value[j : j + TILE]
    for copy in copies[5:]:
        copy.wait()


def inner_kernel(dims, head, table, rates, *refs):
    nseg, nseq, hpd, feats, hid, tokens, chunk = dims
    chips = nseg // CORES
    li, refs = refs[:nseg], refs[nseg:]
    wt, refs = refs[:nseq], refs[nseq:]
    pack, refs = refs[0], refs[1:]
    gp, refs = refs[:nseq], refs[nseq:]
    gq, sent, kept, qkv, wts, cts, ht, rt, g1, g2p, gu, gab, res, wide = refs
    rows = 3 * feats
    own = hpd * feats
    first = head * feats
    for back in range(nseq):
        at = pl.multiple_of(table[nseg + back] * chunk, chunk)
        for p in range(3):
            block = wt[back][p * own + first : p * own + first + feats]
            wide[p * feats : (p + 1) * feats, pl.ds(at, chunk)] = block

    deep = pack.shape[0]

    for slot in range(nseg):
        dx, dc = slot // CORES, slot % CORES
        source, low = (pack, 0) if slot == 0 else (li[slot], tokens + (deep * dc if dx else 0))
        for i, piece in enumerate((wts.at[slot, 0], wts.at[slot, 1], cts.at[slot])):
            for j in range(0, feats, TILE):
                top, left = packed((i * hpd + head) * feats + j, deep, hid)
                value = source[low + top : low + top + TILE, left : left + hid]
                piece[j : j + TILE] = value
        total = dot(wide[...], li[slot][:tokens], 1, 1)
        qkv[slot] = total.astype(BF).reshape(3, feats, tokens)
    rate = rates[table[nseg + nseq] + head] * (1.0 / MB)

    def local(slot):
        a_b, b_b = wts[slot, 0], wts[slot, 1]
        q_b, k_b, v_b = qkv[slot, 0], qkv[slot, 1], qkv[slot, 2]
        c_b = cts[slot]
        u = dot(a_b, k_b, 0, 0)
        yield
        square, tanh, half, sech, slope = gelu_parts(u)
        h_b = (u * half).astype(BF)
        yield
        slope1 = half + 0.5 * u * sech * slope
        second = sech * (GELU_A + (6.0 * GELU_A * GELU_B) * square - u * tanh * slope * slope)
        ht[slot] = h_b
        g1[slot] = slope1
        resid = k_b.astype(F32) - v_b.astype(F32) + dot(b_b, h_b, 1, 0)
        r_b = resid.astype(BF)
        yield
        rt[slot] = r_b
        p = dot(b_b, r_b, 0, 0)
        g2p[slot] = second * p
        gu_b = (slope1 * p).astype(BF)
        gu[slot] = gu_b
        yield
        new_a = (a_b.astype(F32) - rate * dot(k_b, gu_b, 1, 1)).astype(BF)
        new_b = (b_b.astype(F32) - rate * dot(r_b, h_b, 1, 1)).astype(BF)
        uq = dot(new_a, q_b, 0, 0)
        yield
        square, tanh, half, sech, slope = gelu_parts(uq)
        hq_b = (uq * half).astype(BF)
        guq_b = ((half + 0.5 * uq * sech * slope) * dot(new_b, c_b, 0, 0)).astype(BF)
        gab[slot, 0] = dot(q_b, guq_b, 1, 1)
        yield
        gab[slot, 1] = dot(c_b, hq_b, 1, 1)
        gq[slot, 0] = (c_b.astype(F32) + dot(new_a, guq_b, 1, 0)).astype(BF)

    for low in range(0, nseg, GROUP):
        for _ in zip_longest(*[local(slot) for slot in range(low, min(low + GROUP, nseg))]):
            pass

    def end(slot, k_b, a_b, ta_b, gu_b, dr, dgu_b, c_a, c_b):
        left = jnp.concatenate([a_b, ta_b], 1)
        gk = dr + dot(left, jnp.concatenate([dgu_b, gu_b], 0), 1, 0)
        gq[slot, 1] = (-rate * gk).astype(BF)
        gq[slot, 2] = (rate * dr).astype(BF)
        res[slot, 0] = c_a.astype(BF)
        res[slot, 1] = c_b.astype(BF)

    c_a = c_b = jnp.zeros((feats, hid), F32)
    late = None
    for turn in range(nseg):
        slot = table[nseg - 1 - turn]
        t_a = c_a + gab[slot, 0]
        t_b = c_b + gab[slot, 1]
        a_b, b_b = wts[slot, 0], wts[slot, 1]
        k_b = qkv[slot, 1]
        h_b, r_b, gu_b = ht[slot], rt[slot], gu[slot]
        ta_b, tb_b = t_a.astype(BF), t_b.astype(BF)
        du = dot(ta_b, k_b, 0, 0)
        dr_h, dp_r = dot(tb_b, h_b, 1, 0), dot(tb_b, r_b, 0, 0)
        if late is not None:
            end(*late)
        dh_b = (g1[slot] * du).astype(BF)
        dr = dot(b_b, dh_b, 1, 0) + dr_h
        dr_b = dr.astype(BF)
        dp = dot(b_b, dr_b, 0, 0) + dp_r
        c_b = t_b - rate * (dot(dr_b, h_b, 1, 1) + dot(r_b, dh_b, 1, 1))
        dgu_b = (g2p[slot] * du + g1[slot] * dp).astype(BF)
        c_a = t_a - rate * dot(k_b, dgu_b, 1, 1)
        late = (slot, k_b, a_b, ta_b, gu_b, dr, dgu_b, c_a, c_b)
    end(*late)

    for slot in range(nseg):
        dx, dc = slot // CORES, slot % CORES
        if dx == 0:
            kept[dc] = res[slot]
        else:
            sent[dx - 1, dc * rows : (dc + 1) * rows] = gq[slot].reshape(rows, tokens)
            at = CORES * rows + dc * 2 * feats
            sent[dx - 1, at : at + 2 * feats] = res[slot].reshape(2 * feats, hid)
    for dz in range(nseq):
        at = pl.multiple_of(table[nseg + (nseq - dz) % nseq] * chunk, chunk)
        total = jnp.zeros((rows, chunk), F32)
        for slot in range(nseg):
            part = li[slot][:tokens, pl.ds(at, chunk)]
            total += dot(gq[slot].reshape(rows, tokens), part, 1, 0)
        gp[dz][...] = total.astype(gp[dz].dtype)


def input_kernel(dims, table, *refs):
    nseg, nseq, hpd, feats, hid, tokens, chunk = dims
    chips = nseg // CORES
    rows = 3 * feats
    gq, refs = refs[:hpd], refs[hpd:]
    kept, refs = refs[:hpd], refs[hpd:]
    sent, refs = refs[: hpd * (chips - 1)], refs[hpd * (chips - 1) :]
    wt, refs = refs[:nseq], refs[nseq:]
    away, (home, aside, leave) = refs[: chips - 1], refs[chips - 1 :]
    for dc in range(CORES):
        left = [gq[h][dc, p] for p in range(3) for h in range(hpd)]
        for dx in range(chips - 1):
            for p in range(3):
                at = dc * rows + p * feats
                left += [sent[h * (chips - 1) + dx][at : at + feats] for h in range(hpd)]
        left = jnp.concatenate(left)
        for back in range(nseq):
            at = pl.multiple_of(table[nseg + back] * chunk, chunk)
            right = jnp.concatenate([wt[back][...]] + [value[back] for value in away])
            value = dot(left, right, 0, 0)
            out = (home, aside)[dc]
            out[:, pl.ds(at, chunk)] = value.astype(out.dtype)
    at = CORES * rows + 2 * feats
    for head in range(hpd):
        leave[head * chips] = kept[head][1].reshape(2 * feats, hid)
        for dx in range(1, chips):
            leave[head * chips + dx] = sent[head * (chips - 1) + dx - 1][at : at + 2 * feats]


def sum_kernel(*refs):
    total = refs[0][...]
    for ref in refs[1:-1]:
        total += ref[...].astype(F32)
    total = total.T.astype(BF)
    half = total.shape[0] // 2
    refs[-1][...] = jnp.concatenate([total[:half], total[half:]], 1)


def join_kernel(dims, table, *refs):
    nseg, nseq, hpd, feats, hid, tokens, chunk = dims
    chips = nseg // CORES
    far, near, out, whole, sem = refs[: hpd * chips], *refs[hpd * chips :]
    wide = CORES * hpd * feats
    half = chunk // 2
    me = table[nseg + nseq + 1]
    chip = me // CORES
    even = me % CORES == 0
    copies = []
    for dx in range(chips):
        source = (chip - dx + chips) % chips
        for side in range(2):
            cut = slice(side * 3 * feats, (side + 1) * 3 * feats)
            mine = [far[h * chips + dx][:, cut].astype(F32) for h in range(hpd)]
            other = [near[h * chips + dx, :, cut].astype(F32) for h in range(hpd)]
            mine, other = (
                [jnp.where(even, a, b) for a, b in zip(mine, other)],
                [jnp.where(even, b, a) for a, b in zip(mine, other)],
            )
            for part in range(3):
                cut = slice(part * feats, (part + 1) * feats)
                whole[dx, side, part] = jnp.concatenate([v[:, cut] for v in mine + other], 1)
                at = pl.multiple_of((part * nseg * hpd * feats) + source * wide, wide)
                copy = pltpu.make_async_copy(
                    whole.at[dx, side, part],
                    out.at[pl.ds(side * half, half), pl.ds(at, wide)],
                    sem.at[len(copies)],
                )
                copy.start()
                copies.append(copy)
    for copy in copies:
        copy.wait()


def weights_kernel(dims, table, *refs):
    nseg, nseq, hpd, feats, hid, tokens, chunk = dims
    chips = nseg // CORES
    kept, refs = refs[:hpd], refs[hpd:]
    sent, refs = refs[: hpd * (chips - 1)], refs[hpd * (chips - 1) :]
    got, out = refs
    at = CORES * 3 * feats
    for head in range(hpd):
        for slot in range(nseg):
            dx, dc = slot // CORES, slot % CORES
            if dc == 1:
                piece = got[head * chips + dx]
            elif dx == 0:
                piece = kept[head][0].reshape(2 * feats, hid)
            else:
                piece = sent[head * (chips - 1) + dx - 1][at : at + 2 * feats]
            index = table[nseg + nseq + 2 + slot] * hpd + head
            out[0, index] = piece[:feats].astype(F32)
            out[1, index] = piece[feats:].astype(F32)


def per_device(layer_input, out_cot, w_proj, inner_start, rates):
    rows = layer_input[0]
    tokens, width = rows.shape
    heads = rates.shape[0]
    feats, hid = inner_start.shape[4:]
    nseg, nseq = lax.axis_size("seg"), lax.axis_size("seq")
    chips = nseg // CORES
    hpd = heads // nseg
    own = hpd * feats
    chunk = width // nseq
    me, place = lax.axis_index("seg"), lax.axis_index("seq")
    chip, core = me // CORES, me % CORES
    barrier = lax.optimization_barrier

    def to_chip(value, dx):
        pairs = [(i, (i + dx * CORES) % nseg) for i in range(nseg)]
        return lax.ppermute(value, "seg", pairs)

    def to_core(value):
        return lax.ppermute(value, "seg", [(i, i ^ 1) for i in range(nseg)])

    def to_seq(value, dz):
        return lax.ppermute(value, "seq", [(i, (i + dz) % nseq) for i in range(nseq)])

    def kernel(body, name, limit, cost, outs, scratch, *operands):
        smem = pl.BlockSpec(memory_space=pltpu.SMEM)
        vmem = pl.BlockSpec(memory_space=pltpu.VMEM)
        return pl.pallas_call(
            body,
            in_specs=[smem if o.ndim == 1 else vmem for o in operands],
            out_specs=[vmem] * len(outs),
            out_shape=[jax.ShapeDtypeStruct(*o) for o in outs],
            scratch_shapes=[pltpu.VMEM(*o) for o in scratch],
            compiler_params=pltpu.CompilerParams(vmem_limit_bytes=limit * MIB),
            cost_estimate=pl.CostEstimate(flops=0, bytes_accessed=cost, transcendentals=0),
            name=name,
        )(*operands)

    def summed(pieces):
        return kernel(sum_kernel, "sum", 12, 0, [((chunk // 2, 6 * feats), BF)], [], *pieces)[0]

    crossed = chips == 2 and lax.axis_size("groups") == 2
    shift = lax.axis_index("groups") if crossed else 0

    segs = jnp.arange(nseg, dtype=jnp.int32)
    slot_of = ((chip - segs // CORES) % chips) * CORES + (core + segs) % CORES
    back = (place - jnp.arange(nseq, dtype=jnp.int32)) % nseq
    dest = ((chip + shift + segs // CORES) % chips) * CORES + (core + segs) % CORES
    table = jnp.concatenate([slot_of, back, jnp.stack([dest[0] * hpd, dest[0]]), dest])
    table = table.astype(jnp.int32)
    dims = (nseg, nseq, hpd, feats, hid, tokens, chunk)

    wide = max(own, 128)
    deep = -(-3 * own * hid // (width * TILE)) * TILE
    hbm = pl.BlockSpec(memory_space=pltpu.HBM)
    vmem = pl.BlockSpec(memory_space=pltpu.VMEM)
    outs = [((3 * own, chunk), BF), ((deep, width), BF), ((tokens + deep, width), BF)]
    outs += [((tokens + CORES * deep, width), BF)] * (chips - 1)
    operands = (rows, w_proj, out_cot[0], inner_start[0, 0])
    mine, pack, *ships = pl.pallas_call(
        functools.partial(prep_kernel, dims),
        in_specs=[pl.BlockSpec(memory_space=pltpu.SMEM)] + [hbm] * 4,
        out_specs=[vmem] * len(outs),
        out_shape=[jax.ShapeDtypeStruct(*o) for o in outs],
        scratch_shapes=[
            pltpu.VMEM((3, chunk, wide), BF),
            pltpu.VMEM((tokens, heads * feats), BF),
            pltpu.VMEM((2, heads, feats, hid), F32),
            pltpu.VMEM((heads * feats, tokens), BF),
            pltpu.SemaphoreType.DMA((5 + chips,)),
        ],
        compiler_params=pltpu.CompilerParams(vmem_limit_bytes=16 * MIB),
        cost_estimate=pl.CostEstimate(flops=0, bytes_accessed=0, transcendentals=0),
        name="prep",
    )(table, *[pltpu.with_memory_space_constraint(o, pltpu.HBM) for o in operands])
    near = to_core(ships[0])
    far = [to_chip(ships[dx], dx) for dx in range(1, chips)]
    wt = [mine] + [to_seq(mine, dz) for dz in range(1, nseq)]
    far, near, wt = barrier((far, near, wt))
    li = [rows, near]
    for value in far:
        li += [value, to_core(value)]

    def to_others(value):
        if crossed:
            return [lax.ppermute(value, "groups", [(0, 1), (1, 0)])]
        return [to_chip(value, -dx) for dx in range(1, chips)]

    def inner(head):
        return kernel(
            functools.partial(inner_kernel, dims, head),
            "inner",
            36,
            0,
            [((3 * feats, chunk), BF if dz else F32) for dz in range(nseq)]
            + [((nseg, 3, feats, tokens), BF)]
            + [((chips - 1, 10 * feats, tokens), BF)]
            + [((CORES, 2, feats, hid), BF)],
            [
                ((nseg, 3, feats, tokens), BF),
                ((nseg, 2, feats, hid), BF),
                ((nseg, feats, tokens), BF),
                ((nseg, hid, tokens), BF),
                ((nseg, feats, tokens), BF),
                ((nseg, hid, tokens), F32),
                ((nseg, hid, tokens), F32),
                ((nseg, hid, tokens), BF),
                ((nseg, 2, feats, hid), F32),
                ((nseg, 2, feats, hid), BF),
                ((3 * feats, width), BF),
            ],
            table,
            rates,
            *li,
            *wt,
            pack,
        )

    away = to_others(jnp.stack(wt))
    grads, kept, sent, projs, pieces = [], [], [], [], None
    for head in range(hpd):
        outs = inner(head)
        gp, gq, send, keep = outs[:nseq], outs[nseq], outs[nseq + 1], outs[nseq + 2]
        if pieces is not None:
            gp, send, pieces[nseq // 2] = barrier((gp, send, pieces[nseq // 2]))
        if pieces is not None:
            total = summed(pieces)
            projs += [total] + [to_chip(total, dx) for dx in range(1, chips)]
        pieces = [gp[0]] + [to_seq(gp[dz], dz) for dz in range(1, nseq)]
        sent += [to_chip(send[dx - 1], -dx) for dx in range(1, chips)]
        grads.append(gq)
        kept.append(keep)

    home, aside, leave = kernel(
        functools.partial(input_kernel, dims),
        "input",
        24,
        10 * MIB,
        [((tokens, width), F32), ((tokens, width), BF)]
        + [((hpd * chips, 2 * feats, hid), BF)],
        [],
        table,
        *grads,
        *kept,
        *sent,
        *wt,
        *away,
    )
    pieces, projs, home, aside, leave = barrier((pieces, projs, home, aside, leave))

    total = summed(pieces)
    projs += [total] + [to_chip(total, dx) for dx in range(1, chips)]
    aside, leave = to_core(aside), to_core(leave)
    grad_input = (home + aside.astype(F32)).astype(BF)
    (grad_inner,) = kernel(
        functools.partial(weights_kernel, dims),
        "weights",
        8,
        10 * MIB,
        [((2, heads, feats, hid), F32)],
        [],
        table,
        *kept,
        *sent,
        leave,
    )
    projs, grad_input, grad_inner = barrier((projs, grad_input, grad_inner))
    near = to_core(jnp.stack(projs))
    grad_proj = pl.pallas_call(
        functools.partial(join_kernel, dims),
        in_specs=[pl.BlockSpec(memory_space=pltpu.SMEM)] + [vmem] * (hpd * chips + 1),
        out_specs=hbm,
        out_shape=jax.ShapeDtypeStruct((chunk, 3 * heads * feats), F32),
        scratch_shapes=[
            pltpu.VMEM((chips, 2, 3, chunk // 2, CORES * own), F32),
            pltpu.SemaphoreType.DMA((6 * chips,)),
        ],
        compiler_params=pltpu.CompilerParams(vmem_limit_bytes=16 * MIB),
        cost_estimate=pl.CostEstimate(flops=0, bytes_accessed=0, transcendentals=0),
        name="join",
    )(table, *projs, near)
    return (grad_input[None], grad_proj, grad_inner[None, None])


def solution(mesh):
    placed = (
        P(("groups", "seq"), "seg", None),
        P(("groups", "seq"), "seg", None),
        P("seq", None),
        P(("groups", "seq"), "seg", None, None, None, None),
        P(),
    )
    return jax.shard_map(
        per_device,
        mesh=mesh,
        in_specs=placed,
        out_specs=(
            P(("groups", "seq"), "seg", None),
            P(("groups", "seq"), None),
            P(("groups", "seq"), "seg", None, None, None, None),
        ),
        check_vma=False,
    )
```
